32 devices in a mesh: dp: 4 (over x, core), fsdp: 8 (over z, y).
Axes of the slice: x: 2, y: 2, z: 4, core: 2. Of those that a mesh axis runs over, the one named last changes fastest.
Arguments:
- tokens: bfloat16 [16384, 768], P(('dp', 'fsdp')), may hold values from -6 to 6
- mask_flags: int32 [16384], P(('dp', 'fsdp')), may hold values from 0 to 1, as said below
- mask_counts: int32 [64], P(('dp', 'fsdp')), may hold values from 80 to 256, as said below
- cotangent: bfloat16 [16384, 768], P(('dp', 'fsdp')), may hold values from -6 to 6
- w_qkv: float32 [768, 2304], P('fsdp'), may hold values from -0.21875 to 0.21875
- w_out: float32 [768, 768], P('fsdp'), may hold values from -1.75 to 1.75
- w_up: float32 [768, 3072], P('fsdp'), may hold values from -0.21875 to 0.21875
- w_down: float32 [3072, 768], P('fsdp'), may hold values from -0.109375 to 0.109375
- vectors: float32 [768, 5], P('fsdp'), may hold values from -4 to 4
- first_qkv: float32 [768, 2304], P('fsdp'), may hold values from -512 to 512
- first_out: float32 [768, 768], P('fsdp'), may hold values from -112 to 112
- first_up: float32 [768, 3072], P('fsdp'), may hold values from -320 to 320
- first_down: float32 [3072, 768], P('fsdp'), may hold values from -640 to 640
- first_vectors: float32 [768, 5], P('fsdp'), may hold values from -768 to 768
- second_qkv: float32 [768, 2304], P('fsdp'), may hold values from 8192 to 32768
- second_out: float32 [768, 768], P('fsdp'), may hold values from 384 to 1536
- second_up: float32 [768, 3072], P('fsdp'), may hold values from 3276 to 13107
- second_down: float32 [3072, 768], P('fsdp'), may hold values from 10922 to 43690
- second_vectors: float32 [768, 5], P('fsdp'), may hold values from 8192 to 16777216
Outputs:
- layer_out: bfloat16 [16384, 768], P(('dp', 'fsdp'))
- token_grad: bfloat16 [16384, 768], P(('dp', 'fsdp'))
- new_first_qkv: float32 [768, 2304], P('fsdp')
- new_first_out: float32 [768, 768], P('fsdp')
- new_first_up: float32 [768, 3072], P('fsdp')
- new_first_down: float32 [3072, 768], P('fsdp')
- new_first_vectors: float32 [768, 5], P('fsdp')
- new_second_qkv: float32 [768, 2304], P('fsdp')
- new_second_out: float32 [768, 768], P('fsdp')
- new_second_up: float32 [768, 3072], P('fsdp')
- new_second_down: float32 [3072, 768], P('fsdp')
- new_second_vectors: float32 [768, 3], P('fsdp')
- new_second_norm_two: float32 [768, 2], P('fsdp')
- new_w_qkv: float32 [768, 2304], P('fsdp')
- new_w_out: float32 [768, 768], P('fsdp')
- new_w_up: float32 [768, 3072], P('fsdp')
- new_w_down: float32 [3072, 768], P('fsdp')
- new_vectors: float32 [768, 5], P('fsdp')
The draws below stay inside these ranges and needn't reach their ends.
Inputs may be any that keep to these rules, and one draw needn't show every extreme that they name: `mask_flags`: in every image of 256 consecutive tokens exactly that image's mask_counts entry of flags is 1. `mask_counts`: some image has 256 masked tokens and some has 80.
All inputs are finite; a program needn't handle non-finite values.
Results may differ from the reference program's by a relative error of at most 0.02.
Values may be sent and summed in bfloat16 or wider, within the bound.
A program may use at most 192 MiB of HBM per device.

```python
import math
import jax
import jax.numpy as jnp
from jax import lax

D = 768
HEADS = 16
HEAD_DIM = 48
FF = 3072
TOK_IMG = 256
STEP = 10
IMAGES = 64
TOKENS = 16384
MIN_MASK = 80


def mask_plan(key):
    counts = jax.random.randint(jax.random.fold_in(key, 11), (IMAGES,), MIN_MASK, TOK_IMG + 1)
    top_at = jax.random.randint(jax.random.fold_in(key, 12), (), 0, IMAGES)
    shift_by = jax.random.randint(jax.random.fold_in(key, 13), (), 1, max(IMAGES, 2))
    bottom_at = (top_at + shift_by) % IMAGES
    counts = counts.at[bottom_at].set(MIN_MASK).at[top_at].set(TOK_IMG)
    scores = jax.random.randint(jax.random.fold_in(key, 14), (IMAGES, TOK_IMG), 0, 2 ** 20)
    scores = scores * TOK_IMG + jnp.arange(TOK_IMG, dtype=jnp.int32)[None, :]
    order = jnp.argsort(scores, axis=1)
    ranks = jnp.argsort(order, axis=1)
    flags = (ranks < counts[:, None]).astype(jnp.int32).reshape(TOKENS)
    return (flags, counts.astype(jnp.int32))


def draw_mask_flags(key, part):
    return mask_plan(key)[0]


def draw_mask_counts(key, part):
    return mask_plan(key)[1]


def draw_vectors(key, part):
    key = jax.random.fold_in(key, 5)
    noise = jnp.clip(jax.random.normal(key, (D, 5), jnp.float32), -3.5, 3.5)
    spread = jnp.array([0.15, 0.4, 0.15, 0.4, 1.0], jnp.float32)
    centre = jnp.array([1.0, 0.0, 1.0, 0.0, 0.0], jnp.float32)
    return centre[None, :] + spread[None, :] * noise


def draw_second_vectors(key, part):
    key = jax.random.fold_in(key, 7)
    strong = 0.64 * TOKENS * TOK_IMG
    weak = 0.64 * TOKENS
    column_scale = jnp.array([strong, strong, weak, weak, strong], jnp.float32)
    factor = jnp.exp(jax.random.uniform(key, (D, 5), jnp.float32, 0.0, 1.3862943611198906))
    return column_scale[None, :] * factor


def steps_of(key, extent, pieces, least, high):
    factor_of, own = 1.0, jax.random.fold_in(key, 6)
    for axis_at, blocks in pieces:
        steps = jnp.exp(jax.random.uniform(jax.random.fold_in(own, axis_at), (blocks,), jnp.float32, least / len(pieces), high / len(pieces)))
        factor_of = factor_of * jnp.repeat(steps, extent[axis_at] // blocks).reshape([-1 if axis == axis_at else 1 for axis in range(len(extent))])
    return factor_of


def scatter_about(own_key, extent, scale, reach, split=(), kind=jnp.bfloat16):
    entries = jax.random.normal(own_key, extent, jnp.float32) * scale
    if len(split) > 0:
        entries = steps_of(own_key, extent, split, -0.22, 0.18) * entries
    return jnp.clip(entries, min=-reach, max=reach).astype(kind)


def setup_inputs(seed: int = 0) -> dict:
    key_list = jax.random.split(jax.random.key(seed), 20)
    tokens = scatter_about(key_list[0], (TOKENS, D), 1.0, 6.0, ((0, 32),))
    mask_flags = draw_mask_flags(jax.random.fold_in(key_list[19], 71), 0)
    mask_counts = draw_mask_counts(jax.random.fold_in(key_list[19], 71), 0)
    cotangent = scatter_about(key_list[3], (TOKENS, D), 1.0, 6.0, ((0, 32),))
    w_qkv = scatter_about(key_list[4], (D, 3 * D), D ** -0.5, 0.21875, ((0, 8),), jnp.float32)
    w_out = scatter_about(key_list[5], (D, D), (D * 4 // TOK_IMG) ** -0.5, 1.75, ((0, 8),), jnp.float32)
    w_up = scatter_about(key_list[6], (D, FF), D ** -0.5, 0.21875, ((0, 8),), jnp.float32)
    w_down = scatter_about(key_list[7], (FF, D), FF ** -0.5, 0.109375, ((0, 8),), jnp.float32)
    vectors = draw_vectors(jax.random.fold_in(key_list[19], 71), 0)
    first_qkv = scatter_about(key_list[9], (D, 3 * D), (0.7 * TOKENS ** 0.5), 512.0, ((0, 8),), jnp.float32)
    first_out = scatter_about(key_list[10], (D, D), (2.4 * (TOKENS // TOK_IMG) ** 0.5), 112.0, ((0, 8),), jnp.float32)
    first_up = scatter_about(key_list[11], (D, FF), (0.45 * TOKENS ** 0.5), 320.0, ((0, 8),), jnp.float32)
    first_down = scatter_about(key_list[12], (FF, D), (0.8 * TOKENS ** 0.5), 640.0, ((0, 8),), jnp.float32)
    first_vectors = scatter_about(key_list[13], (D, 5), (TOKENS ** 0.5), 768.0, ((0, 8),), jnp.float32)
    second_qkv = jnp.clip(jnp.exp(math.log(32768.0) - 1.3862944 * jax.random.uniform(key_list[14], (D, 3 * D), jnp.float32) ** steps_of(key_list[14], (D, 3 * D), ((0, 8),), -0.2, 0.2)), 8192.0, 32768.0)
    second_out = jnp.clip(jnp.exp(math.log(1536.0) - 1.3862944 * jax.random.uniform(key_list[15], (D, D), jnp.float32) ** steps_of(key_list[15], (D, D), ((0, 8),), -0.2, 0.2)), 384.0, 1536.0)
    second_up = jnp.clip(jnp.exp(math.log(13107.0) - 1.3865233 * jax.random.uniform(key_list[16], (D, FF), jnp.float32) ** steps_of(key_list[16], (D, FF), ((0, 8),), -0.2, 0.2)), 3276.0, 13107.0)
    second_down = jnp.clip(jnp.exp(math.log(43690.0) - 1.3863401 * jax.random.uniform(key_list[17], (FF, D), jnp.float32) ** steps_of(key_list[17], (FF, D), ((0, 8),), -0.2, 0.2)), 10922.0, 43690.0)
    second_vectors = draw_second_vectors(jax.random.fold_in(key_list[19], 71), 0)
    return dict(tokens=tokens, mask_flags=mask_flags, mask_counts=mask_counts, cotangent=cotangent, w_qkv=w_qkv, w_out=w_out, w_up=w_up, w_down=w_down, vectors=vectors, first_qkv=first_qkv, first_out=first_out, first_up=first_up, first_down=first_down, first_vectors=first_vectors, second_qkv=second_qkv, second_out=second_out, second_up=second_up, second_down=second_down, second_vectors=second_vectors)


@jax.custom_vjp
def low(v):
    return lax.optimization_barrier(v.astype(jnp.bfloat16)).astype(jnp.float32)

@jax.custom_vjp
def low_back(v):
    return v

def low_keep(v):
    return (low(v), None)

def low_pass(kept, grad):
    return (grad,)

def back_keep(v):
    return (v, None)

def back_low(kept, grad):
    return (low(grad),)
low.defvjp(low_keep, low_pass)
low_back.defvjp(back_keep, back_low)
EPS_NORM = 1e-06
BETA_ONE = 0.5
BETA_TWO = 0.5
ADAM_EPS = 1e-08
DECAY = 0.01
RATE_QKV = 0.02
RATE_OUT = 0.1
RATE_UP = 0.02
RATE_DOWN = 0.01
RATE_VECTORS = 0.2

def rounded_both(values):
    return low_back(low(values))

def matmul(left, right):
    return jnp.dot(left, right, precision=lax.Precision.HIGHEST)

def layer_norm(values, gain, bias):
    mean = lax.optimization_barrier(jnp.mean(values, axis=-1, keepdims=True))
    centred = values - mean
    variance = lax.optimization_barrier(jnp.mean(centred * centred, axis=-1, keepdims=True))
    return centred * lax.rsqrt(variance + EPS_NORM) * gain + bias

def layer(params, tokens, flags):
    w_qkv, w_out, w_up, w_down, vectors = [low(item) for item in params]
    rows = tokens.shape[0]
    images = rows // TOK_IMG
    hidden = jnp.where(flags[:, None] == 1, vectors[:, 4][None, :], tokens)
    entry_one = low(layer_norm(hidden, vectors[:, 0], vectors[:, 1]))
    project = rounded_both(matmul(entry_one, w_qkv)).reshape(images, TOK_IMG, 3, HEADS, HEAD_DIM)
    queries = project[:, :, 0]
    keys = project[:, :, 1]
    values = project[:, :, 2]
    raw = low_back(jnp.einsum('bqhd,bkhd->bhqk', queries, keys, precision=lax.Precision.HIGHEST))
    probs = jax.nn.softmax(raw * HEAD_DIM ** (-0.5), axis=-1)
    mixed = jnp.einsum('bhqk,bkhd->bqhd', low(probs), values, precision=lax.Precision.HIGHEST)
    attended = rounded_both(mixed).reshape(rows, D)
    middle = hidden + low_back(matmul(attended, w_out))
    entry_two = low(layer_norm(middle, vectors[:, 2], vectors[:, 3]))
    rising = low_back(matmul(entry_two, w_up))
    active = low(jax.nn.gelu(rising, approximate=False))
    return middle + low_back(matmul(active, w_down))

def adamw(weight, grad, first, second, rate):
    new_first = BETA_ONE * first + (1.0 - BETA_ONE) * grad
    new_second = BETA_TWO * second + (1.0 - BETA_TWO) * grad * grad
    fix_one = 1.0 - BETA_ONE ** STEP
    fix_two = 1.0 - BETA_TWO ** STEP
    ratio = new_first / fix_one / (jnp.sqrt(new_second / fix_two) + ADAM_EPS)
    return (new_first, new_second, weight - rate * (ratio + DECAY * weight))

def reference(tokens, mask_flags, mask_counts, cotangent, w_qkv, w_out, w_up, w_down, vectors, first_qkv, first_out, first_up, first_down, first_vectors, second_qkv, second_out, second_up, second_down, second_vectors):
    per_block = math.gcd(IMAGES, max(1, 4096 // TOK_IMG))
    blocks = IMAGES // per_block
    rows = per_block * TOK_IMG
    params = (w_qkv, w_out, w_up, w_down, vectors)
    inputs = tokens.astype(jnp.float32).reshape(blocks, rows, D)
    flag_rows = mask_flags.reshape(blocks, rows)
    count_rows = mask_counts.reshape(blocks, per_block)
    back_rows = cotangent.astype(jnp.float32).reshape(blocks, rows, D)

    def block_step(acc, item):
        block_in, flags, counts, back = item
        result, pull = jax.vjp(lambda prm, inp: layer(prm, inp, flags), params, block_in)
        weight_row = jnp.repeat(TOK_IMG / counts.astype(jnp.float32), TOK_IMG, total_repeat_length=rows) * flags
        grad_params, grad_in = pull(back * weight_row[:, None])
        acc = jax.tree.map(lambda left, right: left + right, acc, grad_params)
        return (acc, (result.astype(jnp.bfloat16), grad_in.astype(jnp.bfloat16)))
    zeros = jax.tree.map(jnp.zeros_like, params)
    grads, (outputs, grad_inputs) = lax.scan(block_step, zeros, (inputs, flag_rows, count_rows, back_rows))
    firsts = (first_qkv, first_out, first_up, first_down, first_vectors)
    seconds = (second_qkv, second_out, second_up, second_down, second_vectors)
    rates = (RATE_QKV, RATE_OUT, RATE_UP, RATE_DOWN, RATE_VECTORS)
    updated = [adamw(params[i], grads[i], firsts[i], seconds[i], rates[i]) for i in range(5)]
    vec_second = updated[4][1]
    second_front = jnp.concatenate([vec_second[:, 0:2], vec_second[:, 4:5]], axis=1)
    second_later = vec_second[:, 2:4]
    return (outputs.reshape(TOKENS, D), grad_inputs.reshape(TOKENS, D), updated[0][0], updated[1][0], updated[2][0], updated[3][0], updated[4][0], updated[0][1], updated[1][1], updated[2][1], updated[3][1], second_front, second_later, updated[0][2], updated[1][2], updated[2][2], updated[3][2], updated[4][2])
```

```python
import functools

import jax
import jax.numpy as jnp
from jax import lax
from jax.experimental import pallas as pl
from jax.experimental.pallas import tpu as pltpu
from jax.sharding import PartitionSpec as P

HEADS = 16
HEAD_DIM = 48
STEP = 10


EPS_NORM = 1e-06
BETA_ONE = 0.5
BETA_TWO = 0.5
ADAM_EPS = 1e-08
DECAY = 0.01
RATE_QKV = 0.02
RATE_OUT = 0.1
RATE_UP = 0.02
RATE_DOWN = 0.01
RATE_VECTORS = 0.2

BF = jnp.bfloat16
F32 = jnp.float32
MESH = pl.DeviceIdType.MESH

RU, CW, H = 96, 768, 48
BLOCKS = 12
GATHER_ITEMS = ((0, 1), (2,), (3, 4), (5, 6), (7,), (8, 9), (10,), (11,))
REDUCE_ITEMS = ((10,), (8, 9), (11,), (4, 5), (6,), (0, 1), (7,), (3,), (2,))
VMEM_LIMIT = 62 * 2**20


def standardize(values):
    mean = jnp.mean(values, axis=-1, keepdims=True)
    centred = values - mean
    inverse = lax.rsqrt(jnp.mean(centred * centred, axis=-1, keepdims=True) + EPS_NORM)
    return (centred * inverse, inverse)


def norm_back(grad, normed, inverse, gain):
    scaled = grad * gain[None, :]
    first = jnp.mean(scaled, axis=-1, keepdims=True)
    second = jnp.mean(scaled * normed, axis=-1, keepdims=True)
    return (
        inverse * (scaled - first - normed * second),
        jnp.sum(grad * normed, axis=0),
        jnp.sum(grad, axis=0),
    )


def gelu_exact(values):
    return jax.nn.gelu(values, approximate=False)


def adamw(weight, grad, first, second, rate):
    new_first = BETA_ONE * first + (1.0 - BETA_ONE) * grad
    new_second = BETA_TWO * second + (1.0 - BETA_TWO) * grad * grad
    fix_one = 1.0 - BETA_ONE**STEP
    fix_two = 1.0 - BETA_TWO**STEP
    ratio = new_first / fix_one / (jnp.sqrt(new_second / fix_two) + ADAM_EPS)
    return (new_first, new_second, weight - rate * (ratio + DECAY * weight))


class Place:
    def __init__(self):
        dp, fs = lax.axis_index("dp"), lax.axis_index("fsdp")
        self.x, self.c = dp // 2, dp % 2
        self.z, self.y = fs // 2, fs % 2
        x, y, z, c = self.x, self.y, self.z, self.c
        self.sib = self.dev(x, y, z, 1 - c)
        self.xn = self.dev(1 - x, y, z, c)
        self.yn = self.dev(x, 1 - y, z, c)
        self.end = (z == 0) | (z == 3)
        self.mid = (z == 1) | (z == 2)
        self.inner = self.dev(x, y, z + 1 - 2 * (z // 2), c)
        self.outer = self.dev(x, y, (z + 3 + 2 * (z // 2)) % 4, c)
        self.up = self.dev(x, y, (z + 1) % 4, c)
        self.down = self.dev(x, y, (z + 3) % 4, c)
        self.far = self.dev(x, y, (z + 2) % 4, c)

    def dev(self, x, y, z, c):
        return (x * 2 + c, z * 2 + y)

    def mine(self, blocks):
        return blocks[0] if len(blocks) == 1 else blocks[0] + self.x * (blocks[1] - blocks[0])

    def theirs(self, blocks):
        return blocks[1] + self.x * (blocks[0] - blocks[1])


def arrived(ref, sem):
    pltpu.make_async_copy(ref, ref, sem).wait()


def add_into(dst, left, right):
    for row in range(0, dst.shape[-2], 16):
        dst[row : row + 16] = (left[row : row + 16].astype(F32) + right[row : row + 16].astype(F32)).astype(BF)


def gather_kernel(w_qkv, w_out, w_up, w_down, tile, full, tiles, own, zs, ys, xs, cs, vs, local_sem, snd):
    at = Place()
    x, y, z, c = at.x, at.y, at.z, at.c
    fs = z * 2 + y
    others = [((z + dz) % 4, (y + dy) % 2) for dz in range(4) for dy in range(2) if dz + dy > 0]
    barrier = pltpu.get_barrier_semaphore()
    peers = [at.sib, at.xn] + [at.dev(x, yy, zz, c) for zz, yy in others]
    for peer in peers:
        pl.semaphore_signal(barrier, inc=1, device_id=peer, device_id_type=MESH)
    for k in range(3):
        own[k] = w_qkv[:, k * CW : (k + 1) * CW].astype(BF)
    own[3] = w_out[...].astype(BF)
    for k in range(4):
        own[4 + k] = w_up[:, k * CW : (k + 1) * CW].astype(BF)
    for k in range(4):
        own[8 + k] = w_down[k * RU : (k + 1) * RU, :].astype(BF)
    pl.semaphore_wait(barrier, len(peers))
    local = pltpu.make_async_copy(own, full.at[:, z, y], local_sem.at[0])
    local.start()
    local_tile = pltpu.make_async_copy(tile, tiles.at[fs], local_sem.at[1])
    local_tile.start()
    half = pl.ds(pl.multiple_of(c * H, H), H)
    other = pl.ds(pl.multiple_of((1 - c) * H, H), H)
    sends = []

    def send(src, dst, sem, to, cond=None):
        copy = pltpu.make_async_remote_copy(
            src_ref=src, dst_ref=dst, send_sem=snd, recv_sem=sem, device_id=to, device_id_type=MESH
        )
        if cond is None:
            copy.start()
        else:
            pl.when(cond)(copy.start)
        sends.append((cond, copy))

    for k, (zz, yy) in enumerate(others):
        send(tile, tiles.at[fs], vs.at[fs], at.dev(x, yy, zz, c))

    def piece(j, zz, yy):
        return full.at[j, zz, yy, half, :]

    def start(i):
        j = at.mine(GATHER_ITEMS[i])
        src = own.at[j, half, :]
        send(src, piece(j, z, y), zs.at[i, 0, 0], at.up, z < 3)
        send(src, piece(j, z, y), zs.at[i, 0, 1], at.down, z > 0)
        send(src, piece(j, z, y), ys.at[i, z], at.yn)

    def hop(i, d):
        blocks = GATHER_ITEMS[i]
        j = at.mine(blocks)
        for way in (0, 1):
            has = (z - d - 1 >= 0) if way == 0 else (z + d + 1 <= 3)
            zz = jnp.maximum(z - d - 1, 0) if way == 0 else jnp.minimum(z + d + 1, 3)
            p = piece(j, zz, y)
            sem = zs.at[i, d, way]
            pl.when(has)(functools.partial(arrived, p, sem))
            if d < 2 and way == 0:
                send(p, p, zs.at[i, d + 1, 0], at.up, has & (z < 3))
            if d < 2 and way == 1:
                send(p, p, zs.at[i, d + 1, 1], at.down, has & (z > 0))
            send(p, p, ys.at[i, zz], at.yn, has)
            if len(blocks) == 2:
                send(p, p, xs.at[i, zz, y], at.xn, has)
            send(p, p, cs.at[j, zz, y], at.sib, has)

    def across(i):
        blocks = GATHER_ITEMS[i]
        j = at.mine(blocks)
        for dz in range(4):
            zz = (z + dz) % 4
            p = piece(j, zz, 1 - y)
            arrived(p, ys.at[i, zz])
            if len(blocks) == 2:
                send(p, p, xs.at[i, zz, 1 - y], at.xn)
            send(p, p, cs.at[j, zz, 1 - y], at.sib)

    def handed(i):
        if len(GATHER_ITEMS[i]) == 2:
            j = at.theirs(GATHER_ITEMS[i])
            for zz, yy in others:
                p = piece(j, zz, yy)
                arrived(p, xs.at[i, zz, yy])
                send(p, p, cs.at[j, zz, yy], at.sib)

    def shared(i):
        for j in GATHER_ITEMS[i]:
            for zz, yy in others:
                arrived(full.at[j, zz, yy, other, :], cs.at[j, zz, yy])

    n, lead = len(GATHER_ITEMS), 3
    for i in range(lead):
        start(i)
    for t in range(n + 5):
        if t + lead < n:
            start(t + lead)
        for d in range(3):
            if 0 <= t - d < n:
                hop(t - d, d)
        for stage, lag in ((across, 3), (handed, 4), (shared, 5)):
            if 0 <= t - lag < n:
                stage(t - lag)
    for zz, yy in others:
        arrived(tiles.at[zz * 2 + yy], vs.at[zz * 2 + yy])
    for cond, copy in sends:
        if cond is None:
            copy.wait_send()
        else:
            pl.when(cond)(copy.wait_send)
    local.wait()
    local_tile.wait()


def gather_weights(w_qkv, w_out, w_up, w_down, tile):
    n = len(GATHER_ITEMS)
    vmem = pl.BlockSpec(memory_space=pltpu.VMEM)
    dma = pltpu.SemaphoreType.DMA
    return pl.pallas_call(
        gather_kernel,
        out_shape=(
            jax.ShapeDtypeStruct((BLOCKS, 4, 2, RU, CW), BF),
            jax.ShapeDtypeStruct((8,) + tile.shape, BF),
        ),
        in_specs=[vmem] * 5,
        out_specs=(vmem, vmem),
        scratch_shapes=[
            pltpu.VMEM((BLOCKS, RU, CW), BF),
            dma((n, 3, 2)),
            dma((n, 4)),
            dma((n, 4, 2)),
            dma((BLOCKS, 4, 2)),
            dma((8,)),
            dma((2,)),
            dma,
        ],
        compiler_params=pltpu.CompilerParams(collective_id=0, has_side_effects=True, vmem_limit_bytes=VMEM_LIMIT),
        name="gather_weights",
    )(w_qkv, w_out, w_up, w_down, tile)


class Task:
    def __init__(self, name, time, needs, sends=(), rank=0):
        self.name, self.time, self.needs, self.sends, self.rank = name, time, tuple(needs), tuple(sends), rank


def plan(tasks, rates, window, arrive, sent, issue=0.1):
    now = 0.0
    links = {name: dict(active={}, queue=[], over=[], late=[], last=0.0) for name in rates}
    done, left, order, count = {}, list(tasks), [], 0

    def advance(to):
        for name, link in links.items():
            at = link["last"]
            while link["active"]:
                share = rates[name] / len(link["active"])
                token = min(link["active"], key=lambda q: link["active"][q])
                rest = link["active"][token]
                end = at + rest / share
                if end > to + 1e-9:
                    for q in link["active"]:
                        link["active"][q] -= (to - at) * share
                    at = to
                    break
                for q in link["active"]:
                    link["active"][q] -= rest
                del link["active"][token]
                at = end
                done[token] = end + arrive
                link["late"].append((end + sent, token))
            link["last"] = max(at, to)

    while left or any(link["queue"] or link["active"] for link in links.values()):
        advance(now)
        moved = False
        for name, link in links.items():
            link["over"] += [q[1] for q in link["late"] if q[0] <= now]
            link["late"] = [q for q in link["late"] if q[0] > now]
            while link["queue"] and len(link["active"]) + len(link["late"]) < window[name]:
                link["queue"].sort()
                _, _, token, size = link["queue"].pop(0)
                order.append(("issue", token, link["over"]))
                link["over"] = []
                now += issue
                advance(now)
                link["active"][token] = size
                moved = True
        ready = [q for q in left if all(done.get(need, 1e18) <= now for need in q.needs)]
        if ready:
            task = min(ready, key=lambda q: q.rank)
            left.remove(task)
            order.append(("run", task.name))
            now += task.time
            advance(now)
            done[task.name] = now
            for name, size, token, rank in task.sends:
                count += 1
                links[name]["queue"].append((rank, count, token, size))
            moved = True
        if not moved:
            times = [v for v in done.values() if v > now]
            for name, link in links.items():
                times += [q[0] for q in link["late"] if q[0] > now]
                if link["active"]:
                    times.append(link["last"] + min(link["active"].values()) * len(link["active"]) / rates[name])
            now = max(min(times), now) + 1e-6
    order.append(("waits", [t for link in links.values() for t in link["over"] + [q[1] for q in link["late"]]]))
    return order


RATES = dict(c=350e3, x=45e3, y=45e3, z=45e3, w=45e3, v=45e3)
WINDOW = dict(c=8, x=8, y=8, z=8, w=8, v=8)
SPLIT = 3


def reduce_items():
    rows = H // SPLIT
    return [(blocks, k * rows, rows) for blocks in REDUCE_ITEMS for k in range(SPLIT)]


def reduce_tasks(items, made):
    tasks = []
    for i, (blocks, _, rows) in enumerate(items):
        pair, size, add = len(blocks) == 2, rows * CW * 2, 0.04 * rows / H
        needs = [made[j] for j in blocks if made[j] is not None]
        to_sib = [("c", 8 * size, ("mine", i), i)]
        to_y = [("y", 2 * size, ("y0", i), i), ("y", 2 * size, ("y1", i), i)]
        if pair:
            to_x = [("x", 4 * size, ("x0", i), i), ("x", 4 * size, ("x1", i), i)]
            tasks.append(Task(("A", i), 0.05, needs, [("c", 8 * size, ("theirs", i), i)] + to_sib, i))
            tasks.append(Task(("Bt", i), 8 * add, [("theirs", i)], to_x, i))
            tasks.append(Task(("Bm", i), 8 * add, [("mine", i)], [], i))
            tasks.append(Task(("C", i), 8 * add, [("x0", i), ("x1", i), ("Bm", i)], to_y, i))
        else:
            tasks.append(Task(("A", i), 0.05, needs, to_sib, i))
            tasks.append(Task(("Bm", i), 8 * add, [("mine", i)], to_y, i))
        tasks.append(Task(("D", i), 4 * add, [("y0", i), ("y1", i)], [("z", 3 * size, ("za", i), i)], i))
        tasks.append(Task(("E1", i), 3 * add, [("za", i)], [("w", 2 * size, ("zb", i), i - 50)], i))
        tasks.append(Task(("E2", i), 2 * add, [("zb", i)], [("v", size, ("zc", i), i - 50)], i))
        tasks.append(Task(("E3", i), add, [("zc", i)], [("x", size, ("xf", i), i - 100)], i))
        finals = [("f%d" % k, i) for k in range(len(blocks))]
        tasks.append(Task(("G", i), 2 * add, [("xf", i)], [("c", size, f, i) for f in finals], i))
        tasks.append(Task(("H", i), 0.05, finals, [], i))
    return tasks


def vector_tasks(made):
    size = 8 * CW * 4
    needs = [] if made is None else [made]
    return [
        Task(("V0", 0), 0.05, needs, [("c", size, ("vc", 0), -200)], -200),
        Task(("V1", 0), 0.05, [("vc", 0)], [("x", size, ("vx", 0), -200)], -200),
        Task(("V2", 0), 0.05, [("vx", 0)], [("y", size, ("vy", 0), -200)], -200),
        Task(("V3", 0), 0.05, [("vy", 0)], [("z", size, ("vz%d" % d, 0), -200) for d in (1, 2, 3)], -200),
        Task(("V4", 0), 0.05, [("vz%d" % d, 0) for d in (1, 2, 3)], [], -200),
    ]


class Sender:
    def __init__(self, sems, window):
        self.sems, self.queued, self.under_way = sems, {}, {}
        self.free, first = {}, 0
        for name, slots in window.items():
            self.free[name] = list(range(first, first + slots))
            first += slots

    def put(self, token, link, src, dst, sem, to, cond=None):
        self.queued[token] = (link, src, dst, sem, to, cond)

    def issue(self, token, over):
        self.wait(over)
        link, src, dst, sem, to, cond = self.queued.pop(token)
        slot = self.free[link].pop(0)
        copy = pltpu.make_async_remote_copy(
            src_ref=src, dst_ref=dst, send_sem=self.sems.at[slot], recv_sem=sem, device_id=to, device_id_type=MESH
        )
        if cond is None:
            copy.start()
        else:
            pl.when(cond)(copy.start)
        self.under_way[token] = (link, slot, copy, cond)

    def wait(self, tokens):
        for token in tokens:
            link, slot, copy, cond = self.under_way.pop(token)
            self.free[link].append(slot)
            if cond is None:
                copy.wait_send()
            else:
                pl.when(cond)(copy.wait_send)


class Reducer:
    def __init__(self, at, items, sender, g, fin, sr, xr, yr, zr, xf, vec, vr, sems):
        self.at, self.items, self.sender = at, items, sender
        self.g, self.fin, self.sr, self.xr, self.yr, self.zr, self.xf = g, fin, sr, xr, yr, zr, xf
        self.vec, self.vr = vec, vr
        self.ssem, self.xsem, self.ysem, self.zsem, self.xfsem, self.fsem, self.vsem = sems

    def run(self, op, i):
        if op[0] == "V":
            return self.vectors(op)
        at, g, y, z = self.at, self.g, self.at.y, self.at.z
        blocks, first, count = self.items[i]
        pair, key, m = len(blocks) == 2, blocks[0], self.at.mine(blocks)
        loc = pl.ds(first, count)
        own_rows = pl.ds(pl.multiple_of(at.c * H + first, 16), count)
        sib_rows = pl.ds(pl.multiple_of((1 - at.c) * H + first, 16), count)

        def add_shards(j, src):
            def body(k, _):
                d = g.at[j, k // 2, k % 2, own_rows, :]
                add_into(d, d, src.at[k // 2, k % 2, loc, :])
                return 0

            lax.fori_loop(0, 8, body, 0)

        def to_y():
            for q in range(2):
                two = pl.ds(2 * q, 2)
                self.sender.put(
                    ("y%d" % q, i), "y", g.at[m, two, 1 - y, own_rows, :], self.yr.at[key, two, loc, :],
                    self.ysem.at[i, q], at.yn,
                )

        if op == "A":
            if pair:
                t = at.theirs(blocks)
                self.sender.put(
                    ("theirs", i), "c", g.at[t, :, :, sib_rows, :], self.sr.at[t, :, :, loc, :], self.ssem.at[i, 1], at.sib
                )
            self.sender.put(
                ("mine", i), "c", g.at[m, :, :, sib_rows, :], self.sr.at[m, :, :, loc, :], self.ssem.at[i, 0], at.sib
            )
        elif op == "Bm":
            arrived(self.sr.at[m, :, :, loc, :], self.ssem.at[i, 0])
            add_shards(m, self.sr.at[m])
            if not pair:
                to_y()
        elif op == "Bt":
            t = at.theirs(blocks)
            arrived(self.sr.at[t, :, :, loc, :], self.ssem.at[i, 1])
            add_shards(t, self.sr.at[t])
            for q in range(2):
                two = pl.ds(2 * q, 2)
                self.sender.put(
                    ("x%d" % q, i), "x", g.at[t, two, :, own_rows, :], self.xr.at[key // 4, two, :, loc, :],
                    self.xsem.at[i, q], at.xn,
                )
        elif op == "C":
            for q in range(2):
                arrived(self.xr.at[key // 4, pl.ds(2 * q, 2), :, loc, :], self.xsem.at[i, q])
            add_shards(m, self.xr.at[key // 4])
            to_y()
        elif op == "D":
            for q in range(2):
                arrived(self.yr.at[key, pl.ds(2 * q, 2), loc, :], self.ysem.at[i, q])

            def body(k, _):
                d = g.at[m, k, y, own_rows, :]
                add_into(d, d, self.yr.at[key, k, loc, :])
                return 0

            lax.fori_loop(0, 4, body, 0)
            self.sender.put(
                ("za", i), "z", g.at[m, pl.ds(1 - z // 3, 3), y, own_rows, :], self.zr.at[key, pl.ds(0, 3), loc, :],
                self.zsem.at[i, 0], at.inner, at.end,
            )
        elif op == "E1":

            @pl.when(at.mid)
            def _():
                arrived(self.zr.at[key, pl.ds(0, 3), loc, :], self.zsem.at[i, 0])
                for k in range(3):
                    d = g.at[m, 2 - z + k, y, own_rows, :]
                    add_into(d, d, self.zr.at[key, k, loc, :])

            self.sender.put(
                ("zb", i), "w", g.at[m, pl.ds(2 * (2 - z), 2), y, own_rows, :], self.zr.at[key, pl.ds(3, 2), loc, :],
                self.zsem.at[i, 1], at.inner, at.mid,
            )
        elif op == "E2":

            @pl.when(at.mid)
            def _():
                arrived(self.zr.at[key, pl.ds(3, 2), loc, :], self.zsem.at[i, 1])
                for k in range(2):
                    d = g.at[m, 2 * (z - 1) + k, y, own_rows, :]
                    add_into(d, d, self.zr.at[key, 3 + k, loc, :])

            self.sender.put(
                ("zc", i), "v", g.at[m, 3 * (z - 1), y, own_rows, :], self.zr.at[key, 0, loc, :],
                self.zsem.at[i, 2], at.outer, at.mid,
            )
        elif op == "E3":
            d = g.at[m, z, y, own_rows, :]

            @pl.when(at.end)
            def _():
                arrived(self.zr.at[key, 0, loc, :], self.zsem.at[i, 2])
                add_into(d, d, self.zr.at[key, 0, loc, :])

            self.sender.put(("xf", i), "x", d, self.xf.at[key, loc, :], self.xfsem.at[i], at.xn)
        elif op == "G":
            arrived(self.xf.at[key, loc, :], self.xfsem.at[i])
            d = g.at[m, z, y, own_rows, :]
            if pair:
                self.fin[m, own_rows, :] = d[...]
                self.fin[at.theirs(blocks), own_rows, :] = self.xf[key, loc, :]
            else:
                add_into(self.fin.at[m, own_rows, :], d, self.xf.at[key, loc, :])
            for k, j in enumerate((m, at.theirs(blocks)) if pair else blocks):
                f = self.fin.at[j, own_rows, :]
                self.sender.put(("f%d" % k, i), "c", f, f, self.fsem.at[i, k], at.sib)
        elif op == "H":
            for k, j in enumerate((m, at.theirs(blocks)) if pair else blocks):
                arrived(self.fin.at[j, sib_rows, :], self.fsem.at[i, k])

    def vectors(self, op):
        at, vec, vr, vsem = self.at, self.vec, self.vr, self.vsem
        if op == "V0":
            self.sender.put(("vc", 0), "c", vec.at[0], vr.at[0], vsem.at[0], at.sib)
        elif op == "V1":
            arrived(vr.at[0], vsem.at[0])
            vec[1] = vec[0] + vr[0]
            self.sender.put(("vx", 0), "x", vec.at[1], vr.at[1], vsem.at[1], at.xn)
        elif op == "V2":
            arrived(vr.at[1], vsem.at[1])
            vec[2] = vec[1] + vr[1]
            self.sender.put(("vy", 0), "y", vec.at[2], vr.at[2], vsem.at[2], at.yn)
        elif op == "V3":
            arrived(vr.at[2], vsem.at[2])
            vec[3] = vec[2] + vr[2]
            vr[3 + at.z] = vec[3]
            for d, to in ((1, at.up), (2, at.far), (3, at.down)):
                self.sender.put(("vz%d" % d, 0), "z", vec.at[3], vr.at[3 + at.z], vsem.at[3 + at.z], to)
        else:
            for d in (1, 2, 3):
                arrived(vr.at[3 + (at.z + d) % 4], vsem.at[3 + (at.z + d) % 4])
            vec[4] = ((vr[3] + vr[4]) + vr[5]) + vr[6]


def reduce_barrier(at):
    barrier = pltpu.get_barrier_semaphore()
    peers = [at.sib, at.xn, at.yn, at.up, at.far, at.down]
    for peer in peers:
        pl.semaphore_signal(barrier, inc=1, device_id=peer, device_id_type=MESH)
    pl.semaphore_wait(barrier, len(peers))


def reduce_scratch(n):
    dma = pltpu.SemaphoreType.DMA
    return [
        pltpu.VMEM((BLOCKS, 4, 2, H, CW), BF),
        pltpu.VMEM((3, 4, 2, H, CW), BF),
        pltpu.VMEM((BLOCKS, 4, H, CW), BF),
        pltpu.VMEM((BLOCKS, 5, H, CW), BF),
        pltpu.VMEM((BLOCKS, H, CW), BF),
        pltpu.VMEM((5, 8, CW), F32),
        pltpu.VMEM((7, 8, CW), F32),
        dma((n, 2)),
        dma((n, 2)),
        dma((n, 2)),
        dma((n, 3)),
        dma((n,)),
        dma((n, 2)),
        dma((7,)),
        dma((sum(WINDOW.values()),)),
    ]


def reduce_kernel(items, order, g_in, vec_in, fin, vec_out, g, sr, xr, yr, zr, xf, vec, vr, *sems):
    at = Place()
    load = pltpu.make_async_copy(g_in, g, sems[-1])
    load.start()
    vec[0] = vec_in[...]
    reduce_barrier(at)
    load.wait()
    sender = Sender(sems[-2], WINDOW)
    steps = Reducer(at, items, sender, g, fin, sr, xr, yr, zr, xf, vec, vr, sems[:7])
    for entry in order:
        if entry[0] == "run":
            steps.run(*entry[1])
        elif entry[0] == "issue":
            sender.issue(entry[1], entry[2])
        else:
            sender.wait(entry[1])
    vec_out[...] = vec[4]


def reduce_grads(g, vec):
    items = reduce_items()
    order = plan(reduce_tasks(items, [None] * BLOCKS) + vector_tasks(None), RATES, WINDOW, 6.0, 3.0)
    vmem = pl.BlockSpec(memory_space=pltpu.VMEM)
    return pl.pallas_call(
        functools.partial(reduce_kernel, items, order),
        out_shape=(jax.ShapeDtypeStruct((BLOCKS, RU, CW), BF), jax.ShapeDtypeStruct((8, CW), F32)),
        in_specs=[pl.BlockSpec(memory_space=pl.ANY), vmem],
        out_specs=(vmem, vmem),
        scratch_shapes=[pltpu.VMEM((BLOCKS, 4, 2, RU, CW), BF)]
        + reduce_scratch(len(items))
        + [pltpu.SemaphoreType.DMA],
        compiler_params=pltpu.CompilerParams(collective_id=1, has_side_effects=True, vmem_limit_bytes=VMEM_LIMIT),
        name="reduce_grads",
    )(g, vec)


def on_device_plain(
    tokens,
    mask_flags,
    mask_counts,
    cotangent,
    w_qkv,
    w_out,
    w_up,
    w_down,
    vectors,
    first_qkv,
    first_out,
    first_up,
    first_down,
    first_vectors,
    second_qkv,
    second_out,
    second_up,
    second_down,
    second_vectors,
):
    rows, width = tokens.shape
    images = mask_counts.shape[0]
    length = rows // images
    factor = HEAD_DIM ** (-0.5)
    attn_shards = (
        w_qkv.astype(jnp.bfloat16),
        w_out.astype(jnp.bfloat16),
        vectors.astype(jnp.bfloat16),
    )
    mlp_shards = (w_up.astype(jnp.bfloat16), w_down.astype(jnp.bfloat16))
    full_qkv, full_out, full_vec = (
        lax.all_gather(attn_shards[0], "fsdp", axis=0, tiled=True),
        lax.all_gather(attn_shards[1], "fsdp", axis=0, tiled=True),
        lax.all_gather(attn_shards[2], "fsdp", axis=0, tiled=True),
    )
    full_up, full_down = (
        lax.all_gather(mlp_shards[0], "fsdp", axis=0, tiled=True),
        lax.all_gather(mlp_shards[1], "fsdp", axis=0, tiled=True),
    )
    params = full_vec.astype(jnp.float32)
    masked = (mask_flags == 1)[:, None]
    hidden = jnp.where(masked, params[:, 4][None, :], tokens.astype(jnp.float32))
    normed_one, inverse_one = standardize(hidden)
    entry_one = (normed_one * params[:, 0] + params[:, 1]).astype(jnp.bfloat16)
    project = jnp.dot(entry_one, full_qkv, preferred_element_type=jnp.float32).astype(jnp.bfloat16)
    split = project.reshape(images, length, 3, HEADS, HEAD_DIM)
    queries = split[:, :, 0]
    keys = split[:, :, 1]
    values = split[:, :, 2]
    scores = (
        jnp.einsum("bqhd,bkhd->bhqk", queries, keys, preferred_element_type=jnp.float32) * factor
    )
    top = jnp.max(scores, axis=-1, keepdims=True)
    total = jnp.sum(jnp.exp(scores - top), axis=-1, keepdims=True)
    logsum = top + jnp.log(total)
    probs_low = jnp.exp(scores - logsum).astype(jnp.bfloat16)
    mixed = jnp.einsum("bhqk,bkhd->bqhd", probs_low, values, preferred_element_type=jnp.float32)
    attended = mixed.astype(jnp.bfloat16).reshape(rows, width)
    middle = hidden + jnp.dot(attended, full_out, preferred_element_type=jnp.float32)
    normed_two, inverse_two = standardize(middle)
    entry_two = (normed_two * params[:, 2] + params[:, 3]).astype(jnp.bfloat16)
    rising = jnp.dot(entry_two, full_up, preferred_element_type=jnp.float32)
    activated, gelu_pull = jax.vjp(gelu_exact, rising)
    active = activated.astype(jnp.bfloat16)
    layer_out = (middle + jnp.dot(active, full_down, preferred_element_type=jnp.float32)).astype(
        jnp.bfloat16
    )
    row_weight = jnp.repeat(
        length / mask_counts.astype(jnp.float32), length, total_repeat_length=rows
    )
    grad_out = (
        cotangent.astype(jnp.float32) * (row_weight * mask_flags.astype(jnp.float32))[:, None]
    )
    back_up, back_down = (
        lax.all_gather(mlp_shards[0], "fsdp", axis=0, tiled=True),
        lax.all_gather(mlp_shards[1], "fsdp", axis=0, tiled=True),
    )
    back_qkv, back_out, back_vec = (
        lax.all_gather(attn_shards[0], "fsdp", axis=0, tiled=True),
        lax.all_gather(attn_shards[1], "fsdp", axis=0, tiled=True),
        lax.all_gather(attn_shards[2], "fsdp", axis=0, tiled=True),
    )
    gains = back_vec.astype(jnp.float32)
    grad_low = grad_out.astype(jnp.bfloat16)
    grad_down = jnp.einsum("tf,td->fd", active, grad_low, preferred_element_type=jnp.float32)
    grad_active = jnp.einsum("td,fd->tf", grad_low, back_down, preferred_element_type=jnp.float32)
    grad_rising = gelu_pull(grad_active)[0].astype(jnp.bfloat16)
    grad_up = jnp.einsum("td,tf->df", entry_two, grad_rising, preferred_element_type=jnp.float32)
    grad_entry_two = jnp.einsum(
        "tf,df->td", grad_rising, back_up, preferred_element_type=jnp.float32
    )
    mlp_sums = (
        lax.psum_scatter(grad_up, "fsdp", scatter_dimension=0, tiled=True),
        lax.psum_scatter(grad_down, "fsdp", scatter_dimension=0, tiled=True),
    )
    back_two, gain_two, bias_two = norm_back(grad_entry_two, normed_two, inverse_two, gains[:, 2])
    grad_middle = grad_out + back_two
    middle_low = grad_middle.astype(jnp.bfloat16)
    grad_wout = jnp.einsum("tc,td->cd", attended, middle_low, preferred_element_type=jnp.float32)
    grad_attended = jnp.einsum(
        "td,cd->tc", middle_low, back_out, preferred_element_type=jnp.float32
    )
    grad_attended = grad_attended.astype(jnp.bfloat16).reshape(images, length, HEADS, HEAD_DIM)
    again_scores = (
        jnp.einsum("bqhd,bkhd->bhqk", queries, keys, preferred_element_type=jnp.float32) * factor
    )
    probs = jnp.exp(again_scores - logsum)
    again_low = probs.astype(jnp.bfloat16)
    grad_values = jnp.einsum(
        "bhqk,bqhd->bkhd", again_low, grad_attended, preferred_element_type=jnp.float32
    )
    grad_probs = jnp.einsum(
        "bqhd,bkhd->bhqk", grad_attended, values, preferred_element_type=jnp.float32
    )
    grad_scores = probs * (grad_probs - jnp.sum(grad_probs * probs, axis=-1, keepdims=True))
    grad_raw = (grad_scores * factor).astype(jnp.bfloat16)
    grad_queries = jnp.einsum("bhqk,bkhd->bqhd", grad_raw, keys, preferred_element_type=jnp.float32)
    grad_keys = jnp.einsum("bhqk,bqhd->bkhd", grad_raw, queries, preferred_element_type=jnp.float32)
    grad_project = (
        jnp.stack([grad_queries, grad_keys, grad_values], axis=2)
        .reshape(rows, 3 * width)
        .astype(jnp.bfloat16)
    )
    grad_qkv = jnp.einsum("td,te->de", entry_one, grad_project, preferred_element_type=jnp.float32)
    grad_entry_one = jnp.einsum(
        "te,de->td", grad_project, back_qkv, preferred_element_type=jnp.float32
    )
    back_one, gain_one, bias_one = norm_back(grad_entry_one, normed_one, inverse_one, gains[:, 0])
    grad_hidden = back_one + grad_middle
    token_grad = jnp.where(masked, 0.0, grad_hidden).astype(jnp.bfloat16)
    grad_mask = jnp.sum(jnp.where(masked, grad_hidden, 0.0), axis=0)
    grad_vec = jnp.stack([gain_one, bias_one, gain_two, bias_two, grad_mask], axis=1)
    attn_sums = (
        lax.psum_scatter(grad_qkv, "fsdp", scatter_dimension=0, tiled=True),
        lax.psum_scatter(grad_wout, "fsdp", scatter_dimension=0, tiled=True),
        lax.psum_scatter(grad_vec, "fsdp", scatter_dimension=0, tiled=True),
    )
    sum_qkv, sum_out, sum_vec, sum_up, sum_down = (
        lax.psum(attn_sums[0].astype(jnp.bfloat16), "dp").astype(jnp.float32),
        lax.psum(attn_sums[1].astype(jnp.bfloat16), "dp").astype(jnp.float32),
        lax.psum(attn_sums[2].astype(jnp.bfloat16), "dp").astype(jnp.float32),
        lax.psum(mlp_sums[0].astype(jnp.bfloat16), "dp").astype(jnp.float32),
        lax.psum(mlp_sums[1].astype(jnp.bfloat16), "dp").astype(jnp.float32),
    )
    qkv_first, qkv_second, qkv_new = adamw(w_qkv, sum_qkv, first_qkv, second_qkv, RATE_QKV)
    out_first, out_second, out_new = adamw(w_out, sum_out, first_out, second_out, RATE_OUT)
    up_first, up_second, up_new = adamw(w_up, sum_up, first_up, second_up, RATE_UP)
    down_first, down_second, down_new = adamw(w_down, sum_down, first_down, second_down, RATE_DOWN)
    vec_first, vec_second, vec_new = adamw(
        vectors, sum_vec, first_vectors, second_vectors, RATE_VECTORS
    )
    second_front = jnp.concatenate([vec_second[:, 0:2], vec_second[:, 4:5]], axis=1)
    second_later = vec_second[:, 2:4]
    return (
        layer_out,
        token_grad,
        qkv_first,
        out_first,
        up_first,
        down_first,
        vec_first,
        qkv_second,
        out_second,
        up_second,
        down_second,
        second_front,
        second_later,
        qkv_new,
        out_new,
        up_new,
        down_new,
        vec_new,
    )


def on_device_fast(
    tokens,
    mask_flags,
    mask_counts,
    cotangent,
    w_qkv,
    w_out,
    w_up,
    w_down,
    vectors,
    first_qkv,
    first_out,
    first_up,
    first_down,
    first_vectors,
    second_qkv,
    second_out,
    second_up,
    second_down,
    second_vectors,
):
    rows, width = tokens.shape
    images = mask_counts.shape[0]
    length = rows // images
    factor = HEAD_DIM ** (-0.5)
    fs = lax.axis_index("fsdp")
    tile = jnp.pad(vectors.astype(BF).T, ((0, 11), (0, 128 - RU)))
    full, tiles = gather_weights(w_qkv, w_out, w_up, w_down, tile)
    params = tiles[:, :5, :RU].transpose(0, 2, 1).reshape(width, 5).astype(F32)
    full = full.reshape(BLOCKS, CW, CW)
    full_down = full[8:12].reshape(4, 8, RU, CW).transpose(1, 0, 2, 3).reshape(4 * CW, CW)
    masked = (mask_flags == 1)[:, None]
    hidden = jnp.where(masked, params[:, 4][None, :], tokens.astype(F32))
    normed_one, inverse_one = standardize(hidden)
    entry_one = (normed_one * params[:, 0] + params[:, 1]).astype(BF)
    queries, keys, values = [
        jnp.dot(entry_one, full[k], preferred_element_type=F32).astype(BF).reshape(images, length, HEADS, HEAD_DIM)
        for k in range(3)
    ]
    scores = (
        jnp.einsum("bqhd,bkhd->bhqk", queries, keys, preferred_element_type=F32) * factor
    )
    top = jnp.max(scores, axis=-1, keepdims=True)
    total = jnp.sum(jnp.exp(scores - top), axis=-1, keepdims=True)
    logsum = top + jnp.log(total)
    probs_low = jnp.exp(scores - logsum).astype(BF)
    mixed = jnp.einsum("bhqk,bkhd->bqhd", probs_low, values, preferred_element_type=F32)
    attended = mixed.astype(BF).reshape(rows, width)
    middle = hidden + jnp.dot(attended, full[3], preferred_element_type=F32)
    normed_two, inverse_two = standardize(middle)
    entry_two = (normed_two * params[:, 2] + params[:, 3]).astype(BF)
    full_up = jnp.concatenate([full[4 + k] for k in range(4)], axis=1)
    rising = jnp.dot(entry_two, full_up, preferred_element_type=F32)
    activated, gelu_pull = jax.vjp(gelu_exact, rising)
    active = activated.astype(BF)
    layer_out = (middle + jnp.dot(active, full_down, preferred_element_type=F32)).astype(
        BF
    )
    row_weight = jnp.repeat(
        length / mask_counts.astype(F32), length, total_repeat_length=rows
    )
    grad_out = (
        cotangent.astype(F32) * (row_weight * mask_flags.astype(F32))[:, None]
    )
    grad_low = grad_out.astype(jnp.bfloat16)
    grad_down = jnp.einsum("tf,td->fd", active, grad_low, preferred_element_type=jnp.float32)
    grad_active = jnp.einsum("td,fd->tf", grad_low, full_down, preferred_element_type=jnp.float32)
    grad_rising = gelu_pull(grad_active)[0].astype(jnp.bfloat16)
    grad_up = jnp.einsum("td,tf->df", entry_two, grad_rising, preferred_element_type=jnp.float32)
    grad_entry_two = jnp.einsum(
        "tf,df->td", grad_rising, full_up, preferred_element_type=jnp.float32
    )
    back_two, gain_two, bias_two = norm_back(grad_entry_two, normed_two, inverse_two, params[:, 2])
    grad_middle = grad_out + back_two
    middle_low = grad_middle.astype(jnp.bfloat16)
    grad_wout = jnp.einsum("tc,td->cd", attended, middle_low, preferred_element_type=jnp.float32)
    grad_attended = jnp.einsum(
        "td,cd->tc", middle_low, full[3], preferred_element_type=jnp.float32
    )
    grad_attended = grad_attended.astype(jnp.bfloat16).reshape(images, length, HEADS, HEAD_DIM)
    again_scores = (
        jnp.einsum("bqhd,bkhd->bhqk", queries, keys, preferred_element_type=jnp.float32) * factor
    )
    probs = jnp.exp(again_scores - logsum)
    again_low = probs.astype(jnp.bfloat16)
    grad_values = jnp.einsum(
        "bhqk,bqhd->bkhd", again_low, grad_attended, preferred_element_type=jnp.float32
    )
    grad_probs = jnp.einsum(
        "bqhd,bkhd->bhqk", grad_attended, values, preferred_element_type=jnp.float32
    )
    grad_scores = probs * (grad_probs - jnp.sum(grad_probs * probs, axis=-1, keepdims=True))
    grad_raw = (grad_scores * factor).astype(jnp.bfloat16)
    grad_queries = jnp.einsum("bhqk,bkhd->bqhd", grad_raw, keys, preferred_element_type=jnp.float32)
    grad_keys = jnp.einsum("bhqk,bqhd->bkhd", grad_raw, queries, preferred_element_type=jnp.float32)
    grad_parts = [p.reshape(rows, width).astype(BF) for p in (grad_queries, grad_keys, grad_values)]
    grad_qkv = [jnp.einsum("td,te->de", entry_one, p, preferred_element_type=F32) for p in grad_parts]
    grad_entry_one = sum(
        jnp.einsum("te,de->td", p, full[k], preferred_element_type=F32) for k, p in enumerate(grad_parts)
    )
    back_one, gain_one, bias_one = norm_back(grad_entry_one, normed_one, inverse_one, params[:, 0])
    grad_hidden = back_one + grad_middle
    token_grad = jnp.where(masked, 0.0, grad_hidden).astype(BF)
    grad_mask = jnp.sum(jnp.where(masked, grad_hidden, 0.0), axis=0)
    none = jnp.zeros_like(grad_mask)
    grad_vec = jnp.stack([gain_one, bias_one, gain_two, bias_two, grad_mask, none, none, none])
    grads = [p.astype(BF).reshape(1, 8, RU, CW) for p in grad_qkv + [grad_wout]]
    grads.append(grad_up.astype(BF).reshape(8, RU, 4, CW).transpose(2, 0, 1, 3))
    grads.append(grad_down.astype(BF).reshape(8, 4, RU, CW).transpose(1, 0, 2, 3))
    sums, sum_vec = reduce_grads(jnp.concatenate(grads).reshape(BLOCKS, 4, 2, RU, CW), grad_vec)
    sums = sums.astype(F32)
    sum_qkv = jnp.concatenate([sums[k] for k in range(3)], axis=1)
    sum_out = sums[3]
    sum_up = jnp.concatenate([sums[4 + k] for k in range(4)], axis=1)
    sum_down = sums[8:12].reshape(4 * RU, CW)
    sum_vec = lax.dynamic_slice(sum_vec, (0, fs * RU), (5, RU)).T
    qkv_first, qkv_second, qkv_new = adamw(w_qkv, sum_qkv, first_qkv, second_qkv, RATE_QKV)
    out_first, out_second, out_new = adamw(w_out, sum_out, first_out, second_out, RATE_OUT)
    up_first, up_second, up_new = adamw(w_up, sum_up, first_up, second_up, RATE_UP)
    down_first, down_second, down_new = adamw(w_down, sum_down, first_down, second_down, RATE_DOWN)
    vec_first, vec_second, vec_new = adamw(
        vectors, sum_vec, first_vectors, second_vectors, RATE_VECTORS
    )
    second_front = jnp.concatenate([vec_second[:, 0:2], vec_second[:, 4:5]], axis=1)
    second_later = vec_second[:, 2:4]
    return (
        layer_out,
        token_grad,
        qkv_first,
        out_first,
        up_first,
        down_first,
        vec_first,
        qkv_second,
        out_second,
        up_second,
        down_second,
        second_front,
        second_later,
        qkv_new,
        out_new,
        up_new,
        down_new,
        vec_new,
    )


def solution(mesh):
    placed = (
        P(("dp", "fsdp"), None),
        P(("dp", "fsdp")),
        P(("dp", "fsdp")),
        P(("dp", "fsdp"), None),
        P("fsdp", None),
        P("fsdp", None),
        P("fsdp", None),
        P("fsdp", None),
        P("fsdp", None),
        P("fsdp", None),
        P("fsdp", None),
        P("fsdp", None),
        P("fsdp", None),
        P("fsdp", None),
        P("fsdp", None),
        P("fsdp", None),
        P("fsdp", None),
        P("fsdp", None),
        P("fsdp", None),
    )
    shape = dict(mesh.shape)
    fast = shape["dp"] == 4 and shape["fsdp"] == 8
    return jax.shard_map(
        on_device_fast if fast else on_device_plain,
        mesh=mesh,
        in_specs=placed,
        out_specs=(
            P(("dp", "fsdp"), None),
            P(("dp", "fsdp"), None),
            P("fsdp", None),
            P("fsdp", None),
            P("fsdp", None),
            P("fsdp", None),
            P("fsdp", None),
            P("fsdp", None),
            P("fsdp", None),
            P("fsdp", None),
            P("fsdp", None),
            P("fsdp", None),
            P("fsdp", None),
            P("fsdp", None),
            P("fsdp", None),
            P("fsdp", None),
            P("fsdp", None),
            P("fsdp", None),
        ),
        check_vma=False,
    )
```

```python
import functools

import jax
import jax.numpy as jnp
from jax import lax
from jax.experimental import pallas as pl
from jax.experimental.pallas import tpu as pltpu
from jax.sharding import PartitionSpec as P

HEADS = 16
HEAD_DIM = 48
STEP = 10


EPS_NORM = 1e-06
BETA_ONE = 0.5
BETA_TWO = 0.5
ADAM_EPS = 1e-08
DECAY = 0.01
RATE_QKV = 0.02
RATE_OUT = 0.1
RATE_UP = 0.02
RATE_DOWN = 0.01
RATE_VECTORS = 0.2

BF = jnp.bfloat16
F32 = jnp.float32
MESH = pl.DeviceIdType.MESH

RU, CW, H = 96, 768, 48
BLOCKS = 12
GATHER_ITEMS = ((0, 1), (2,), (3, 4), (5, 6), (7,), (8, 9), (10,), (11,))
REDUCE_ITEMS = ((10,), (8, 9), (11,), (4, 5), (6,), (0, 1), (7,), (3,), (2,))
VMEM_LIMIT = 62 * 2**20


def standardize(values):
    mean = jnp.mean(values, axis=-1, keepdims=True)
    centred = values - mean
    inverse = lax.rsqrt(jnp.mean(centred * centred, axis=-1, keepdims=True) + EPS_NORM)
    return (centred * inverse, inverse)


def norm_back(grad, normed, inverse, gain):
    scaled = grad * gain[None, :]
    first = jnp.mean(scaled, axis=-1, keepdims=True)
    second = jnp.mean(scaled * normed, axis=-1, keepdims=True)
    return (
        inverse * (scaled - first - normed * second),
        jnp.sum(grad * normed, axis=0),
        jnp.sum(grad, axis=0),
    )


def gelu_exact(values):
    return jax.nn.gelu(values, approximate=False)


def adamw(weight, grad, first, second, rate):
    new_first = BETA_ONE * first + (1.0 - BETA_ONE) * grad
    new_second = BETA_TWO * second + (1.0 - BETA_TWO) * grad * grad
    fix_one = 1.0 - BETA_ONE**STEP
    fix_two = 1.0 - BETA_TWO**STEP
    ratio = new_first / fix_one / (jnp.sqrt(new_second / fix_two) + ADAM_EPS)
    return (new_first, new_second, weight - rate * (ratio + DECAY * weight))


class Place:
    def __init__(self):
        dp, fs = lax.axis_index("dp"), lax.axis_index("fsdp")
        self.x, self.c = dp // 2, dp % 2
        self.z, self.y = fs // 2, fs % 2
        x, y, z, c = self.x, self.y, self.z, self.c
        self.sib = self.dev(x, y, z, 1 - c)
        self.xn = self.dev(1 - x, y, z, c)
        self.yn = self.dev(x, 1 - y, z, c)
        self.end = (z == 0) | (z == 3)
        self.mid = (z == 1) | (z == 2)
        self.inner = self.dev(x, y, z + 1 - 2 * (z // 2), c)
        self.outer = self.dev(x, y, (z + 3 + 2 * (z // 2)) % 4, c)
        self.up = self.dev(x, y, (z + 1) % 4, c)
        self.down = self.dev(x, y, (z + 3) % 4, c)
        self.far = self.dev(x, y, (z + 2) % 4, c)

    def dev(self, x, y, z, c):
        return (x * 2 + c, z * 2 + y)

    def mine(self, blocks):
        return blocks[0] if len(blocks) == 1 else blocks[0] + self.x * (blocks[1] - blocks[0])

    def theirs(self, blocks):
        return blocks[1] + self.x * (blocks[0] - blocks[1])


def arrived(ref, sem):
    pltpu.make_async_copy(ref, ref, sem).wait()


def add_into(dst, left, right):
    for row in range(0, dst.shape[-2], 16):
        dst[row : row + 16] = (left[row : row + 16].astype(F32) + right[row : row + 16].astype(F32)).astype(BF)


ROWS, IMAGE = 512, 256
FACTOR = HEAD_DIM**-0.5
LOG2E = 1.4426950408889634


def dot(left, right, over_left=1, over_right=0):
    return lax.dot_general(left, right, (((over_left,), (over_right,)), ((), ())), preferred_element_type=F32)


def matrix(w, j):
    return w[j].reshape(CW, CW)


def down_rows(w, s):
    return jnp.concatenate([w[8 + k, s // 2, s % 2] for k in range(4)], axis=0)


def part(i, rows):
    return pl.ds(pl.multiple_of(i * rows, rows), rows)


def flag_column(flags, fcol):
    spot = lax.broadcasted_iota(jnp.int32, (IMAGE, IMAGE), 0) == lax.broadcasted_iota(jnp.int32, (IMAGE, IMAGE), 1)
    for b in range(2):
        row = jnp.broadcast_to((flags[:, b * IMAGE : (b + 1) * IMAGE] == 1).astype(F32), (8, IMAGE)).astype(BF)
        fcol[b * IMAGE : (b + 1) * IMAGE, :] = dot(spot.astype(F32).astype(BF), row, 1, 1)[:, 0:1]


def vector_tile(vectors, tile):
    pick = lax.broadcasted_iota(jnp.int32, (16, 5), 0) == lax.broadcasted_iota(jnp.int32, (16, 5), 1)
    tile[...] = jnp.zeros_like(tile)
    tile[:, 0:RU] = dot(pick.astype(F32).astype(BF), vectors[...].astype(BF), 1, 1).astype(BF)


def spread(s):
    row = lax.broadcasted_iota(jnp.int32, (128, CW), 0)
    column = lax.broadcasted_iota(jnp.int32, (128, CW), 1)
    return ((row < RU) & (column == row + s * RU)).astype(F32).astype(BF)


def vector_rows(tiles, pv):
    total = dot(tiles[0], spread(0))
    for s in range(1, 8):
        total = total + dot(tiles[s], spread(s))
    pv[...] = total


def hidden_rows(tok, fcol, pv, r):
    return jnp.where(fcol[r, :] > 0.5, pv[4:5, :], tok[r, :].astype(F32))


def norm_one(tok, fcol, pv, e1, i, rows=128):
    for k in range(rows // 64):
        r = pl.ds(pl.multiple_of(i * rows + k * 64, 64), 64)
        n, _ = standardize(hidden_rows(tok, fcol, pv, r))
        e1[r, :] = (n * pv[0:1, :] + pv[1:2, :]).astype(BF)


def project_part(e1, w, proj, j, i):
    r = part(i, 256)
    proj[j, r, :] = dot(e1[r, :], matrix(w, j)).astype(BF)


def head_lanes():
    return [(h * HEAD_DIM, range(h * HEAD_DIM // 128, (h * HEAD_DIM + HEAD_DIM - 1) // 128 + 1)) for h in range(8)]


def lane_mask(first, t):
    lane = lax.broadcasted_iota(jnp.int32, (1, 128), 1) + t * 128
    return ((lane >= first) & (lane < first + HEAD_DIM)).astype(F32).astype(BF)


def attend(proj, att, b, group):
    rows = part(b, IMAGE)

    def lanes(t):
        return pl.ds(pl.multiple_of(group * 384 + t * 128, 128), 128)

    acc = [None] * 3
    for first, tiles in head_lanes():
        masks = {t: lane_mask(first, t) for t in tiles}
        s = sum(dot(proj[0, rows, lanes(t)] * masks[t], proj[1, rows, lanes(t)], 1, 1) for t in tiles)
        top = jnp.max(s, axis=-1, keepdims=True)
        e = jnp.exp2((s - top) * (FACTOR * LOG2E))
        p = (e * (1.0 / jnp.sum(e, axis=-1, keepdims=True))).astype(BF)
        for t in tiles:
            o = dot(p, proj[2, rows, lanes(t)] * masks[t])
            acc[t] = o if acc[t] is None else acc[t] + o
    for t in range(3):
        att[rows, lanes(t)] = acc[t].astype(BF)


def norm_two(tok, fcol, pv, att, w, mid, e2, i):
    r = part(i, 256)
    v = hidden_rows(tok, fcol, pv, r) + dot(att[r, :], matrix(w, 3))
    mid[r, :] = v
    n, _ = standardize(v)
    e2[r, :] = (n * pv[2:3, :] + pv[3:4, :]).astype(BF)


def rise(e2, w, act, dg, k, i):
    r = part(i, 128)
    v = dot(e2[r, :], matrix(w, 4 + k))
    cdf = 0.5 * (1.0 + lax.erf(v * 0.7071067811865476))
    act[k, r, :] = (v * cdf).astype(BF)
    dg[k, r, :] = (cdf + v * (jnp.exp2(v * v * (-0.5 * LOG2E)) * 0.3989422804014327)).astype(BF)


def lower(act, w, mid, out, i):
    r = part(i, 256)
    total = mid[r, :]
    for s in range(8):
        total = total + dot(act[s // 2, r, (s % 2) * 384 : (s % 2) * 384 + 384], down_rows(w, s))
    out[r, :] = total.astype(BF)


class Gatherer:
    def __init__(self, at, w, zs, ys, xs, cs, snd):
        self.at, self.w, self.zs, self.ys, self.xs, self.cs, self.snd = at, w, zs, ys, xs, cs, snd
        self.half = pl.ds(pl.multiple_of(at.c * H, H), H)
        self.other = pl.ds(pl.multiple_of((1 - at.c) * H, H), H)
        self.others = [((at.z + dz) % 4, (at.y + dy) % 2) for dz in range(4) for dy in range(2) if dz + dy > 0]
        self.sends = []

    def send(self, src, dst, sem, to, cond=None):
        copy = pltpu.make_async_remote_copy(
            src_ref=src, dst_ref=dst, send_sem=self.snd, recv_sem=sem, device_id=to, device_id_type=MESH
        )
        if cond is None:
            copy.start()
        else:
            pl.when(cond)(copy.start)
        self.sends.append((cond, copy))

    def piece(self, j, z, y):
        return self.w.at[j, z, y, self.half, :]

    def start(self, i):
        at = self.at
        p = self.piece(at.mine(GATHER_ITEMS[i]), at.z, at.y)
        self.send(p, p, self.zs.at[i, 0, 0], at.up, at.z < 3)
        self.send(p, p, self.zs.at[i, 0, 1], at.down, at.z > 0)
        self.send(p, p, self.ys.at[i, at.z], at.yn)

    def hop(self, i, d):
        at, z, blocks = self.at, self.at.z, GATHER_ITEMS[i]
        j = at.mine(blocks)
        for way in (0, 1):
            has = (z - d - 1 >= 0) if way == 0 else (z + d + 1 <= 3)
            zz = jnp.maximum(z - d - 1, 0) if way == 0 else jnp.minimum(z + d + 1, 3)
            p = self.piece(j, zz, at.y)
            pl.when(has)(functools.partial(arrived, p, self.zs.at[i, d, way]))
            if d < 2 and way == 0:
                self.send(p, p, self.zs.at[i, d + 1, 0], at.up, has & (z < 3))
            if d < 2 and way == 1:
                self.send(p, p, self.zs.at[i, d + 1, 1], at.down, has & (z > 0))
            self.send(p, p, self.ys.at[i, zz], at.yn, has)
            if len(blocks) == 2:
                self.send(p, p, self.xs.at[i, zz, at.y], at.xn, has)
            self.send(p, p, self.cs.at[j, zz, at.y], at.sib, has)

    def across(self, i):
        at, blocks = self.at, GATHER_ITEMS[i]
        j, yy = at.mine(blocks), 1 - at.y
        for dz in range(4):
            zz = (at.z + dz) % 4
            p = self.piece(j, zz, yy)
            arrived(p, self.ys.at[i, zz])
            if len(blocks) == 2:
                self.send(p, p, self.xs.at[i, zz, yy], at.xn)
            self.send(p, p, self.cs.at[j, zz, yy], at.sib)

    def handed(self, i):
        if len(GATHER_ITEMS[i]) == 2:
            j = self.at.theirs(GATHER_ITEMS[i])
            for zz, yy in self.others:
                p = self.piece(j, zz, yy)
                arrived(p, self.xs.at[i, zz, yy])
                self.send(p, p, self.cs.at[j, zz, yy], self.at.sib)

    def shared(self, i):
        for j in GATHER_ITEMS[i]:
            for zz, yy in self.others:
                arrived(self.w.at[j, zz, yy, self.other, :], self.cs.at[j, zz, yy])

    def finish(self):
        for cond, copy in self.sends:
            if cond is None:
                copy.wait_send()
            else:
                pl.when(cond)(copy.wait_send)


def forward_kernel(
    w_qkv, w_out, w_up, w_down, vectors, tok, flags,
    lo_h, w_h, pv_h, e1_h, proj_h, att_h, mid_h, e2_h, act_h, dg_h,
    w, tile, tiles, pv, fcol, e1, proj, att, mid, e2, act, dg, lo, zs, ys, xs, cs, vs, save_sem, snd,
):
    at = Place()
    fs = at.z * 2 + at.y
    comm = Gatherer(at, w, zs, ys, xs, cs, snd)
    barrier = pltpu.get_barrier_semaphore()
    peers = [at.sib, at.xn] + [at.dev(at.x, yy, zz, at.c) for zz, yy in comm.others]
    for peer in peers:
        pl.semaphore_signal(barrier, inc=1, device_id=peer, device_id_type=MESH)
    vector_tile(vectors, tile)
    tiles[fs] = tile[...]
    for k in range(3):
        w[k, at.z, at.y] = w_qkv[:, k * CW : (k + 1) * CW].astype(BF)
    w[3, at.z, at.y] = w_out[...].astype(BF)
    for k in range(4):
        w[4 + k, at.z, at.y] = w_up[:, k * CW : (k + 1) * CW].astype(BF)
    for k in range(4):
        w[8 + k, at.z, at.y] = w_down[k * RU : (k + 1) * RU, :].astype(BF)
    pl.semaphore_wait(barrier, len(peers))
    for zz, yy in comm.others:
        comm.send(tile, tiles.at[fs], vs.at[fs], at.dev(at.x, yy, zz, at.c))
    saves = []

    def save(src, dst):
        copy = pltpu.make_async_copy(src, dst, save_sem.at[len(saves)])
        copy.start()
        saves.append(copy)

    def vectors_in():
        for zz, yy in comm.others:
            arrived(tiles.at[zz * 2 + yy], vs.at[zz * 2 + yy])
        vector_rows(tiles, pv)
        save(pv, pv_h)

    steps = [(-1, lambda: flag_column(flags, fcol)), (-1, vectors_in)]
    steps += [(-1, lambda i=i: norm_one(tok, fcol, pv, e1, i)) for i in range(4)]
    steps += [(0, lambda j=j, i=i: project_part(e1, w, proj, j, i)) for j in range(2) for i in range(2)]
    steps += [(1, lambda i=i: project_part(e1, w, proj, 2, i)) for i in range(2)]
    steps += [(1, lambda: save(e1, e1_h)), (1, lambda: save(proj, proj_h))]
    steps += [(1, lambda b=b, k=k: attend(proj, att, b, k)) for b in range(2) for k in range(2)]
    steps += [(2, lambda i=i: norm_two(tok, fcol, pv, att, w, mid, e2, i)) for i in range(2)]
    steps += [(2, lambda: save(att, att_h)), (2, lambda: save(mid, mid_h)), (2, lambda: save(e2, e2_h))]
    for k, need in enumerate((2, 3, 3, 4)):
        steps += [(need, lambda k=k, i=i: rise(e2, w, act, dg, k, i)) for i in range(4)]
        steps += [(need, lambda k=k: save(act.at[k], act_h.at[k])), (need, lambda k=k: save(dg.at[k], dg_h.at[k]))]
    steps += [(7, lambda i=i: lower(act, w, mid, lo, i)) for i in range(2)]
    steps += [(7, lambda: save(lo, lo_h))]
    there = -1

    def fill(count):
        while steps and count and steps[0][0] <= there:
            steps.pop(0)[1]()
            count -= 1

    n, lead = len(GATHER_ITEMS), 3
    for i in range(lead):
        comm.start(i)
    for t in range(n + 5):
        each = 1 if t < 8 else 2
        if t + lead < n:
            comm.start(t + lead)
        for d in range(3):
            if 0 <= t - d < n:
                comm.hop(t - d, d)
                fill(each if t else 0)
        for stage, lag in ((comm.across, 3), (comm.handed, 4), (comm.shared, 5)):
            if 0 <= t - lag < n:
                stage(t - lag)
                if lag == 5:
                    there = t - lag
                    for j in GATHER_ITEMS[there]:
                        save(w.at[j], w_h.at[j])
                fill(each)
    fill(len(steps))
    comm.finish()
    for copy in saves:
        copy.wait()


def forward(w_qkv, w_out, w_up, w_down, vectors, tokens, flags):
    n = len(GATHER_ITEMS)
    vmem, anywhere = pl.BlockSpec(memory_space=pltpu.VMEM), pl.BlockSpec(memory_space=pl.ANY)
    dma = pltpu.SemaphoreType.DMA
    whole, three, four = (ROWS, CW), (3, ROWS, CW), (4, ROWS, CW)
    shapes = [
        (whole, BF), ((BLOCKS, 4, 2, RU, CW), BF), ((16, CW), F32), (whole, BF), (three, BF), (whole, BF), (whole, F32),
        (whole, BF), (four, BF), (four, BF),
    ]
    return pl.pallas_call(
        forward_kernel,
        out_shape=[jax.ShapeDtypeStruct(s, t) for s, t in shapes],
        in_specs=[vmem] * 7,
        out_specs=[anywhere] * len(shapes),
        scratch_shapes=[
            pltpu.VMEM((BLOCKS, 4, 2, RU, CW), BF),
            pltpu.VMEM((16, 128), BF),
            pltpu.VMEM((8, 16, 128), BF),
            pltpu.VMEM((16, CW), F32),
            pltpu.VMEM((ROWS, 1), F32),
            pltpu.VMEM(whole, BF),
            pltpu.VMEM(three, BF),
            pltpu.VMEM(whole, BF),
            pltpu.VMEM(whole, F32),
            pltpu.VMEM(whole, BF),
            pltpu.VMEM(four, BF),
            pltpu.VMEM(four, BF),
            pltpu.VMEM(whole, BF),
            dma((n, 3, 2)),
            dma((n, 4)),
            dma((n, 4, 2)),
            dma((BLOCKS, 4, 2)),
            dma((8,)),
            dma((32,)),
            dma,
        ],
        compiler_params=pltpu.CompilerParams(collective_id=0, has_side_effects=True, vmem_limit_bytes=VMEM_LIMIT),
        name="forward",
    )(w_qkv, w_out, w_up, w_down, vectors, tokens, flags)


def grad_out_rows(cot, fcol, counts, r, b):
    weight = float(IMAGE) / jnp.full((1, 1), counts[b], jnp.int32).astype(F32)
    return cot[r, :].astype(F32) * (fcol[r, :] * weight)


def grad_low_part(cot, fcol, counts, gl, b):
    for k in range(4):
        r = pl.ds(b * IMAGE + k * 64, 64)
        gl[r, :] = grad_out_rows(cot, fcol, counts, r, b).astype(BF)


def grad_down_part(act, gl, g, s):
    d = dot(act[s // 2, :, (s % 2) * 384 : (s % 2) * 384 + 384], gl[...], 0, 0).astype(BF)
    for k in range(4):
        g[8 + k, s // 2, s % 2] = d[k * RU : (k + 1) * RU]


def grad_rising_part(gl, w, dg, s):
    lanes = slice((s % 2) * 384, (s % 2) * 384 + 384)
    grad = dot(gl[...], down_rows(w, s), 1, 1)
    dg[s // 2, :, lanes] = (grad * dg[s // 2, :, lanes].astype(F32)).astype(BF)


def weight_grad_part(left, right, g, j, i):
    d = dot(left[:, i * 384 : i * 384 + 384], right[...], 0, 0).astype(BF)
    g[j, 2 * i : 2 * i + 2] = d.reshape(2, 2, RU, CW)


def norm_back_rows(grad, n, inverse, gain):
    scaled = grad * gain
    first = jnp.mean(scaled, axis=-1, keepdims=True)
    second = jnp.mean(scaled * n, axis=-1, keepdims=True)
    return inverse * (scaled - first - n * second)


def row_sum(values):
    return jnp.sum(values, axis=0, keepdims=True)


def back_two_part(gr, w, mid, pv, cot, fcol, counts, gm, ml, vec, i):
    r = part(i, 128)
    grad = sum(dot(gr[k, r, :], matrix(w, 4 + k), 1, 1) for k in range(4))
    n, inverse = standardize(mid[r, :])
    total = grad_out_rows(cot, fcol, counts, r, i // 2) + norm_back_rows(grad, n, inverse, pv[2:3, :])
    gm[r, :] = total
    ml[r, :] = total.astype(BF)
    vec[0, 2:3, :] += row_sum(grad * n)
    vec[0, 3:4, :] += row_sum(grad)


def grad_attended_part(ml, w, ga, i):
    r = part(i, 256)
    ga[r, :] = dot(ml[r, :], matrix(w, 3), 1, 1).astype(BF)


def attend_back(proj, ga, dproj, b, group):
    rows = part(b, IMAGE)

    def lanes(t):
        return pl.ds(pl.multiple_of(group * 384 + t * 128, 128), 128)

    acc = [[None] * 3 for _ in range(3)]

    def add(k, t, value):
        acc[k][t] = value if acc[k][t] is None else acc[k][t] + value

    for first, tiles in head_lanes():
        s = grad = 0.0
        masked = {}
        for t in tiles:
            m = lane_mask(first, t)
            q, k, v, o = proj[0, rows, lanes(t)], proj[1, rows, lanes(t)], proj[2, rows, lanes(t)], ga[rows, lanes(t)]
            masked[t] = (q * m, k * m, o * m)
            s = s + dot(q * m, k, 1, 1)
            grad = grad + dot(o * m, v, 1, 1)
        top = jnp.max(s, axis=-1, keepdims=True)
        e = jnp.exp2((s - top) * (FACTOR * LOG2E))
        p = e * (1.0 / jnp.sum(e, axis=-1, keepdims=True))
        delta = jnp.sum(grad * p, axis=-1, keepdims=True)
        raw = (p * ((grad - delta) * FACTOR)).astype(BF)
        low = p.astype(BF)
        for t in tiles:
            q, k, o = masked[t]
            add(0, t, dot(raw, k))
            add(1, t, dot(raw, q, 0, 0))
            add(2, t, dot(low, o, 0, 0))
    for k in range(3):
        for t in range(3):
            dproj[k, rows, lanes(t)] = acc[k][t].astype(BF)


def back_one_part(dproj, w, tok, fcol, pv, gm, tg, vec, i):
    r = part(i, 128)
    grad = sum(dot(dproj[k, r, :], matrix(w, k), 1, 1) for k in range(3))
    n, inverse = standardize(hidden_rows(tok, fcol, pv, r))
    total = norm_back_rows(grad, n, inverse, pv[0:1, :]) + gm[r, :]
    on = fcol[r, :] > 0.5
    tg[r, :] = jnp.where(on, 0.0, total).astype(BF)
    vec[0, 0:1, :] += row_sum(grad * n)
    vec[0, 1:2, :] += row_sum(grad)
    vec[0, 4:5, :] += row_sum(jnp.where(on, total, 0.0))


def backward_kernel(
    tok, flags, counts, cot, pv, e1, proj, att, mid, e2, act, dg_in, w_h,
    tg, g_h, vec_out,
    w, g, fcol, gl, dg, gm, ml, ga, dproj, vec, sem,
):
    loads = [pltpu.make_async_copy(w_h.at[j], w.at[j], sem.at[j]) for j in range(BLOCKS)]
    for copy in loads:
        copy.start()
    vec[...] = jnp.zeros_like(vec)
    flag_column(flags, fcol)
    for b in range(2):
        grad_low_part(cot, fcol, counts, gl, b)
    for s in range(8):
        grad_down_part(act, gl, g, s)
    for copy in loads:
        copy.wait()
    dg[...] = dg_in[...]
    for s in range(8):
        grad_rising_part(gl, w, dg, s)
    for k in range(4):
        for i in range(2):
            weight_grad_part(e2, dg.at[k], g, 4 + k, i)
    for i in range(4):
        back_two_part(dg, w, mid, pv, cot, fcol, counts, gm, ml, vec, i)
    for i in range(2):
        weight_grad_part(att, ml, g, 3, i)
        grad_attended_part(ml, w, ga, i)
    for b in range(2):
        for k in range(2):
            attend_back(proj, ga, dproj, b, k)
    for j in range(3):
        for i in range(2):
            weight_grad_part(e1, dproj.at[j], g, j, i)
    saves = [pltpu.make_async_copy(g.at[j], g_h.at[j], sem.at[j]) for j in range(BLOCKS)]
    for copy in saves:
        copy.start()
    for i in range(4):
        back_one_part(dproj, w, tok, fcol, pv, gm, tg, vec, i)
    vec_out[...] = vec[0]
    for copy in saves:
        copy.wait()


def backward(tokens, flags, counts, cotangent, pv, e1, proj, att, mid, e2, act, dg, w):
    vmem, anywhere = pl.BlockSpec(memory_space=pltpu.VMEM), pl.BlockSpec(memory_space=pl.ANY)
    whole, three, four = (ROWS, CW), (3, ROWS, CW), (4, ROWS, CW)
    grads = (BLOCKS, 4, 2, RU, CW)
    return pl.pallas_call(
        backward_kernel,
        out_shape=[
            jax.ShapeDtypeStruct(whole, BF), jax.ShapeDtypeStruct(grads, BF), jax.ShapeDtypeStruct((8, CW), F32)
        ],
        in_specs=[vmem, vmem, pl.BlockSpec(memory_space=pltpu.SMEM)] + [vmem] * 9 + [anywhere],
        out_specs=[vmem, anywhere, vmem],
        scratch_shapes=[
            pltpu.VMEM(grads, BF),
            pltpu.VMEM(grads, BF),
            pltpu.VMEM((ROWS, 1), F32),
            pltpu.VMEM(whole, BF),
            pltpu.VMEM(four, BF),
            pltpu.VMEM(whole, F32),
            pltpu.VMEM(whole, BF),
            pltpu.VMEM(whole, BF),
            pltpu.VMEM(three, BF),
            pltpu.VMEM((1, 8, CW), F32),
            pltpu.SemaphoreType.DMA((BLOCKS,)),
        ],
        compiler_params=pltpu.CompilerParams(vmem_limit_bytes=VMEM_LIMIT),
        name="backward",
    )(tokens, flags, counts, cotangent, pv, e1, proj, att, mid, e2, act, dg, w)


class Task:
    def __init__(self, name, time, needs, sends=(), rank=0):
        self.name, self.time, self.needs, self.sends, self.rank = name, time, tuple(needs), tuple(sends), rank


def plan(tasks, rates, window, arrive, sent, issue=0.1):
    now = 0.0
    links = {name: dict(active={}, queue=[], over=[], late=[], last=0.0) for name in rates}
    done, left, order, count = {}, list(tasks), [], 0

    def advance(to):
        for name, link in links.items():
            at = link["last"]
            while link["active"]:
                share = rates[name] / len(link["active"])
                token = min(link["active"], key=lambda q: link["active"][q])
                rest = link["active"][token]
                end = at + rest / share
                if end > to + 1e-9:
                    for q in link["active"]:
                        link["active"][q] -= (to - at) * share
                    at = to
                    break
                for q in link["active"]:
                    link["active"][q] -= rest
                del link["active"][token]
                at = end
                done[token] = end + arrive
                link["late"].append((end + sent, token))
            link["last"] = max(at, to)

    while left or any(link["queue"] or link["active"] for link in links.values()):
        advance(now)
        moved = False
        for name, link in links.items():
            link["over"] += [q[1] for q in link["late"] if q[0] <= now]
            link["late"] = [q for q in link["late"] if q[0] > now]
            while link["queue"] and len(link["active"]) + len(link["late"]) < window[name]:
                link["queue"].sort()
                _, _, token, size = link["queue"].pop(0)
                order.append(("issue", token, link["over"]))
                link["over"] = []
                now += issue
                advance(now)
                link["active"][token] = size
                moved = True
        ready = [q for q in left if all(done.get(need, 1e18) <= now for need in q.needs)]
        if ready:
            task = min(ready, key=lambda q: q.rank)
            left.remove(task)
            order.append(("run", task.name))
            now += task.time
            advance(now)
            done[task.name] = now
            for name, size, token, rank in task.sends:
                count += 1
                links[name]["queue"].append((rank, count, token, size))
            moved = True
        if not moved:
            times = [v for v in done.values() if v > now]
            for name, link in links.items():
                times += [q[0] for q in link["late"] if q[0] > now]
                if link["active"]:
                    times.append(link["last"] + min(link["active"].values()) * len(link["active"]) / rates[name])
            now = max(min(times), now) + 1e-6
    order.append(("waits", [t for link in links.values() for t in link["over"] + [q[1] for q in link["late"]]]))
    return order


RATES = dict(c=350e3, x=45e3, y=45e3, z=45e3, w=45e3, v=45e3)
WINDOW = dict(c=8, x=8, y=8, z=8, w=8, v=8)
SPLIT = 3


def reduce_items():
    rows = H // SPLIT
    return [(blocks, k * rows, rows) for blocks in REDUCE_ITEMS for k in range(SPLIT)]


def reduce_tasks(items, made):
    tasks = []
    for i, (blocks, _, rows) in enumerate(items):
        pair, size, add = len(blocks) == 2, rows * CW * 2, 0.04 * rows / H
        needs = [made[j] for j in blocks if made[j] is not None]
        to_sib = [("c", 8 * size, ("mine", i), i)]
        to_y = [("y", 2 * size, ("y0", i), i), ("y", 2 * size, ("y1", i), i)]
        if pair:
            to_x = [("x", 4 * size, ("x0", i), i), ("x", 4 * size, ("x1", i), i)]
            tasks.append(Task(("A", i), 0.05, needs, [("c", 8 * size, ("theirs", i), i)] + to_sib, i))
            tasks.append(Task(("Bt", i), 8 * add, [("theirs", i)], to_x, i))
            tasks.append(Task(("Bm", i), 8 * add, [("mine", i)], [], i))
            tasks.append(Task(("C", i), 8 * add, [("x0", i), ("x1", i), ("Bm", i)], to_y, i))
        else:
            tasks.append(Task(("A", i), 0.05, needs, to_sib, i))
            tasks.append(Task(("Bm", i), 8 * add, [("mine", i)], to_y, i))
        tasks.append(Task(("D", i), 4 * add, [("y0", i), ("y1", i)], [("z", 3 * size, ("za", i), i)], i))
        tasks.append(Task(("E1", i), 3 * add, [("za", i)], [("w", 2 * size, ("zb", i), i - 50)], i))
        tasks.append(Task(("E2", i), 2 * add, [("zb", i)], [("v", size, ("zc", i), i - 50)], i))
        tasks.append(Task(("E3", i), add, [("zc", i)], [("x", size, ("xf", i), i - 100)], i))
        finals = [("f%d" % k, i) for k in range(len(blocks))]
        tasks.append(Task(("G", i), 2 * add, [("xf", i)], [("c", size, f, i) for f in finals], i))
        tasks.append(Task(("H", i), 0.05, finals, [], i))
    return tasks


def vector_tasks(made):
    size = 8 * CW * 4
    needs = [] if made is None else [made]
    return [
        Task(("V0", 0), 0.05, needs, [("c", size, ("vc", 0), -200)], -200),
        Task(("V1", 0), 0.05, [("vc", 0)], [("x", size, ("vx", 0), -200)], -200),
        Task(("V2", 0), 0.05, [("vx", 0)], [("y", size, ("vy", 0), -200)], -200),
        Task(("V3", 0), 0.05, [("vy", 0)], [("z", size, ("vz%d" % d, 0), -200) for d in (1, 2, 3)], -200),
        Task(("V4", 0), 0.05, [("vz%d" % d, 0) for d in (1, 2, 3)], [], -200),
    ]


class Sender:
    def __init__(self, sems, window):
        self.sems, self.queued, self.under_way = sems, {}, {}
        self.free, first = {}, 0
        for name, slots in window.items():
            self.free[name] = list(range(first, first + slots))
            first += slots

    def put(self, token, link, src, dst, sem, to, cond=None):
        self.queued[token] = (link, src, dst, sem, to, cond)

    def issue(self, token, over):
        self.wait(over)
        link, src, dst, sem, to, cond = self.queued.pop(token)
        slot = self.free[link].pop(0)
        copy = pltpu.make_async_remote_copy(
            src_ref=src, dst_ref=dst, send_sem=self.sems.at[slot], recv_sem=sem, device_id=to, device_id_type=MESH
        )
        if cond is None:
            copy.start()
        else:
            pl.when(cond)(copy.start)
        self.under_way[token] = (link, slot, copy, cond)

    def wait(self, tokens):
        for token in tokens:
            link, slot, copy, cond = self.under_way.pop(token)
            self.free[link].append(slot)
            if cond is None:
                copy.wait_send()
            else:
                pl.when(cond)(copy.wait_send)


class Reducer:
    def __init__(self, at, items, sender, g, fin, sr, xr, yr, zr, xf, vec, vr, sems):
        self.at, self.items, self.sender = at, items, sender
        self.g, self.fin, self.sr, self.xr, self.yr, self.zr, self.xf = g, fin, sr, xr, yr, zr, xf
        self.vec, self.vr = vec, vr
        self.ssem, self.xsem, self.ysem, self.zsem, self.xfsem, self.fsem, self.vsem = sems

    def run(self, op, i):
        if op[0] == "V":
            return self.vectors(op)
        at, g, y, z = self.at, self.g, self.at.y, self.at.z
        blocks, first, count = self.items[i]
        pair, key, m = len(blocks) == 2, blocks[0], self.at.mine(blocks)
        loc = pl.ds(first, count)
        own_rows = pl.ds(pl.multiple_of(at.c * H + first, 16), count)
        sib_rows = pl.ds(pl.multiple_of((1 - at.c) * H + first, 16), count)

        def add_shards(j, src):
            def body(k, _):
                d = g.at[j, k // 2, k % 2, own_rows, :]
                add_into(d, d, src.at[k // 2, k % 2, loc, :])
                return 0

            lax.fori_loop(0, 8, body, 0)

        def to_y():
            for q in range(2):
                two = pl.ds(2 * q, 2)
                self.sender.put(
                    ("y%d" % q, i), "y", g.at[m, two, 1 - y, own_rows, :], self.yr.at[key, two, loc, :],
                    self.ysem.at[i, q], at.yn,
                )

        if op == "A":
            if pair:
                t = at.theirs(blocks)
                self.sender.put(
                    ("theirs", i), "c", g.at[t, :, :, sib_rows, :], self.sr.at[t, :, :, loc, :], self.ssem.at[i, 1], at.sib
                )
            self.sender.put(
                ("mine", i), "c", g.at[m, :, :, sib_rows, :], self.sr.at[m, :, :, loc, :], self.ssem.at[i, 0], at.sib
            )
        elif op == "Bm":
            arrived(self.sr.at[m, :, :, loc, :], self.ssem.at[i, 0])
            add_shards(m, self.sr.at[m])
            if not pair:
                to_y()
        elif op == "Bt":
            t = at.theirs(blocks)
            arrived(self.sr.at[t, :, :, loc, :], self.ssem.at[i, 1])
            add_shards(t, self.sr.at[t])
            for q in range(2):
                two = pl.ds(2 * q, 2)
                self.sender.put(
                    ("x%d" % q, i), "x", g.at[t, two, :, own_rows, :], self.xr.at[key // 4, two, :, loc, :],
                    self.xsem.at[i, q], at.xn,
                )
        elif op == "C":
            for q in range(2):
                arrived(self.xr.at[key // 4, pl.ds(2 * q, 2), :, loc, :], self.xsem.at[i, q])
            add_shards(m, self.xr.at[key // 4])
            to_y()
        elif op == "D":
            for q in range(2):
                arrived(self.yr.at[key, pl.ds(2 * q, 2), loc, :], self.ysem.at[i, q])

            def body(k, _):
                d = g.at[m, k, y, own_rows, :]
                add_into(d, d, self.yr.at[key, k, loc, :])
                return 0

            lax.fori_loop(0, 4, body, 0)
            self.sender.put(
                ("za", i), "z", g.at[m, pl.ds(1 - z // 3, 3), y, own_rows, :], self.zr.at[key, pl.ds(0, 3), loc, :],
                self.zsem.at[i, 0], at.inner, at.end,
            )
        elif op == "E1":

            @pl.when(at.mid)
            def _():
                arrived(self.zr.at[key, pl.ds(0, 3), loc, :], self.zsem.at[i, 0])
                for k in range(3):
                    d = g.at[m, 2 - z + k, y, own_rows, :]
                    add_into(d, d, self.zr.at[key, k, loc, :])

            self.sender.put(
                ("zb", i), "w", g.at[m, pl.ds(2 * (2 - z), 2), y, own_rows, :], self.zr.at[key, pl.ds(3, 2), loc, :],
                self.zsem.at[i, 1], at.inner, at.mid,
            )
        elif op == "E2":

            @pl.when(at.mid)
            def _():
                arrived(self.zr.at[key, pl.ds(3, 2), loc, :], self.zsem.at[i, 1])
                for k in range(2):
                    d = g.at[m, 2 * (z - 1) + k, y, own_rows, :]
                    add_into(d, d, self.zr.at[key, 3 + k, loc, :])

            self.sender.put(
                ("zc", i), "v", g.at[m, 3 * (z - 1), y, own_rows, :], self.zr.at[key, 0, loc, :],
                self.zsem.at[i, 2], at.outer, at.mid,
            )
        elif op == "E3":
            d = g.at[m, z, y, own_rows, :]

            @pl.when(at.end)
            def _():
                arrived(self.zr.at[key, 0, loc, :], self.zsem.at[i, 2])
                add_into(d, d, self.zr.at[key, 0, loc, :])

            self.sender.put(("xf", i), "x", d, self.xf.at[key, loc, :], self.xfsem.at[i], at.xn)
        elif op == "G":
            arrived(self.xf.at[key, loc, :], self.xfsem.at[i])
            d = g.at[m, z, y, own_rows, :]
            if pair:
                self.fin[m, own_rows, :] = d[...]
                self.fin[at.theirs(blocks), own_rows, :] = self.xf[key, loc, :]
            else:
                add_into(self.fin.at[m, own_rows, :], d, self.xf.at[key, loc, :])
            for k, j in enumerate((m, at.theirs(blocks)) if pair else blocks):
                f = self.fin.at[j, own_rows, :]
                self.sender.put(("f%d" % k, i), "c", f, f, self.fsem.at[i, k], at.sib)
        elif op == "H":
            for k, j in enumerate((m, at.theirs(blocks)) if pair else blocks):
                arrived(self.fin.at[j, sib_rows, :], self.fsem.at[i, k])

    def vectors(self, op):
        at, vec, vr, vsem = self.at, self.vec, self.vr, self.vsem
        if op == "V0":
            self.sender.put(("vc", 0), "c", vec.at[0], vr.at[0], vsem.at[0], at.sib)
        elif op == "V1":
            arrived(vr.at[0], vsem.at[0])
            vec[1] = vec[0] + vr[0]
            self.sender.put(("vx", 0), "x", vec.at[1], vr.at[1], vsem.at[1], at.xn)
        elif op == "V2":
            arrived(vr.at[1], vsem.at[1])
            vec[2] = vec[1] + vr[1]
            self.sender.put(("vy", 0), "y", vec.at[2], vr.at[2], vsem.at[2], at.yn)
        elif op == "V3":
            arrived(vr.at[2], vsem.at[2])
            vec[3] = vec[2] + vr[2]
            vr[3 + at.z] = vec[3]
            for d, to in ((1, at.up), (2, at.far), (3, at.down)):
                self.sender.put(("vz%d" % d, 0), "z", vec.at[3], vr.at[3 + at.z], vsem.at[3 + at.z], to)
        else:
            for d in (1, 2, 3):
                arrived(vr.at[3 + (at.z + d) % 4], vsem.at[3 + (at.z + d) % 4])
            vec[4] = ((vr[3] + vr[4]) + vr[5]) + vr[6]


def reduce_barrier(at):
    barrier = pltpu.get_barrier_semaphore()
    peers = [at.sib, at.xn, at.yn, at.up, at.far, at.down]
    for peer in peers:
        pl.semaphore_signal(barrier, inc=1, device_id=peer, device_id_type=MESH)
    pl.semaphore_wait(barrier, len(peers))


def reduce_scratch(n):
    dma = pltpu.SemaphoreType.DMA
    return [
        pltpu.VMEM((BLOCKS, 4, 2, H, CW), BF),
        pltpu.VMEM((3, 4, 2, H, CW), BF),
        pltpu.VMEM((BLOCKS, 4, H, CW), BF),
        pltpu.VMEM((BLOCKS, 5, H, CW), BF),
        pltpu.VMEM((BLOCKS, H, CW), BF),
        pltpu.VMEM((5, 8, CW), F32),
        pltpu.VMEM((7, 8, CW), F32),
        dma((n, 2)),
        dma((n, 2)),
        dma((n, 2)),
        dma((n, 3)),
        dma((n,)),
        dma((n, 2)),
        dma((7,)),
        dma((sum(WINDOW.values()),)),
    ]


def reduce_kernel(items, order, g_in, vec_in, fin, vec_out, g, sr, xr, yr, zr, xf, vec, vr, *sems):
    at = Place()
    load = pltpu.make_async_copy(g_in, g, sems[-1])
    load.start()
    vec[0] = vec_in[...]
    reduce_barrier(at)
    load.wait()
    sender = Sender(sems[-2], WINDOW)
    steps = Reducer(at, items, sender, g, fin, sr, xr, yr, zr, xf, vec, vr, sems[:7])
    for entry in order:
        if entry[0] == "run":
            steps.run(*entry[1])
        elif entry[0] == "issue":
            sender.issue(entry[1], entry[2])
        else:
            sender.wait(entry[1])
    vec_out[...] = vec[4]


def reduce_grads(g, vec):
    items = reduce_items()
    order = plan(reduce_tasks(items, [None] * BLOCKS) + vector_tasks(None), RATES, WINDOW, 6.0, 3.0)
    vmem = pl.BlockSpec(memory_space=pltpu.VMEM)
    return pl.pallas_call(
        functools.partial(reduce_kernel, items, order),
        out_shape=(jax.ShapeDtypeStruct((BLOCKS, RU, CW), BF), jax.ShapeDtypeStruct((8, CW), F32)),
        in_specs=[pl.BlockSpec(memory_space=pl.ANY), vmem],
        out_specs=(vmem, vmem),
        scratch_shapes=[pltpu.VMEM((BLOCKS, 4, 2, RU, CW), BF)]
        + reduce_scratch(len(items))
        + [pltpu.SemaphoreType.DMA],
        compiler_params=pltpu.CompilerParams(collective_id=1, has_side_effects=True, vmem_limit_bytes=VMEM_LIMIT),
        name="reduce_grads",
    )(g, vec)


def on_device_plain(
    tokens,
    mask_flags,
    mask_counts,
    cotangent,
    w_qkv,
    w_out,
    w_up,
    w_down,
    vectors,
    first_qkv,
    first_out,
    first_up,
    first_down,
    first_vectors,
    second_qkv,
    second_out,
    second_up,
    second_down,
    second_vectors,
):
    rows, width = tokens.shape
    images = mask_counts.shape[0]
    length = rows // images
    factor = HEAD_DIM ** (-0.5)
    attn_shards = (
        w_qkv.astype(jnp.bfloat16),
        w_out.astype(jnp.bfloat16),
        vectors.astype(jnp.bfloat16),
    )
    mlp_shards = (w_up.astype(jnp.bfloat16), w_down.astype(jnp.bfloat16))
    full_qkv, full_out, full_vec = (
        lax.all_gather(attn_shards[0], "fsdp", axis=0, tiled=True),
        lax.all_gather(attn_shards[1], "fsdp", axis=0, tiled=True),
        lax.all_gather(attn_shards[2], "fsdp", axis=0, tiled=True),
    )
    full_up, full_down = (
        lax.all_gather(mlp_shards[0], "fsdp", axis=0, tiled=True),
        lax.all_gather(mlp_shards[1], "fsdp", axis=0, tiled=True),
    )
    params = full_vec.astype(jnp.float32)
    masked = (mask_flags == 1)[:, None]
    hidden = jnp.where(masked, params[:, 4][None, :], tokens.astype(jnp.float32))
    normed_one, inverse_one = standardize(hidden)
    entry_one = (normed_one * params[:, 0] + params[:, 1]).astype(jnp.bfloat16)
    project = jnp.dot(entry_one, full_qkv, preferred_element_type=jnp.float32).astype(jnp.bfloat16)
    split = project.reshape(images, length, 3, HEADS, HEAD_DIM)
    queries = split[:, :, 0]
    keys = split[:, :, 1]
    values = split[:, :, 2]
    scores = (
        jnp.einsum("bqhd,bkhd->bhqk", queries, keys, preferred_element_type=jnp.float32) * factor
    )
    top = jnp.max(scores, axis=-1, keepdims=True)
    total = jnp.sum(jnp.exp(scores - top), axis=-1, keepdims=True)
    logsum = top + jnp.log(total)
    probs_low = jnp.exp(scores - logsum).astype(jnp.bfloat16)
    mixed = jnp.einsum("bhqk,bkhd->bqhd", probs_low, values, preferred_element_type=jnp.float32)
    attended = mixed.astype(jnp.bfloat16).reshape(rows, width)
    middle = hidden + jnp.dot(attended, full_out, preferred_element_type=jnp.float32)
    normed_two, inverse_two = standardize(middle)
    entry_two = (normed_two * params[:, 2] + params[:, 3]).astype(jnp.bfloat16)
    rising = jnp.dot(entry_two, full_up, preferred_element_type=jnp.float32)
    activated, gelu_pull = jax.vjp(gelu_exact, rising)
    active = activated.astype(jnp.bfloat16)
    layer_out = (middle + jnp.dot(active, full_down, preferred_element_type=jnp.float32)).astype(
        jnp.bfloat16
    )
    row_weight = jnp.repeat(
        length / mask_counts.astype(jnp.float32), length, total_repeat_length=rows
    )
    grad_out = (
        cotangent.astype(jnp.float32) * (row_weight * mask_flags.astype(jnp.float32))[:, None]
    )
    back_up, back_down = (
        lax.all_gather(mlp_shards[0], "fsdp", axis=0, tiled=True),
        lax.all_gather(mlp_shards[1], "fsdp", axis=0, tiled=True),
    )
    back_qkv, back_out, back_vec = (
        lax.all_gather(attn_shards[0], "fsdp", axis=0, tiled=True),
        lax.all_gather(attn_shards[1], "fsdp", axis=0, tiled=True),
        lax.all_gather(attn_shards[2], "fsdp", axis=0, tiled=True),
    )
    gains = back_vec.astype(jnp.float32)
    grad_low = grad_out.astype(jnp.bfloat16)
    grad_down = jnp.einsum("tf,td->fd", active, grad_low, preferred_element_type=jnp.float32)
    grad_active = jnp.einsum("td,fd->tf", grad_low, back_down, preferred_element_type=jnp.float32)
    grad_rising = gelu_pull(grad_active)[0].astype(jnp.bfloat16)
    grad_up = jnp.einsum("td,tf->df", entry_two, grad_rising, preferred_element_type=jnp.float32)
    grad_entry_two = jnp.einsum(
        "tf,df->td", grad_rising, back_up, preferred_element_type=jnp.float32
    )
    mlp_sums = (
        lax.psum_scatter(grad_up, "fsdp", scatter_dimension=0, tiled=True),
        lax.psum_scatter(grad_down, "fsdp", scatter_dimension=0, tiled=True),
    )
    back_two, gain_two, bias_two = norm_back(grad_entry_two, normed_two, inverse_two, gains[:, 2])
    grad_middle = grad_out + back_two
    middle_low = grad_middle.astype(jnp.bfloat16)
    grad_wout = jnp.einsum("tc,td->cd", attended, middle_low, preferred_element_type=jnp.float32)
    grad_attended = jnp.einsum(
        "td,cd->tc", middle_low, back_out, preferred_element_type=jnp.float32
    )
    grad_attended = grad_attended.astype(jnp.bfloat16).reshape(images, length, HEADS, HEAD_DIM)
    again_scores = (
        jnp.einsum("bqhd,bkhd->bhqk", queries, keys, preferred_element_type=jnp.float32) * factor
    )
    probs = jnp.exp(again_scores - logsum)
    again_low = probs.astype(jnp.bfloat16)
    grad_values = jnp.einsum(
        "bhqk,bqhd->bkhd", again_low, grad_attended, preferred_element_type=jnp.float32
    )
    grad_probs = jnp.einsum(
        "bqhd,bkhd->bhqk", grad_attended, values, preferred_element_type=jnp.float32
    )
    grad_scores = probs * (grad_probs - jnp.sum(grad_probs * probs, axis=-1, keepdims=True))
    grad_raw = (grad_scores * factor).astype(jnp.bfloat16)
    grad_queries = jnp.einsum("bhqk,bkhd->bqhd", grad_raw, keys, preferred_element_type=jnp.float32)
    grad_keys = jnp.einsum("bhqk,bqhd->bkhd", grad_raw, queries, preferred_element_type=jnp.float32)
    grad_project = (
        jnp.stack([grad_queries, grad_keys, grad_values], axis=2)
        .reshape(rows, 3 * width)
        .astype(jnp.bfloat16)
    )
    grad_qkv = jnp.einsum("td,te->de", entry_one, grad_project, preferred_element_type=jnp.float32)
    grad_entry_one = jnp.einsum(
        "te,de->td", grad_project, back_qkv, preferred_element_type=jnp.float32
    )
    back_one, gain_one, bias_one = norm_back(grad_entry_one, normed_one, inverse_one, gains[:, 0])
    grad_hidden = back_one + grad_middle
    token_grad = jnp.where(masked, 0.0, grad_hidden).astype(jnp.bfloat16)
    grad_mask = jnp.sum(jnp.where(masked, grad_hidden, 0.0), axis=0)
    grad_vec = jnp.stack([gain_one, bias_one, gain_two, bias_two, grad_mask], axis=1)
    attn_sums = (
        lax.psum_scatter(grad_qkv, "fsdp", scatter_dimension=0, tiled=True),
        lax.psum_scatter(grad_wout, "fsdp", scatter_dimension=0, tiled=True),
        lax.psum_scatter(grad_vec, "fsdp", scatter_dimension=0, tiled=True),
    )
    sum_qkv, sum_out, sum_vec, sum_up, sum_down = (
        lax.psum(attn_sums[0].astype(jnp.bfloat16), "dp").astype(jnp.float32),
        lax.psum(attn_sums[1].astype(jnp.bfloat16), "dp").astype(jnp.float32),
        lax.psum(attn_sums[2].astype(jnp.bfloat16), "dp").astype(jnp.float32),
        lax.psum(mlp_sums[0].astype(jnp.bfloat16), "dp").astype(jnp.float32),
        lax.psum(mlp_sums[1].astype(jnp.bfloat16), "dp").astype(jnp.float32),
    )
    qkv_first, qkv_second, qkv_new = adamw(w_qkv, sum_qkv, first_qkv, second_qkv, RATE_QKV)
    out_first, out_second, out_new = adamw(w_out, sum_out, first_out, second_out, RATE_OUT)
    up_first, up_second, up_new = adamw(w_up, sum_up, first_up, second_up, RATE_UP)
    down_first, down_second, down_new = adamw(w_down, sum_down, first_down, second_down, RATE_DOWN)
    vec_first, vec_second, vec_new = adamw(
        vectors, sum_vec, first_vectors, second_vectors, RATE_VECTORS
    )
    second_front = jnp.concatenate([vec_second[:, 0:2], vec_second[:, 4:5]], axis=1)
    second_later = vec_second[:, 2:4]
    return (
        layer_out,
        token_grad,
        qkv_first,
        out_first,
        up_first,
        down_first,
        vec_first,
        qkv_second,
        out_second,
        up_second,
        down_second,
        second_front,
        second_later,
        qkv_new,
        out_new,
        up_new,
        down_new,
        vec_new,
    )


def on_device_fast(
    tokens,
    mask_flags,
    mask_counts,
    cotangent,
    w_qkv,
    w_out,
    w_up,
    w_down,
    vectors,
    first_qkv,
    first_out,
    first_up,
    first_down,
    first_vectors,
    second_qkv,
    second_out,
    second_up,
    second_down,
    second_vectors,
):
    flags = mask_flags.reshape(1, ROWS)
    layer_out, w, pv, e1, proj, att, mid, e2, act, dg = forward(w_qkv, w_out, w_up, w_down, vectors, tokens, flags)
    token_grad, grads, grad_vec = backward(
        tokens, flags, mask_counts, cotangent, pv, e1, proj, att, mid, e2, act, dg, w
    )
    sums, sum_vec = reduce_grads(grads, grad_vec)
    sums = sums.astype(F32)
    sum_qkv = jnp.concatenate([sums[k] for k in range(3)], axis=1)
    sum_out = sums[3]
    sum_up = jnp.concatenate([sums[4 + k] for k in range(4)], axis=1)
    sum_down = sums[8:12].reshape(4 * RU, CW)
    sum_vec = lax.dynamic_slice(sum_vec, (0, lax.axis_index("fsdp") * RU), (5, RU)).T
    qkv_first, qkv_second, qkv_new = adamw(w_qkv, sum_qkv, first_qkv, second_qkv, RATE_QKV)
    out_first, out_second, out_new = adamw(w_out, sum_out, first_out, second_out, RATE_OUT)
    up_first, up_second, up_new = adamw(w_up, sum_up, first_up, second_up, RATE_UP)
    down_first, down_second, down_new = adamw(w_down, sum_down, first_down, second_down, RATE_DOWN)
    vec_first, vec_second, vec_new = adamw(
        vectors, sum_vec, first_vectors, second_vectors, RATE_VECTORS
    )
    second_front = jnp.concatenate([vec_second[:, 0:2], vec_second[:, 4:5]], axis=1)
    second_later = vec_second[:, 2:4]
    return (
        layer_out,
        token_grad,
        qkv_first,
        out_first,
        up_first,
        down_first,
        vec_first,
        qkv_second,
        out_second,
        up_second,
        down_second,
        second_front,
        second_later,
        qkv_new,
        out_new,
        up_new,
        down_new,
        vec_new,
    )


def solution(mesh):
    placed = (
        P(("dp", "fsdp"), None),
        P(("dp", "fsdp")),
        P(("dp", "fsdp")),
        P(("dp", "fsdp"), None),
        P("fsdp", None),
        P("fsdp", None),
        P("fsdp", None),
        P("fsdp", None),
        P("fsdp", None),
        P("fsdp", None),
        P("fsdp", None),
        P("fsdp", None),
        P("fsdp", None),
        P("fsdp", None),
        P("fsdp", None),
        P("fsdp", None),
        P("fsdp", None),
        P("fsdp", None),
        P("fsdp", None),
    )
    shape = dict(mesh.shape)
    fast = shape["dp"] == 4 and shape["fsdp"] == 8
    return jax.shard_map(
        on_device_fast if fast else on_device_plain,
        mesh=mesh,
        in_specs=placed,
        out_specs=(
            P(("dp", "fsdp"), None),
            P(("dp", "fsdp"), None),
            P("fsdp", None),
            P("fsdp", None),
            P("fsdp", None),
            P("fsdp", None),
            P("fsdp", None),
            P("fsdp", None),
            P("fsdp", None),
            P("fsdp", None),
            P("fsdp", None),
            P("fsdp", None),
            P("fsdp", None),
            P("fsdp", None),
            P("fsdp", None),
            P("fsdp", None),
            P("fsdp", None),
            P("fsdp", None),
        ),
        check_vma=False,
    )
```

```python
import functools

import jax
import jax.numpy as jnp
from jax import lax
from jax.experimental import pallas as pl
from jax.experimental.pallas import tpu as pltpu
from jax.sharding import PartitionSpec as P

HEADS = 16
HEAD_DIM = 48
STEP = 10


EPS_NORM = 1e-06
BETA_ONE = 0.5
BETA_TWO = 0.5
ADAM_EPS = 1e-08
DECAY = 0.01
RATE_QKV = 0.02
RATE_OUT = 0.1
RATE_UP = 0.02
RATE_DOWN = 0.01
RATE_VECTORS = 0.2

BF = jnp.bfloat16
F32 = jnp.float32
MESH = pl.DeviceIdType.MESH

RU, CW, H = 96, 768, 48
BLOCKS = 12
GATHER_ITEMS = ((0, 1), (2,), (3, 4), (5, 6), (7,), (8, 9), (10,), (11,))
VMEM_LIMIT = 62 * 2**20


def standardize(values):
    mean = jnp.mean(values, axis=-1, keepdims=True)
    centred = values - mean
    inverse = lax.rsqrt(jnp.mean(centred * centred, axis=-1, keepdims=True) + EPS_NORM)
    return (centred * inverse, inverse)


def norm_back(grad, normed, inverse, gain):
    scaled = grad * gain[None, :]
    first = jnp.mean(scaled, axis=-1, keepdims=True)
    second = jnp.mean(scaled * normed, axis=-1, keepdims=True)
    return (
        inverse * (scaled - first - normed * second),
        jnp.sum(grad * normed, axis=0),
        jnp.sum(grad, axis=0),
    )


def gelu_exact(values):
    return jax.nn.gelu(values, approximate=False)


def adamw(weight, grad, first, second, rate):
    new_first = BETA_ONE * first + (1.0 - BETA_ONE) * grad
    new_second = BETA_TWO * second + (1.0 - BETA_TWO) * grad * grad
    fix_one = 1.0 - BETA_ONE**STEP
    fix_two = 1.0 - BETA_TWO**STEP
    ratio = new_first / fix_one / (jnp.sqrt(new_second / fix_two) + ADAM_EPS)
    return (new_first, new_second, weight - rate * (ratio + DECAY * weight))


class Place:
    def __init__(self):
        dp, fs = lax.axis_index("dp"), lax.axis_index("fsdp")
        self.x, self.c = dp // 2, dp % 2
        self.z, self.y = fs // 2, fs % 2
        x, y, z, c = self.x, self.y, self.z, self.c
        self.sib = self.dev(x, y, z, 1 - c)
        self.xn = self.dev(1 - x, y, z, c)
        self.yn = self.dev(x, 1 - y, z, c)
        self.end = (z == 0) | (z == 3)
        self.mid = (z == 1) | (z == 2)
        self.inner = self.dev(x, y, z + 1 - 2 * (z // 2), c)
        self.outer = self.dev(x, y, (z + 3 + 2 * (z // 2)) % 4, c)
        self.up = self.dev(x, y, (z + 1) % 4, c)
        self.down = self.dev(x, y, (z + 3) % 4, c)
        self.far = self.dev(x, y, (z + 2) % 4, c)

    def dev(self, x, y, z, c):
        return (x * 2 + c, z * 2 + y)

    def mine(self, blocks):
        return blocks[0] if len(blocks) == 1 else blocks[0] + self.x * (blocks[1] - blocks[0])

    def theirs(self, blocks):
        return blocks[1] + self.x * (blocks[0] - blocks[1])


def arrived(ref, sem):
    pltpu.make_async_copy(ref, ref, sem).wait()


def add_into(dst, left, right):
    for row in range(0, dst.shape[-2], 16):
        dst[row : row + 16] = (left[row : row + 16].astype(F32) + right[row : row + 16].astype(F32)).astype(BF)


ROWS, IMAGE = 512, 256
FACTOR = HEAD_DIM**-0.5
LOG2E = 1.4426950408889634


def dot(left, right, over_left=1, over_right=0):
    return lax.dot_general(left, right, (((over_left,), (over_right,)), ((), ())), preferred_element_type=F32)


def matrix(w, j):
    return w[j].reshape(CW, CW)


def down_rows(w, s, first=8):
    return jnp.concatenate([w[first + k, s // 2, s % 2] for k in range(4)], axis=0)


def part(i, rows):
    return pl.ds(pl.multiple_of(i * rows, rows), rows)


def flag_column(flags, fcol):
    spot = lax.broadcasted_iota(jnp.int32, (IMAGE, IMAGE), 0) == lax.broadcasted_iota(jnp.int32, (IMAGE, IMAGE), 1)
    for b in range(2):
        row = jnp.broadcast_to((flags[:, b * IMAGE : (b + 1) * IMAGE] == 1).astype(F32), (8, IMAGE)).astype(BF)
        fcol[b * IMAGE : (b + 1) * IMAGE, :] = dot(spot.astype(F32).astype(BF), row, 1, 1)[:, 0:1]


def vector_tile(vectors, tile):
    tile[...] = jnp.zeros_like(tile)
    tile[0:5, 0:RU] = vectors[...].astype(BF)


def spread(s):
    row = lax.broadcasted_iota(jnp.int32, (128, CW), 0)
    column = lax.broadcasted_iota(jnp.int32, (128, CW), 1)
    return ((row < RU) & (column == row + s * RU)).astype(F32).astype(BF)


def vector_rows(tiles, pv):
    total = dot(tiles[0], spread(0))
    for s in range(1, 8):
        total = total + dot(tiles[s], spread(s))
    pv[...] = total


def hidden_rows(tok, fcol, pv, r):
    return jnp.where(fcol[r, :] > 0.5, pv[4:5, :], tok[r, :].astype(F32))


def norm_one(tok, fcol, pv, e1, i, rows=128):
    for k in range(rows // 64):
        r = pl.ds(pl.multiple_of(i * rows + k * 64, 64), 64)
        n, _ = standardize(hidden_rows(tok, fcol, pv, r))
        e1[r, :] = (n * pv[0:1, :] + pv[1:2, :]).astype(BF)


def project_part(e1, w, proj, j, i):
    r = part(i, 256)
    proj[j, r, :] = dot(e1[r, :], matrix(w, j)).astype(BF)


def head_lanes():
    return [(h * HEAD_DIM, range(h * HEAD_DIM // 128, (h * HEAD_DIM + HEAD_DIM - 1) // 128 + 1)) for h in range(8)]


def lane_mask(first, t):
    lane = lax.broadcasted_iota(jnp.int32, (1, 128), 1) + t * 128
    return ((lane >= first) & (lane < first + HEAD_DIM)).astype(F32).astype(BF)


def attend(proj, att, b, group):
    rows = part(b, IMAGE)

    def lanes(t):
        return pl.ds(pl.multiple_of(group * 384 + t * 128, 128), 128)

    acc = [None] * 3
    for first, tiles in head_lanes():
        masks = {t: lane_mask(first, t) for t in tiles}
        s = sum(dot(proj[0, rows, lanes(t)] * masks[t], proj[1, rows, lanes(t)], 1, 1) for t in tiles)
        top = jnp.max(s, axis=-1, keepdims=True)
        e = jnp.exp2((s - top) * (FACTOR * LOG2E))
        p = (e * (1.0 / jnp.sum(e, axis=-1, keepdims=True))).astype(BF)
        for t in tiles:
            o = dot(p, proj[2, rows, lanes(t)] * masks[t])
            acc[t] = o if acc[t] is None else acc[t] + o
    for t in range(3):
        att[rows, lanes(t)] = acc[t].astype(BF)


def norm_two(tok, fcol, pv, att, w, mid, e2, i):
    r = part(i, 256)
    v = hidden_rows(tok, fcol, pv, r) + dot(att[r, :], matrix(w, 3))
    mid[r, :] = v
    n, _ = standardize(v)
    e2[r, :] = (n * pv[2:3, :] + pv[3:4, :]).astype(BF)


def rise(e2, w, act, dg, k, i):
    r = part(i, 128)
    v = dot(e2[r, :], matrix(w, 4 + k))
    cdf = 0.5 * (1.0 + lax.erf(v * 0.7071067811865476))
    act[k, r, :] = (v * cdf).astype(BF)
    dg[k, r, :] = (cdf + v * (jnp.exp2(v * v * (-0.5 * LOG2E)) * 0.3989422804014327)).astype(BF)


def lower(act, w, mid, out, i):
    r = part(i, 256)
    total = mid[r, :]
    for s in range(8):
        total = total + dot(act[s // 2, r, (s % 2) * 384 : (s % 2) * 384 + 384], down_rows(w, s))
    out[r, :] = total.astype(BF)


class Gatherer:
    def __init__(self, at, w, zs, ys, xs, cs, snd):
        self.at, self.w, self.zs, self.ys, self.xs, self.cs, self.snd = at, w, zs, ys, xs, cs, snd
        self.half = pl.ds(pl.multiple_of(at.c * H, H), H)
        self.other = pl.ds(pl.multiple_of((1 - at.c) * H, H), H)
        self.others = [((at.z + dz) % 4, (at.y + dy) % 2) for dz in range(4) for dy in range(2) if dz + dy > 0]
        self.sends = []

    def send(self, src, dst, sem, to, cond=None):
        copy = pltpu.make_async_remote_copy(
            src_ref=src, dst_ref=dst, send_sem=self.snd, recv_sem=sem, device_id=to, device_id_type=MESH
        )
        if cond is None:
            copy.start()
        else:
            pl.when(cond)(copy.start)
        self.sends.append((cond, copy))

    def piece(self, j, z, y):
        return self.w.at[j, z, y, self.half, :]

    def start(self, i):
        at = self.at
        p = self.piece(at.mine(GATHER_ITEMS[i]), at.z, at.y)
        self.send(p, p, self.zs.at[i, 0, 0], at.up, at.z < 3)
        self.send(p, p, self.zs.at[i, 0, 1], at.down, at.z > 0)
        self.send(p, p, self.ys.at[i, at.z], at.yn)

    def hop(self, i, d):
        at, z, blocks = self.at, self.at.z, GATHER_ITEMS[i]
        j = at.mine(blocks)
        for way in (0, 1):
            has = (z - d - 1 >= 0) if way == 0 else (z + d + 1 <= 3)
            zz = jnp.maximum(z - d - 1, 0) if way == 0 else jnp.minimum(z + d + 1, 3)
            p = self.piece(j, zz, at.y)
            pl.when(has)(functools.partial(arrived, p, self.zs.at[i, d, way]))
            if d < 2 and way == 0:
                self.send(p, p, self.zs.at[i, d + 1, 0], at.up, has & (z < 3))
            if d < 2 and way == 1:
                self.send(p, p, self.zs.at[i, d + 1, 1], at.down, has & (z > 0))
            self.send(p, p, self.ys.at[i, zz], at.yn, has)
            if len(blocks) == 2:
                self.send(p, p, self.xs.at[i, zz, at.y], at.xn, has)
            self.send(p, p, self.cs.at[j, zz, at.y], at.sib, has)

    def across(self, i):
        at, blocks = self.at, GATHER_ITEMS[i]
        j, yy = at.mine(blocks), 1 - at.y
        for dz in range(4):
            zz = (at.z + dz) % 4
            p = self.piece(j, zz, yy)
            arrived(p, self.ys.at[i, zz])
            if len(blocks) == 2:
                self.send(p, p, self.xs.at[i, zz, yy], at.xn)
            self.send(p, p, self.cs.at[j, zz, yy], at.sib)

    def handed(self, i):
        if len(GATHER_ITEMS[i]) == 2:
            j = self.at.theirs(GATHER_ITEMS[i])
            for zz, yy in self.others:
                p = self.piece(j, zz, yy)
                arrived(p, self.xs.at[i, zz, yy])
                self.send(p, p, self.cs.at[j, zz, yy], self.at.sib)

    def shared(self, i):
        for j in GATHER_ITEMS[i]:
            for zz, yy in self.others:
                arrived(self.w.at[j, zz, yy, self.other, :], self.cs.at[j, zz, yy])

    def finish(self):
        for cond, copy in self.sends:
            if cond is None:
                copy.wait_send()
            else:
                pl.when(cond)(copy.wait_send)


def forward_kernel(
    w_qkv, w_out, w_up, w_down, vectors, tok, flags,
    lo_h, w_h, pv_h, e1_h, proj_h, att_h, mid_h, e2_h, act_h, dg_h,
    w, tile, tiles, pv, fcol, e1, proj, att, mid, e2, act, dg, lo, zs, ys, xs, cs, vs, save_sem, snd,
):
    at = Place()
    fs = at.z * 2 + at.y
    comm = Gatherer(at, w, zs, ys, xs, cs, snd)
    barrier = pltpu.get_barrier_semaphore()
    peers = [at.sib, at.xn] + [at.dev(at.x, yy, zz, at.c) for zz, yy in comm.others]
    for peer in peers:
        pl.semaphore_signal(barrier, inc=1, device_id=peer, device_id_type=MESH)
    vector_tile(vectors, tile)
    tiles[fs] = tile[...]
    for k in range(3):
        w[k, at.z, at.y] = w_qkv[:, k * CW : (k + 1) * CW].astype(BF)
    w[3, at.z, at.y] = w_out[...].astype(BF)
    for k in range(4):
        w[4 + k, at.z, at.y] = w_up[:, k * CW : (k + 1) * CW].astype(BF)
    for k in range(4):
        w[8 + k, at.z, at.y] = w_down[k * RU : (k + 1) * RU, :].astype(BF)
    pl.semaphore_wait(barrier, len(peers))
    for zz, yy in comm.others:
        comm.send(tile, tiles.at[fs], vs.at[fs], at.dev(at.x, yy, zz, at.c))
    saves = []

    def save(src, dst):
        copy = pltpu.make_async_copy(src, dst, save_sem.at[len(saves)])
        copy.start()
        saves.append(copy)

    def vectors_in():
        for zz, yy in comm.others:
            arrived(tiles.at[zz * 2 + yy], vs.at[zz * 2 + yy])
        vector_rows(tiles, pv)
        save(pv, pv_h)

    steps = [(-1, lambda: flag_column(flags, fcol)), (-1, vectors_in)]
    steps += [(-1, lambda i=i: norm_one(tok, fcol, pv, e1, i)) for i in range(4)]
    steps += [(0, lambda j=j, i=i: project_part(e1, w, proj, j, i)) for j in range(2) for i in range(2)]
    steps += [(1, lambda i=i: project_part(e1, w, proj, 2, i)) for i in range(2)]
    steps += [(1, lambda: save(e1, e1_h)), (1, lambda: save(proj, proj_h))]
    steps += [(1, lambda b=b, k=k: attend(proj, att, b, k)) for b in range(2) for k in range(2)]
    steps += [(2, lambda i=i: norm_two(tok, fcol, pv, att, w, mid, e2, i)) for i in range(2)]
    steps += [(2, lambda: save(att, att_h)), (2, lambda: save(mid, mid_h)), (2, lambda: save(e2, e2_h))]
    for k, need in enumerate((2, 3, 3, 4)):
        steps += [(need, lambda k=k, i=i: rise(e2, w, act, dg, k, i)) for i in range(4)]
        steps += [(need, lambda k=k: save(act.at[k], act_h.at[k])), (need, lambda k=k: save(dg.at[k], dg_h.at[k]))]
    steps += [(7, lambda i=i: lower(act, w, mid, lo, i)) for i in range(2)]
    steps += [(7, lambda: save(lo, lo_h))]
    there = -1

    def fill(count):
        while steps and count and steps[0][0] <= there:
            steps.pop(0)[1]()
            count -= 1

    n, lead = len(GATHER_ITEMS), 3
    for i in range(lead):
        comm.start(i)
    for t in range(n + 5):
        each = 1 if t < 8 else 2
        if t + lead < n:
            comm.start(t + lead)
        for d in range(3):
            if 0 <= t - d < n:
                comm.hop(t - d, d)
                fill(each if t else 0)
        for stage, lag in ((comm.across, 3), (comm.handed, 4), (comm.shared, 5)):
            if 0 <= t - lag < n:
                stage(t - lag)
                if lag == 5:
                    there = t - lag
                    for j in GATHER_ITEMS[there]:
                        save(w.at[j], w_h.at[j])
                fill(each)
    fill(len(steps))
    comm.finish()
    for copy in saves:
        copy.wait()


def forward(w_qkv, w_out, w_up, w_down, vectors, tokens, flags):
    n = len(GATHER_ITEMS)
    vmem, anywhere = pl.BlockSpec(memory_space=pltpu.VMEM), pl.BlockSpec(memory_space=pl.ANY)
    dma = pltpu.SemaphoreType.DMA
    whole, three, four = (ROWS, CW), (3, ROWS, CW), (4, ROWS, CW)
    shapes = [
        (whole, BF), ((BLOCKS, 4, 2, RU, CW), BF), ((16, CW), F32), (whole, BF), (three, BF), (whole, BF), (whole, F32),
        (whole, BF), (four, BF), (four, BF),
    ]
    return pl.pallas_call(
        forward_kernel,
        out_shape=[jax.ShapeDtypeStruct(s, t) for s, t in shapes],
        in_specs=[vmem] * 7,
        out_specs=[anywhere] * len(shapes),
        scratch_shapes=[
            pltpu.VMEM((BLOCKS, 4, 2, RU, CW), BF),
            pltpu.VMEM((16, 128), BF),
            pltpu.VMEM((8, 16, 128), BF),
            pltpu.VMEM((16, CW), F32),
            pltpu.VMEM((ROWS, 1), F32),
            pltpu.VMEM(whole, BF),
            pltpu.VMEM(three, BF),
            pltpu.VMEM(whole, BF),
            pltpu.VMEM(whole, F32),
            pltpu.VMEM(whole, BF),
            pltpu.VMEM(four, BF),
            pltpu.VMEM(four, BF),
            pltpu.VMEM(whole, BF),
            dma((n, 3, 2)),
            dma((n, 4)),
            dma((n, 4, 2)),
            dma((BLOCKS, 4, 2)),
            dma((8,)),
            dma((32,)),
            dma,
        ],
        compiler_params=pltpu.CompilerParams(collective_id=0, has_side_effects=True, vmem_limit_bytes=VMEM_LIMIT),
        name="forward",
    )(w_qkv, w_out, w_up, w_down, vectors, tokens, flags)


def grad_out_rows(cot, fcol, counts, r, b):
    weight = float(IMAGE) / jnp.full((1, 1), counts[b], jnp.int32).astype(F32)
    return cot[r, :].astype(F32) * (fcol[r, :] * weight)


def grad_low_part(cot, fcol, counts, gl, b):
    for k in range(4):
        r = pl.ds(b * IMAGE + k * 64, 64)
        gl[r, :] = grad_out_rows(cot, fcol, counts, r, b).astype(BF)


def grad_down_part(act, gl, g, s):
    d = dot(act[s // 2, :, (s % 2) * 384 : (s % 2) * 384 + 384], gl[...], 0, 0).astype(BF)
    for k in range(4):
        g[8 + k, s // 2, s % 2] = d[k * RU : (k + 1) * RU]


def grad_rising_part(gl, w, dg, s):
    lanes = slice((s % 2) * 384, (s % 2) * 384 + 384)
    grad = dot(gl[...], down_rows(w, s, 0), 1, 1)
    dg[s // 2, :, lanes] = (grad * dg[s // 2, :, lanes].astype(F32)).astype(BF)


def weight_grad_part(left, right, g, j, i):
    d = dot(left[:, i * 384 : i * 384 + 384], right[...], 0, 0).astype(BF)
    g[j, 2 * i : 2 * i + 2] = d.reshape(2, 2, RU, CW)


def norm_back_rows(grad, n, inverse, gain):
    scaled = grad * gain
    first = jnp.mean(scaled, axis=-1, keepdims=True)
    second = jnp.mean(scaled * n, axis=-1, keepdims=True)
    return inverse * (scaled - first - n * second)


def row_sum(values):
    return jnp.sum(values, axis=0, keepdims=True)


def back_two_part(gr, w, mid, pv, cot, fcol, counts, gm, ml, vec, i):
    r = part(i, 128)
    grad = sum(dot(gr[k, r, :], matrix(w, k), 1, 1) for k in range(4))
    n, inverse = standardize(mid[r, :])
    total = grad_out_rows(cot, fcol, counts, r, i // 2) + norm_back_rows(grad, n, inverse, pv[2:3, :])
    gm[r, :] = total
    ml[r, :] = total.astype(BF)
    vec[0, 2:3, :] += row_sum(grad * n)
    vec[0, 3:4, :] += row_sum(grad)


def grad_attended_part(ml, w, ga, i):
    r = part(i, 256)
    ga[r, :] = dot(ml[r, :], matrix(w, 4), 1, 1).astype(BF)


def attend_back(proj, ga, dproj, b, group):
    rows = part(b, IMAGE)

    def lanes(t):
        return pl.ds(pl.multiple_of(group * 384 + t * 128, 128), 128)

    acc = [[None] * 3 for _ in range(3)]

    def add(k, t, value):
        acc[k][t] = value if acc[k][t] is None else acc[k][t] + value

    for first, tiles in head_lanes():
        s = grad = 0.0
        masked = {}
        for t in tiles:
            m = lane_mask(first, t)
            q, k, v, o = proj[0, rows, lanes(t)], proj[1, rows, lanes(t)], proj[2, rows, lanes(t)], ga[rows, lanes(t)]
            masked[t] = (q * m, k * m, o * m)
            s = s + dot(q * m, k, 1, 1)
            grad = grad + dot(o * m, v, 1, 1)
        top = jnp.max(s, axis=-1, keepdims=True)
        e = jnp.exp2((s - top) * (FACTOR * LOG2E))
        p = e * (1.0 / jnp.sum(e, axis=-1, keepdims=True))
        delta = jnp.sum(grad * p, axis=-1, keepdims=True)
        raw = (p * ((grad - delta) * FACTOR)).astype(BF)
        low = p.astype(BF)
        for t in tiles:
            q, k, o = masked[t]
            add(0, t, dot(raw, k))
            add(1, t, dot(raw, q, 0, 0))
            add(2, t, dot(low, o, 0, 0))
    for k in range(3):
        for t in range(3):
            dproj[k, rows, lanes(t)] = acc[k][t].astype(BF)


def back_one_part(dproj, w, tok, fcol, pv, gm, tg, vec, i):
    r = part(i, 128)
    grad = sum(dot(dproj[k, r, :], matrix(w, k), 1, 1) for k in range(3))
    n, inverse = standardize(hidden_rows(tok, fcol, pv, r))
    total = norm_back_rows(grad, n, inverse, pv[0:1, :]) + gm[r, :]
    on = fcol[r, :] > 0.5
    tg[r, :] = jnp.where(on, 0.0, total).astype(BF)
    vec[0, 0:1, :] += row_sum(grad * n)
    vec[0, 1:2, :] += row_sum(grad)
    vec[0, 4:5, :] += row_sum(jnp.where(on, total, 0.0))


class Task:
    def __init__(self, name, time, needs, sends=(), rank=0):
        self.name, self.time, self.needs, self.sends, self.rank = name, time, tuple(needs), tuple(sends), rank


def plan(tasks, rates, window, arrive, sent, issue=0.1):
    now = 0.0
    links = {name: dict(active={}, queue=[], over=[], late=[], last=0.0) for name in rates}
    done, left, order, count = {}, list(tasks), [], 0

    def advance(to):
        for name, link in links.items():
            at = link["last"]
            while link["active"]:
                share = rates[name] / len(link["active"])
                token = min(link["active"], key=lambda q: link["active"][q])
                rest = link["active"][token]
                end = at + rest / share
                if end > to + 1e-9:
                    for q in link["active"]:
                        link["active"][q] -= (to - at) * share
                    at = to
                    break
                for q in link["active"]:
                    link["active"][q] -= rest
                del link["active"][token]
                at = end
                done[token] = end + arrive
                link["late"].append((end + sent, token))
            link["last"] = max(at, to)

    while left or any(link["queue"] or link["active"] for link in links.values()):
        advance(now)
        moved = False
        for name, link in links.items():
            link["over"] += [q[1] for q in link["late"] if q[0] <= now]
            link["late"] = [q for q in link["late"] if q[0] > now]
            while link["queue"] and len(link["active"]) + len(link["late"]) < window[name]:
                link["queue"].sort()
                _, _, token, size = link["queue"].pop(0)
                order.append(("issue", token, link["over"]))
                link["over"] = []
                now += issue
                advance(now)
                link["active"][token] = size
                moved = True
        ready = [q for q in left if all(done.get(need, 1e18) <= now for need in q.needs)]
        if ready:
            task = min(ready, key=lambda q: q.rank)
            left.remove(task)
            order.append(("run", task.name))
            now += task.time
            advance(now)
            done[task.name] = now
            for name, size, token, rank in task.sends:
                count += 1
                links[name]["queue"].append((rank, count, token, size))
            moved = True
        if not moved:
            times = [v for v in done.values() if v > now]
            for name, link in links.items():
                times += [q[0] for q in link["late"] if q[0] > now]
                if link["active"]:
                    times.append(link["last"] + min(link["active"].values()) * len(link["active"]) / rates[name])
            now = max(min(times), now) + 1e-6
    order.append(("waits", [t for link in links.values() for t in link["over"] + [q[1] for q in link["late"]]]))
    return order


RATES = dict(c=350e3, x=45e3, y=45e3, z=45e3, w=45e3, v=45e3)
WINDOW = dict(c=4, x=4, y=4, z=4, w=4, v=4)
REDUCE_ITEMS = (
    ((8, 9), 1), ((10, 11), 1), ((4, 5), 1), ((6,), 1), ((7,), 1), ((3,), 1), ((0,), 3), ((1,), 3), ((2,), 3)
)
SLOT = {blocks: k for k, (blocks, _) in enumerate(REDUCE_ITEMS)}
PAIR_SLOT = {blocks: k for k, blocks in enumerate(b for b, _ in REDUCE_ITEMS if len(b) == 2)}


def reduce_items():
    return [(blocks, k * (H // parts), H // parts) for blocks, parts in REDUCE_ITEMS for k in range(parts)]


def reduce_tasks(items, made):
    tasks = []
    for i, (blocks, _, rows) in enumerate(items):
        pair, size, add = len(blocks) == 2, rows * CW * 2, 0.04 * rows / H
        needs = [token for j in blocks for token in made[j]]
        to_sib = [("c", 8 * size, ("mine", i), i)]
        to_y = [("y", 2 * size, ("y0", i), i), ("y", 2 * size, ("y1", i), i)]
        if pair:
            to_x = [("x", 4 * size, ("x0", i), i), ("x", 4 * size, ("x1", i), i)]
            tasks.append(Task(("A", i), 0.05, needs, [("c", 8 * size, ("theirs", i), i)] + to_sib, i))
            tasks.append(Task(("Bt", i), 8 * add, [("theirs", i)], to_x, i))
            tasks.append(Task(("Bm", i), 8 * add, [("mine", i)], [], i))
            tasks.append(Task(("C", i), 8 * add, [("x0", i), ("x1", i), ("Bm", i)], to_y, i))
        else:
            tasks.append(Task(("A", i), 0.05, needs, to_sib, i))
            tasks.append(Task(("Bm", i), 8 * add, [("mine", i)], to_y, i))
        tasks.append(Task(("D", i), 4 * add, [("y0", i), ("y1", i)], [("z", 3 * size, ("za", i), i)], i))
        tasks.append(Task(("E1", i), 3 * add, [("za", i)], [("w", 2 * size, ("zb", i), i - 50)], i))
        tasks.append(Task(("E2", i), 2 * add, [("zb", i)], [("v", size, ("zc", i), i - 50)], i))
        tasks.append(Task(("E3", i), add, [("zc", i)], [("x", size, ("xf", i), i - 100)], i))
        finals = [("f%d" % k, i) for k in range(len(blocks))]
        tasks.append(Task(("G", i), 2 * add, [("xf", i)], [("c", size, f, i) for f in finals], i))
        tasks.append(Task(("H", i), 0.05, finals, [], i))
    return tasks


def vector_tasks(made):
    size = 8 * CW * 4
    return [
        Task(("V0", 0), 0.05, made, [("c", size, ("vc", 0), -200)], -200),
        Task(("V1", 0), 0.05, [("vc", 0)], [("x", size, ("vx", 0), -200)], -200),
        Task(("V2", 0), 0.05, [("vx", 0)], [("y", size, ("vy", 0), -200)], -200),
        Task(("V3", 0), 0.05, [("vy", 0)], [("z", size, ("vz%d" % d, 0), -200) for d in (1, 2, 3)], -200),
        Task(("V4", 0), 0.05, [("vz%d" % d, 0) for d in (1, 2, 3)], [], -200),
    ]


class Sender:
    def __init__(self, sems, window):
        self.sems, self.queued, self.under_way = sems, {}, {}
        self.free, first = {}, 0
        for name, slots in window.items():
            self.free[name] = list(range(first, first + slots))
            first += slots

    def put(self, token, link, src, dst, sem, to, cond=None):
        self.queued[token] = (link, src, dst, sem, to, cond)

    def issue(self, token, over):
        self.wait(over)
        link, src, dst, sem, to, cond = self.queued.pop(token)
        slot = self.free[link].pop(0)
        copy = pltpu.make_async_remote_copy(
            src_ref=src, dst_ref=dst, send_sem=self.sems.at[slot], recv_sem=sem, device_id=to, device_id_type=MESH
        )
        if cond is None:
            copy.start()
        else:
            pl.when(cond)(copy.start)
        self.under_way[token] = (link, slot, copy, cond)

    def wait(self, tokens):
        for token in tokens:
            link, slot, copy, cond = self.under_way.pop(token)
            self.free[link].append(slot)
            if cond is None:
                copy.wait_send()
            else:
                pl.when(cond)(copy.wait_send)


class Reducer:
    def __init__(self, at, items, sender, g, fin, sr, xr, yr, zr, xf, vec, vr, sems):
        self.at, self.items, self.sender = at, items, sender
        self.g, self.fin, self.sr, self.xr, self.yr, self.zr, self.xf = g, fin, sr, xr, yr, zr, xf
        self.vec, self.vr = vec, vr
        self.ssem, self.xsem, self.ysem, self.zsem, self.xfsem, self.fsem, self.vsem = sems

    def run(self, op, i):
        if op[0] == "V":
            return self.vectors(op)
        at, g, y, z = self.at, self.g, self.at.y, self.at.z
        blocks, first, count = self.items[i]
        pair, key, m = len(blocks) == 2, SLOT[blocks], self.at.mine(blocks)
        xkey = PAIR_SLOT.get(blocks)
        loc = pl.ds(first, count)
        own_rows = pl.ds(pl.multiple_of(at.c * H + first, 16), count)
        sib_rows = pl.ds(pl.multiple_of((1 - at.c) * H + first, 16), count)

        def add_shards(j, src):
            def body(k, _):
                d = g.at[j, k // 2, k % 2, own_rows, :]
                add_into(d, d, src.at[k // 2, k % 2, loc, :])
                return 0

            lax.fori_loop(0, 8, body, 0)

        def to_y():
            for q in range(2):
                two = pl.ds(2 * q, 2)
                self.sender.put(
                    ("y%d" % q, i), "y", g.at[m, two, 1 - y, own_rows, :], self.yr.at[key, two, loc, :],
                    self.ysem.at[i, q], at.yn,
                )

        if op == "A":
            if pair:
                t = at.theirs(blocks)
                self.sender.put(
                    ("theirs", i), "c", g.at[t, :, :, sib_rows, :], self.sr.at[t, :, :, loc, :], self.ssem.at[i, 1], at.sib
                )
            self.sender.put(
                ("mine", i), "c", g.at[m, :, :, sib_rows, :], self.sr.at[m, :, :, loc, :], self.ssem.at[i, 0], at.sib
            )
        elif op == "Bm":
            arrived(self.sr.at[m, :, :, loc, :], self.ssem.at[i, 0])
            add_shards(m, self.sr.at[m])
            if not pair:
                to_y()
        elif op == "Bt":
            t = at.theirs(blocks)
            arrived(self.sr.at[t, :, :, loc, :], self.ssem.at[i, 1])
            add_shards(t, self.sr.at[t])
            for q in range(2):
                two = pl.ds(2 * q, 2)
                self.sender.put(
                    ("x%d" % q, i), "x", g.at[t, two, :, own_rows, :], self.xr.at[xkey, two, :, loc, :],
                    self.xsem.at[i, q], at.xn,
                )
        elif op == "C":
            for q in range(2):
                arrived(self.xr.at[xkey, pl.ds(2 * q, 2), :, loc, :], self.xsem.at[i, q])
            add_shards(m, self.xr.at[xkey])
            to_y()
        elif op == "D":
            for q in range(2):
                arrived(self.yr.at[key, pl.ds(2 * q, 2), loc, :], self.ysem.at[i, q])

            def body(k, _):
                d = g.at[m, k, y, own_rows, :]
                add_into(d, d, self.yr.at[key, k, loc, :])
                return 0

            lax.fori_loop(0, 4, body, 0)
            self.sender.put(
                ("za", i), "z", g.at[m, pl.ds(1 - z // 3, 3), y, own_rows, :], self.zr.at[key, pl.ds(0, 3), loc, :],
                self.zsem.at[i, 0], at.inner, at.end,
            )
        elif op == "E1":

            @pl.when(at.mid)
            def _():
                arrived(self.zr.at[key, pl.ds(0, 3), loc, :], self.zsem.at[i, 0])
                for k in range(3):
                    d = g.at[m, 2 - z + k, y, own_rows, :]
                    add_into(d, d, self.zr.at[key, k, loc, :])

            self.sender.put(
                ("zb", i), "w", g.at[m, pl.ds(2 * (2 - z), 2), y, own_rows, :], self.zr.at[key, pl.ds(3, 2), loc, :],
                self.zsem.at[i, 1], at.inner, at.mid,
            )
        elif op == "E2":

            @pl.when(at.mid)
            def _():
                arrived(self.zr.at[key, pl.ds(3, 2), loc, :], self.zsem.at[i, 1])
                for k in range(2):
                    d = g.at[m, 2 * (z - 1) + k, y, own_rows, :]
                    add_into(d, d, self.zr.at[key, 3 + k, loc, :])

            self.sender.put(
                ("zc", i), "v", g.at[m, 3 * (z - 1), y, own_rows, :], self.zr.at[key, 0, loc, :],
                self.zsem.at[i, 2], at.outer, at.mid,
            )
        elif op == "E3":
            d = g.at[m, z, y, own_rows, :]

            @pl.when(at.end)
            def _():
                arrived(self.zr.at[key, 0, loc, :], self.zsem.at[i, 2])
                add_into(d, d, self.zr.at[key, 0, loc, :])

            self.sender.put(("xf", i), "x", d, self.xf.at[key, loc, :], self.xfsem.at[i], at.xn)
        elif op == "G":
            arrived(self.xf.at[key, loc, :], self.xfsem.at[i])
            d = g.at[m, z, y, own_rows, :]
            if pair:
                self.fin[m, own_rows, :] = d[...]
                self.fin[at.theirs(blocks), own_rows, :] = self.xf[key, loc, :]
            else:
                add_into(self.fin.at[m, own_rows, :], d, self.xf.at[key, loc, :])
            for k, j in enumerate((m, at.theirs(blocks)) if pair else blocks):
                f = self.fin.at[j, own_rows, :]
                self.sender.put(("f%d" % k, i), "c", f, f, self.fsem.at[i, k], at.sib)
        elif op == "H":
            for k, j in enumerate((m, at.theirs(blocks)) if pair else blocks):
                arrived(self.fin.at[j, sib_rows, :], self.fsem.at[i, k])

    def vectors(self, op):
        at, vec, vr, vsem = self.at, self.vec, self.vr, self.vsem
        if op == "V0":
            self.sender.put(("vc", 0), "c", vec.at[0], vr.at[0], vsem.at[0], at.sib)
        elif op == "V1":
            arrived(vr.at[0], vsem.at[0])
            vec[1] = vec[0] + vr[0]
            self.sender.put(("vx", 0), "x", vec.at[1], vr.at[1], vsem.at[1], at.xn)
        elif op == "V2":
            arrived(vr.at[1], vsem.at[1])
            vec[2] = vec[1] + vr[1]
            self.sender.put(("vy", 0), "y", vec.at[2], vr.at[2], vsem.at[2], at.yn)
        elif op == "V3":
            arrived(vr.at[2], vsem.at[2])
            vec[3] = vec[2] + vr[2]
            vr[3 + at.z] = vec[3]
            for d, to in ((1, at.up), (2, at.far), (3, at.down)):
                self.sender.put(("vz%d" % d, 0), "z", vec.at[3], vr.at[3 + at.z], vsem.at[3 + at.z], to)
        else:
            for d in (1, 2, 3):
                arrived(vr.at[3 + (at.z + d) % 4], vsem.at[3 + (at.z + d) % 4])
            vec[4] = ((vr[3] + vr[4]) + vr[5]) + vr[6]


def reduce_barrier(at):
    barrier = pltpu.get_barrier_semaphore()
    peers = [at.sib, at.xn, at.yn, at.up, at.far, at.down]
    for peer in peers:
        pl.semaphore_signal(barrier, inc=1, device_id=peer, device_id_type=MESH)
    pl.semaphore_wait(barrier, len(peers))


def reduce_scratch(n):
    dma = pltpu.SemaphoreType.DMA
    return [
        pltpu.VMEM((BLOCKS, 4, 2, H, CW), BF),
        pltpu.VMEM((len(PAIR_SLOT), 4, 2, H, CW), BF),
        pltpu.VMEM((len(SLOT), 4, H, CW), BF),
        pltpu.VMEM((len(SLOT), 5, H, CW), BF),
        pltpu.VMEM((len(SLOT), H, CW), BF),
        pltpu.VMEM((5, 8, CW), F32),
        pltpu.VMEM((7, 8, CW), F32),
        dma((n, 2)),
        dma((n, 2)),
        dma((n, 2)),
        dma((n, 3)),
        dma((n,)),
        dma((n, 2)),
        dma((7,)),
        dma((sum(WINDOW.values()),)),
    ]


LOADS = ("act", "cot", "dg", "d0", "d1", "d2", "d3", "e2", "mid", "out", "att", "proj", "e1", "tok")


def backward_tasks():
    rows = [(("gl", b), 0.7, []) for b in range(2)]
    low = [("gl", b) for b in range(2)]
    rows += [(("gd", s), 0.6, low) for s in range(8)]
    rows += [(("gr", s), 0.75, low) for s in range(8)]
    rows += [(("gu", k, i), 0.65, [("gr", 2 * k), ("gr", 2 * k + 1)]) for k in range(4) for i in range(2)]
    rows += [(("b2", i), 2.2, [("gr", s) for s in range(8)]) for i in range(4)]
    two = [("b2", i) for i in range(4)]
    rows += [(("go", i), 0.9, two) for i in range(2)]
    rows += [(("ga", i), 0.9, two) for i in range(2)]
    rows += [(("ab", b, k), 4.8, [("ga", b)]) for b in range(2) for k in range(2)]
    heads = [("ab", b, k) for b in range(2) for k in range(2)]
    rows += [(("gq", j, i), 0.75, heads) for j in range(3) for i in range(2)]
    rows += [(("b1", i), 1.7, heads) for i in range(4)]
    made = [[("gq", j, i) for i in range(2)] for j in range(3)]
    made += [[("go", i) for i in range(2)]]
    made += [[("gu", k, i) for i in range(2)] for k in range(4)]
    made += [[("gd", s) for s in range(8)]] * 4
    tasks = [Task(name, time, needs, (), 1000 + k) for k, (name, time, needs) in enumerate(rows)]
    return tasks, made, [("b1", i) for i in range(4)]


def backward_kernel(
    items, order,
    flags, counts, pv, act_h, cot_h, dg_h, w_h, e2_h, mid_h, att_h, proj_h, e1_h, tok_h,
    tg_h, fin, vec_out,
    act, cot, dg, w, e2, mid, att, proj, e1, tok, fcol, gl, gm, ml, g, load_sem, tg_sem, *reduce_refs,
):
    at = Place()
    source = dict(act=act_h, cot=cot_h, dg=dg_h, e2=e2_h, mid=mid_h, att=att_h, proj=proj_h, e1=e1_h, tok=tok_h)
    target = dict(act=act, cot=cot, dg=dg, e2=e2, mid=mid, att=att, proj=proj, e1=e1, tok=tok)
    loads = {}

    def load(name, src, dst):
        loads[name] = pltpu.make_async_copy(src, dst, load_sem.at[len(loads)])
        loads[name].start()

    def need(*names):
        for name in names:
            if loads[name] is not None:
                loads[name].wait()
                loads[name] = None

    for name in LOADS:
        if name in source:
            load(name, source[name], target[name])
        elif name == "out":
            load(name, w_h.at[3], w.at[4])
        else:
            load(name, w_h.at[8 + int(name[1])], w.at[int(name[1])])
    vec = reduce_refs[5]
    vec[0] = jnp.zeros((8, CW), F32)
    flag_column(flags, fcol)
    reduce_barrier(at)
    sender = Sender(reduce_refs[-1], WINDOW)
    steps = Reducer(at, items, sender, g, fin, *reduce_refs[:7], reduce_refs[7:14])
    dproj, ga, tg = act, gl, ml

    def compute(op, *k):
        if op == "gl":
            need("cot")
            grad_low_part(cot, fcol, counts, gl, *k)
        elif op == "gd":
            need("act")
            grad_down_part(act, gl, g, *k)
        elif op == "gr":
            need("dg", "d0", "d1", "d2", "d3")
            grad_rising_part(gl, w, dg, *k)
            if k[0] == 7:
                for j in range(4):
                    load("u%d" % j, w_h.at[4 + j], w.at[j])
        elif op == "gu":
            need("e2")
            weight_grad_part(e2, dg.at[k[0]], g, 4 + k[0], k[1])
        elif op == "b2":
            need("mid", "u0", "u1", "u2", "u3")
            back_two_part(dg, w, mid, pv, cot, fcol, counts, gm, ml, vec, *k)
            if k[0] == 3:
                for j in range(3):
                    load("q%d" % j, w_h.at[j], w.at[j])
        elif op == "go":
            need("att")
            weight_grad_part(att, ml, g, 3, *k)
        elif op == "ga":
            need("out")
            grad_attended_part(ml, w, ga, *k)
        elif op == "ab":
            need("proj")
            attend_back(proj, ga, dproj, *k)
        elif op == "gq":
            need("e1")
            weight_grad_part(e1, dproj.at[k[0]], g, *k)
        elif op == "b1":
            need("tok", "q0", "q1", "q2")
            back_one_part(dproj, w, tok, fcol, pv, gm, tg, vec, *k)
            if k[0] == 3:
                pltpu.make_async_copy(tg, tg_h, tg_sem).start()

    for entry in order:
        if entry[0] == "issue":
            sender.issue(entry[1], entry[2])
        elif entry[0] == "waits":
            sender.wait(entry[1])
        elif entry[1][0][0].isupper():
            steps.run(*entry[1])
        else:
            compute(*entry[1])
    pltpu.make_async_copy(tg, tg_h, tg_sem).wait()
    vec_out[...] = vec[4]


def backward(flags, counts, pv, act, cot, dg, w, e2, mid, att, proj, e1, tok):
    items = reduce_items()
    steps, made, vector_made = backward_tasks()
    order = plan(steps + reduce_tasks(items, made) + vector_tasks(vector_made), RATES, WINDOW, 6.0, 3.0)
    vmem, anywhere = pl.BlockSpec(memory_space=pltpu.VMEM), pl.BlockSpec(memory_space=pl.ANY)
    whole, three, four = (ROWS, CW), (3, ROWS, CW), (4, ROWS, CW)
    dma = pltpu.SemaphoreType.DMA
    return pl.pallas_call(
        functools.partial(backward_kernel, items, order),
        out_shape=[
            jax.ShapeDtypeStruct(whole, BF),
            jax.ShapeDtypeStruct((BLOCKS, RU, CW), BF),
            jax.ShapeDtypeStruct((8, CW), F32),
        ],
        in_specs=[vmem, pl.BlockSpec(memory_space=pltpu.SMEM), vmem] + [anywhere] * 10,
        out_specs=[anywhere, vmem, vmem],
        scratch_shapes=[
            pltpu.VMEM(four, BF),
            pltpu.VMEM(whole, BF),
            pltpu.VMEM(four, BF),
            pltpu.VMEM((5, 4, 2, RU, CW), BF),
            pltpu.VMEM(whole, BF),
            pltpu.VMEM(whole, F32),
            pltpu.VMEM(whole, BF),
            pltpu.VMEM(three, BF),
            pltpu.VMEM(whole, BF),
            pltpu.VMEM(whole, BF),
            pltpu.VMEM((ROWS, 1), F32),
            pltpu.VMEM(whole, BF),
            pltpu.VMEM(whole, F32),
            pltpu.VMEM(whole, BF),
            pltpu.VMEM((BLOCKS, 4, 2, RU, CW), BF),
            dma((24,)),
            dma,
        ]
        + reduce_scratch(len(items)),
        compiler_params=pltpu.CompilerParams(collective_id=1, has_side_effects=True, vmem_limit_bytes=VMEM_LIMIT),
        name="backward",
    )(flags, counts, pv, act, cot, dg, w, e2, mid, att, proj, e1, tok)


def adam_kernel(fin, vec, fs, *refs):
    states, vecs, outs, vec_outs = refs[:12], refs[12:15], refs[15:27], refs[27:31]
    ins, news, in_sem, out_sem = refs[31:]

    def block(ref, j):
        if j < 3:
            return ref.at[:, pl.ds(j * CW, CW)]
        if j == 3:
            return ref
        if j < 8:
            return ref.at[:, pl.ds((j - 4) * CW, CW)]
        return ref.at[pl.ds((j - 8) * RU, RU), :]

    matrix_of = [0] * 3 + [1] + [2] * 4 + [3] * 4
    loads, saves = [], []
    for j in range(BLOCKS):
        three = [
            pltpu.make_async_copy(block(states[3 * matrix_of[j] + k], j), ins.at[j, k], in_sem.at[j, k]) for k in range(3)
        ]
        for copy in three:
            copy.start()
        loads.append(three)
    column = lax.broadcasted_iota(jnp.int32, (RU, CW), 1) == lax.broadcasted_iota(jnp.int32, (RU, CW), 0) + fs[0] * RU
    grad = lax.dot_general(
        vec[...], column.astype(F32), (((1,), (1,)), ((), ())), preferred_element_type=F32,
        precision=lax.Precision.HIGHEST,
    )
    first, second, new = adamw(vecs[0][...], grad[0:5], vecs[1][...], vecs[2][...], RATE_VECTORS)
    vec_outs[0][...] = first
    vec_outs[1][0:2, :] = second[0:2]
    vec_outs[1][2:3, :] = second[4:5]
    vec_outs[2][...] = second[2:4]
    vec_outs[3][...] = new
    for j in range(BLOCKS):
        rate = (RATE_QKV, RATE_OUT, RATE_UP, RATE_DOWN)[matrix_of[j]]
        for copy in loads[j]:
            copy.wait()

        def rows(i, _, j=j, rate=rate):
            r = part(i, 16)
            result = adamw(ins[j, 0, r, :], fin[j, r, :].astype(F32), ins[j, 1, r, :], ins[j, 2, r, :], rate)
            for k in range(3):
                news[j, k, r, :] = result[k]
            return 0

        lax.fori_loop(0, RU // 16, rows, 0)
        for k in range(3):
            copy = pltpu.make_async_copy(news.at[j, k], block(outs[3 * matrix_of[j] + k], j), out_sem.at[j, k])
            copy.start()
            saves.append(copy)
    for copy in saves:
        copy.wait()


def adam(fin, vec, fs, states, vecs):
    vmem, anywhere = pl.BlockSpec(memory_space=pltpu.VMEM), pl.BlockSpec(memory_space=pl.ANY)
    dma = pltpu.SemaphoreType.DMA
    return pl.pallas_call(
        adam_kernel,
        out_shape=[jax.ShapeDtypeStruct(s.shape, F32) for s in states]
        + [jax.ShapeDtypeStruct((n, RU), F32) for n in (5, 3, 2, 5)],
        in_specs=[vmem, vmem, pl.BlockSpec(memory_space=pltpu.SMEM)] + [anywhere] * 12 + [vmem] * 3,
        out_specs=[anywhere] * 12 + [vmem] * 4,
        scratch_shapes=[
            pltpu.VMEM((BLOCKS, 3, RU, CW), F32),
            pltpu.VMEM((BLOCKS, 3, RU, CW), F32),
            dma((BLOCKS, 3)),
            dma((BLOCKS, 3)),
        ],
        compiler_params=pltpu.CompilerParams(vmem_limit_bytes=VMEM_LIMIT),
        name="adam",
    )(fin, vec, fs, *states, *vecs)


def on_device_plain(
    tokens,
    mask_flags,
    mask_counts,
    cotangent,
    w_qkv,
    w_out,
    w_up,
    w_down,
    vectors,
    first_qkv,
    first_out,
    first_up,
    first_down,
    first_vectors,
    second_qkv,
    second_out,
    second_up,
    second_down,
    second_vectors,
):
    rows, width = tokens.shape
    images = mask_counts.shape[0]
    length = rows // images
    factor = HEAD_DIM ** (-0.5)
    attn_shards = (
        w_qkv.astype(jnp.bfloat16),
        w_out.astype(jnp.bfloat16),
        vectors.astype(jnp.bfloat16),
    )
    mlp_shards = (w_up.astype(jnp.bfloat16), w_down.astype(jnp.bfloat16))
    full_qkv, full_out, full_vec = (
        lax.all_gather(attn_shards[0], "fsdp", axis=0, tiled=True),
        lax.all_gather(attn_shards[1], "fsdp", axis=0, tiled=True),
        lax.all_gather(attn_shards[2], "fsdp", axis=0, tiled=True),
    )
    full_up, full_down = (
        lax.all_gather(mlp_shards[0], "fsdp", axis=0, tiled=True),
        lax.all_gather(mlp_shards[1], "fsdp", axis=0, tiled=True),
    )
    params = full_vec.astype(jnp.float32)
    masked = (mask_flags == 1)[:, None]
    hidden = jnp.where(masked, params[:, 4][None, :], tokens.astype(jnp.float32))
    normed_one, inverse_one = standardize(hidden)
    entry_one = (normed_one * params[:, 0] + params[:, 1]).astype(jnp.bfloat16)
    project = jnp.dot(entry_one, full_qkv, preferred_element_type=jnp.float32).astype(jnp.bfloat16)
    split = project.reshape(images, length, 3, HEADS, HEAD_DIM)
    queries = split[:, :, 0]
    keys = split[:, :, 1]
    values = split[:, :, 2]
    scores = (
        jnp.einsum("bqhd,bkhd->bhqk", queries, keys, preferred_element_type=jnp.float32) * factor
    )
    top = jnp.max(scores, axis=-1, keepdims=True)
    total = jnp.sum(jnp.exp(scores - top), axis=-1, keepdims=True)
    logsum = top + jnp.log(total)
    probs_low = jnp.exp(scores - logsum).astype(jnp.bfloat16)
    mixed = jnp.einsum("bhqk,bkhd->bqhd", probs_low, values, preferred_element_type=jnp.float32)
    attended = mixed.astype(jnp.bfloat16).reshape(rows, width)
    middle = hidden + jnp.dot(attended, full_out, preferred_element_type=jnp.float32)
    normed_two, inverse_two = standardize(middle)
    entry_two = (normed_two * params[:, 2] + params[:, 3]).astype(jnp.bfloat16)
    rising = jnp.dot(entry_two, full_up, preferred_element_type=jnp.float32)
    activated, gelu_pull = jax.vjp(gelu_exact, rising)
    active = activated.astype(jnp.bfloat16)
    layer_out = (middle + jnp.dot(active, full_down, preferred_element_type=jnp.float32)).astype(
        jnp.bfloat16
    )
    row_weight = jnp.repeat(
        length / mask_counts.astype(jnp.float32), length, total_repeat_length=rows
    )
    grad_out = (
        cotangent.astype(jnp.float32) * (row_weight * mask_flags.astype(jnp.float32))[:, None]
    )
    back_up, back_down = (
        lax.all_gather(mlp_shards[0], "fsdp", axis=0, tiled=True),
        lax.all_gather(mlp_shards[1], "fsdp", axis=0, tiled=True),
    )
    back_qkv, back_out, back_vec = (
        lax.all_gather(attn_shards[0], "fsdp", axis=0, tiled=True),
        lax.all_gather(attn_shards[1], "fsdp", axis=0, tiled=True),
        lax.all_gather(attn_shards[2], "fsdp", axis=0, tiled=True),
    )
    gains = back_vec.astype(jnp.float32)
    grad_low = grad_out.astype(jnp.bfloat16)
    grad_down = jnp.einsum("tf,td->fd", active, grad_low, preferred_element_type=jnp.float32)
    grad_active = jnp.einsum("td,fd->tf", grad_low, back_down, preferred_element_type=jnp.float32)
    grad_rising = gelu_pull(grad_active)[0].astype(jnp.bfloat16)
    grad_up = jnp.einsum("td,tf->df", entry_two, grad_rising, preferred_element_type=jnp.float32)
    grad_entry_two = jnp.einsum(
        "tf,df->td", grad_rising, back_up, preferred_element_type=jnp.float32
    )
    mlp_sums = (
        lax.psum_scatter(grad_up, "fsdp", scatter_dimension=0, tiled=True),
        lax.psum_scatter(grad_down, "fsdp", scatter_dimension=0, tiled=True),
    )
    back_two, gain_two, bias_two = norm_back(grad_entry_two, normed_two, inverse_two, gains[:, 2])
    grad_middle = grad_out + back_two
    middle_low = grad_middle.astype(jnp.bfloat16)
    grad_wout = jnp.einsum("tc,td->cd", attended, middle_low, preferred_element_type=jnp.float32)
    grad_attended = jnp.einsum(
        "td,cd->tc", middle_low, back_out, preferred_element_type=jnp.float32
    )
    grad_attended = grad_attended.astype(jnp.bfloat16).reshape(images, length, HEADS, HEAD_DIM)
    again_scores = (
        jnp.einsum("bqhd,bkhd->bhqk", queries, keys, preferred_element_type=jnp.float32) * factor
    )
    probs = jnp.exp(again_scores - logsum)
    again_low = probs.astype(jnp.bfloat16)
    grad_values = jnp.einsum(
        "bhqk,bqhd->bkhd", again_low, grad_attended, preferred_element_type=jnp.float32
    )
    grad_probs = jnp.einsum(
        "bqhd,bkhd->bhqk", grad_attended, values, preferred_element_type=jnp.float32
    )
    grad_scores = probs * (grad_probs - jnp.sum(grad_probs * probs, axis=-1, keepdims=True))
    grad_raw = (grad_scores * factor).astype(jnp.bfloat16)
    grad_queries = jnp.einsum("bhqk,bkhd->bqhd", grad_raw, keys, preferred_element_type=jnp.float32)
    grad_keys = jnp.einsum("bhqk,bqhd->bkhd", grad_raw, queries, preferred_element_type=jnp.float32)
    grad_project = (
        jnp.stack([grad_queries, grad_keys, grad_values], axis=2)
        .reshape(rows, 3 * width)
        .astype(jnp.bfloat16)
    )
    grad_qkv = jnp.einsum("td,te->de", entry_one, grad_project, preferred_element_type=jnp.float32)
    grad_entry_one = jnp.einsum(
        "te,de->td", grad_project, back_qkv, preferred_element_type=jnp.float32
    )
    back_one, gain_one, bias_one = norm_back(grad_entry_one, normed_one, inverse_one, gains[:, 0])
    grad_hidden = back_one + grad_middle
    token_grad = jnp.where(masked, 0.0, grad_hidden).astype(jnp.bfloat16)
    grad_mask = jnp.sum(jnp.where(masked, grad_hidden, 0.0), axis=0)
    grad_vec = jnp.stack([gain_one, bias_one, gain_two, bias_two, grad_mask], axis=1)
    attn_sums = (
        lax.psum_scatter(grad_qkv, "fsdp", scatter_dimension=0, tiled=True),
        lax.psum_scatter(grad_wout, "fsdp", scatter_dimension=0, tiled=True),
        lax.psum_scatter(grad_vec, "fsdp", scatter_dimension=0, tiled=True),
    )
    sum_qkv, sum_out, sum_vec, sum_up, sum_down = (
        lax.psum(attn_sums[0].astype(jnp.bfloat16), "dp").astype(jnp.float32),
        lax.psum(attn_sums[1].astype(jnp.bfloat16), "dp").astype(jnp.float32),
        lax.psum(attn_sums[2].astype(jnp.bfloat16), "dp").astype(jnp.float32),
        lax.psum(mlp_sums[0].astype(jnp.bfloat16), "dp").astype(jnp.float32),
        lax.psum(mlp_sums[1].astype(jnp.bfloat16), "dp").astype(jnp.float32),
    )
    qkv_first, qkv_second, qkv_new = adamw(w_qkv, sum_qkv, first_qkv, second_qkv, RATE_QKV)
    out_first, out_second, out_new = adamw(w_out, sum_out, first_out, second_out, RATE_OUT)
    up_first, up_second, up_new = adamw(w_up, sum_up, first_up, second_up, RATE_UP)
    down_first, down_second, down_new = adamw(w_down, sum_down, first_down, second_down, RATE_DOWN)
    vec_first, vec_second, vec_new = adamw(
        vectors, sum_vec, first_vectors, second_vectors, RATE_VECTORS
    )
    second_front = jnp.concatenate([vec_second[:, 0:2], vec_second[:, 4:5]], axis=1)
    second_later = vec_second[:, 2:4]
    return (
        layer_out,
        token_grad,
        qkv_first,
        out_first,
        up_first,
        down_first,
        vec_first,
        qkv_second,
        out_second,
        up_second,
        down_second,
        second_front,
        second_later,
        qkv_new,
        out_new,
        up_new,
        down_new,
        vec_new,
    )


def on_device_fast(
    tokens,
    mask_flags,
    mask_counts,
    cotangent,
    w_qkv,
    w_out,
    w_up,
    w_down,
    vectors,
    first_qkv,
    first_out,
    first_up,
    first_down,
    first_vectors,
    second_qkv,
    second_out,
    second_up,
    second_down,
    second_vectors,
):
    flags = mask_flags.reshape(1, ROWS)
    layer_out, w, pv, e1, proj, att, mid, e2, act, dg = forward(w_qkv, w_out, w_up, w_down, vectors.T, tokens, flags)
    token_grad, sums, sum_vec = backward(flags, mask_counts, pv, act, cotangent, dg, w, e2, mid, att, proj, e1, tokens)
    states = (
        w_qkv, first_qkv, second_qkv, w_out, first_out, second_out,
        w_up, first_up, second_up, w_down, first_down, second_down,
    )
    fs = lax.axis_index("fsdp").astype(jnp.int32).reshape(1)
    new = adam(sums, sum_vec, fs, states, (vectors.T, first_vectors.T, second_vectors.T))
    new_w, new_first, new_second = [[new[3 * m + k] for m in range(4)] for k in (2, 0, 1)]
    vec_first, second_front, second_later, vec_new = [v.T for v in new[12:]]
    return (
        layer_out, token_grad, *new_first, vec_first, *new_second, second_front, second_later, *new_w, vec_new
    )


def solution(mesh):
    placed = (
        P(("dp", "fsdp"), None),
        P(("dp", "fsdp")),
        P(("dp", "fsdp")),
        P(("dp", "fsdp"), None),
        P("fsdp", None),
        P("fsdp", None),
        P("fsdp", None),
        P("fsdp", None),
        P("fsdp", None),
        P("fsdp", None),
        P("fsdp", None),
        P("fsdp", None),
        P("fsdp", None),
        P("fsdp", None),
        P("fsdp", None),
        P("fsdp", None),
        P("fsdp", None),
        P("fsdp", None),
        P("fsdp", None),
    )
    shape = dict(mesh.shape)
    fast = shape["dp"] == 4 and shape["fsdp"] == 8
    return jax.shard_map(
        on_device_fast if fast else on_device_plain,
        mesh=mesh,
        in_specs=placed,
        out_specs=(
            P(("dp", "fsdp"), None),
            P(("dp", "fsdp"), None),
            P("fsdp", None),
            P("fsdp", None),
            P("fsdp", None),
            P("fsdp", None),
            P("fsdp", None),
            P("fsdp", None),
            P("fsdp", None),
            P("fsdp", None),
            P("fsdp", None),
            P("fsdp", None),
            P("fsdp", None),
            P("fsdp", None),
            P("fsdp", None),
            P("fsdp", None),
            P("fsdp", None),
            P("fsdp", None),
        ),
        check_vma=False,
    )
```

```python
import functools

import jax
import jax.numpy as jnp
from jax import lax
from jax.experimental import pallas as pl
from jax.experimental.pallas import tpu as pltpu
from jax.sharding import PartitionSpec as P

HEADS = 16
HEAD_DIM = 48
STEP = 10


EPS_NORM = 1e-06
BETA_ONE = 0.5
BETA_TWO = 0.5
ADAM_EPS = 1e-08
DECAY = 0.01
RATE_QKV = 0.02
RATE_OUT = 0.1
RATE_UP = 0.02
RATE_DOWN = 0.01
RATE_VECTORS = 0.2

BF = jnp.bfloat16
F32 = jnp.float32
MESH = pl.DeviceIdType.MESH

RU, CW, H = 96, 768, 48
BLOCKS = 12
LEAD = 2
EACH = (1,) * 8 + (2,) * 8
GATHER_ITEMS = ((0, 1), (2,), (3, 4), (5, 6), (7,), (8, 9), (10,), (11,))
VMEM_LIMIT = 62 * 2**20


def standardize(values):
    mean = jnp.mean(values, axis=-1, keepdims=True)
    centred = values - mean
    inverse = lax.rsqrt(jnp.mean(centred * centred, axis=-1, keepdims=True) + EPS_NORM)
    return (centred * inverse, inverse)


def norm_back(grad, normed, inverse, gain):
    scaled = grad * gain[None, :]
    first = jnp.mean(scaled, axis=-1, keepdims=True)
    second = jnp.mean(scaled * normed, axis=-1, keepdims=True)
    return (
        inverse * (scaled - first - normed * second),
        jnp.sum(grad * normed, axis=0),
        jnp.sum(grad, axis=0),
    )


def gelu_exact(values):
    return jax.nn.gelu(values, approximate=False)


def adamw(weight, grad, first, second, rate):
    new_first = BETA_ONE * first + (1.0 - BETA_ONE) * grad
    new_second = BETA_TWO * second + (1.0 - BETA_TWO) * grad * grad
    fix_one = 1.0 - BETA_ONE**STEP
    fix_two = 1.0 - BETA_TWO**STEP
    ratio = new_first / fix_one / (jnp.sqrt(new_second / fix_two) + ADAM_EPS)
    return (new_first, new_second, weight - rate * (ratio + DECAY * weight))


class Place:
    def __init__(self):
        dp, fs = lax.axis_index("dp"), lax.axis_index("fsdp")
        self.x, self.c = dp // 2, dp % 2
        self.z, self.y = fs // 2, fs % 2
        x, y, z, c = self.x, self.y, self.z, self.c
        self.sib = self.dev(x, y, z, 1 - c)
        self.xn = self.dev(1 - x, y, z, c)
        self.yn = self.dev(x, 1 - y, z, c)
        self.end = (z == 0) | (z == 3)
        self.mid = (z == 1) | (z == 2)
        self.inner = self.dev(x, y, z + 1 - 2 * (z // 2), c)
        self.outer = self.dev(x, y, (z + 3 + 2 * (z // 2)) % 4, c)
        self.up = self.dev(x, y, (z + 1) % 4, c)
        self.down = self.dev(x, y, (z + 3) % 4, c)
        self.far = self.dev(x, y, (z + 2) % 4, c)

    def dev(self, x, y, z, c):
        return (x * 2 + c, z * 2 + y)

    def mine(self, blocks):
        return blocks[0] if len(blocks) == 1 else blocks[0] + self.x * (blocks[1] - blocks[0])

    def theirs(self, blocks):
        return blocks[1] + self.x * (blocks[0] - blocks[1])


def arrived(ref, sem):
    pltpu.make_async_copy(ref, ref, sem).wait()


def add_into(dst, left, right):
    for row in range(0, dst.shape[-2], 16):
        dst[row : row + 16] = (left[row : row + 16].astype(F32) + right[row : row + 16].astype(F32)).astype(BF)


ROWS, IMAGE = 512, 256
FACTOR = HEAD_DIM**-0.5
LOG2E = 1.4426950408889634


def dot(left, right, over_left=1, over_right=0):
    return lax.dot_general(left, right, (((over_left,), (over_right,)), ((), ())), preferred_element_type=F32)


def matrix(w, j):
    return w[j].reshape(CW, CW)


def down_rows(w, s, first=8):
    return jnp.concatenate([w[first + k, s // 2, s % 2] for k in range(4)], axis=0)


def part(i, rows):
    return pl.ds(pl.multiple_of(i * rows, rows), rows)


def flag_column(flags, fcol):
    spot = lax.broadcasted_iota(jnp.int32, (IMAGE, IMAGE), 0) == lax.broadcasted_iota(jnp.int32, (IMAGE, IMAGE), 1)
    for b in range(2):
        row = jnp.broadcast_to((flags[:, b * IMAGE : (b + 1) * IMAGE] == 1).astype(F32), (8, IMAGE)).astype(BF)
        fcol[b * IMAGE : (b + 1) * IMAGE, :] = dot(spot.astype(F32).astype(BF), row, 1, 1)[:, 0:1]


def vector_tile(vectors, tile):
    tile[...] = jnp.zeros_like(tile)
    tile[0:5, 0:RU] = vectors[...].astype(BF)


def spread(s):
    row = lax.broadcasted_iota(jnp.int32, (128, CW), 0)
    column = lax.broadcasted_iota(jnp.int32, (128, CW), 1)
    return ((row < RU) & (column == row + s * RU)).astype(F32).astype(BF)


def vector_rows(tiles, pv):
    total = dot(tiles[0], spread(0))
    for s in range(1, 8):
        total = total + dot(tiles[s], spread(s))
    pv[...] = total


def hidden_rows(tok, fcol, pv, r):
    return jnp.where(fcol[r, :] > 0.5, pv[4:5, :], tok[r, :].astype(F32))


def norm_one(tok, fcol, pv, e1, i, rows=128):
    for k in range(rows // 64):
        r = pl.ds(pl.multiple_of(i * rows + k * 64, 64), 64)
        n, _ = standardize(hidden_rows(tok, fcol, pv, r))
        e1[r, :] = (n * pv[0:1, :] + pv[1:2, :]).astype(BF)


def project_part(e1, w, proj, j, i):
    r = part(i, 256)
    proj[j, r, :] = dot(e1[r, :], matrix(w, j)).astype(BF)


def head_lanes():
    return [(h * HEAD_DIM, range(h * HEAD_DIM // 128, (h * HEAD_DIM + HEAD_DIM - 1) // 128 + 1)) for h in range(8)]


def lane_mask(first, t):
    lane = lax.broadcasted_iota(jnp.int32, (1, 128), 1) + t * 128
    return ((lane >= first) & (lane < first + HEAD_DIM)).astype(F32).astype(BF)


def attend(proj, att, probs, b, group):
    rows = part(b, IMAGE)

    def lanes(t):
        return slice(group * 384 + t * 128, group * 384 + t * 128 + 128)

    acc = [None] * 3
    for h, (first, tiles) in enumerate(head_lanes()):
        masks = {t: lane_mask(first, t) for t in tiles}
        s = sum(dot(proj[1, rows, lanes(t)], proj[0, rows, lanes(t)] * masks[t], 1, 1) for t in tiles)
        top = jnp.max(s, axis=0, keepdims=True)
        e = jnp.exp2((s - top) * (FACTOR * LOG2E))
        p = (e * (1.0 / jnp.sum(e, axis=0, keepdims=True))).astype(BF)
        probs[2 * b + group, h] = p
        for t in tiles:
            o = dot(p, proj[2, rows, lanes(t)] * masks[t], 0, 0)
            acc[t] = o if acc[t] is None else acc[t] + o
    for t in range(3):
        att[rows, lanes(t)] = acc[t].astype(BF)


def norm_two(tok, fcol, pv, att, w, mid, e2, i):
    r = part(i, 256)
    v = hidden_rows(tok, fcol, pv, r) + dot(att[r, :], matrix(w, 3))
    mid[r, :] = v
    n, _ = standardize(v)
    e2[r, :] = (n * pv[2:3, :] + pv[3:4, :]).astype(BF)


def rise(e2, w, act, dg, k, i, rows=128):
    r = part(i, rows)
    v = dot(e2[r, :], matrix(w, 4 + k))
    cdf = 0.5 * (1.0 + lax.erf(v * 0.7071067811865476))
    act[k, r, :] = (v * cdf).astype(BF)
    dg[k, r, :] = (cdf + v * (jnp.exp2(v * v * (-0.5 * LOG2E)) * 0.3989422804014327)).astype(BF)


def lower(act, w, mid, out, i):
    r = part(i, 256)
    total = mid[r, :]
    for s in range(8):
        total = total + dot(act[s // 2, r, (s % 2) * 384 : (s % 2) * 384 + 384], down_rows(w, s))
    out[r, :] = total.astype(BF)


class Gatherer:
    def __init__(self, at, w, zs, ys, xs, cs, snd):
        self.at, self.w, self.zs, self.ys, self.xs, self.cs, self.snd = at, w, zs, ys, xs, cs, snd
        self.half = pl.ds(pl.multiple_of(at.c * H, H), H)
        self.other = pl.ds(pl.multiple_of((1 - at.c) * H, H), H)
        self.others = [((at.z + dz) % 4, (at.y + dy) % 2) for dz in range(4) for dy in range(2) if dz + dy > 0]
        self.sends = []

    def send(self, src, dst, sem, to, cond=None):
        copy = pltpu.make_async_remote_copy(
            src_ref=src, dst_ref=dst, send_sem=self.snd, recv_sem=sem, device_id=to, device_id_type=MESH
        )
        if cond is None:
            copy.start()
        else:
            pl.when(cond)(copy.start)
        self.sends.append((cond, copy))

    def piece(self, j, z, y):
        return self.w.at[j, z, y, self.half, :]

    def start(self, i):
        at = self.at
        p = self.piece(at.mine(GATHER_ITEMS[i]), at.z, at.y)
        self.send(p, p, self.zs.at[i, 0, 0], at.up, at.z < 3)
        self.send(p, p, self.zs.at[i, 0, 1], at.down, at.z > 0)
        self.send(p, p, self.ys.at[i, at.z], at.yn)

    def hop(self, i, d):
        at, z, blocks = self.at, self.at.z, GATHER_ITEMS[i]
        j = at.mine(blocks)
        for way in (0, 1):
            has = (z - d - 1 >= 0) if way == 0 else (z + d + 1 <= 3)
            zz = jnp.maximum(z - d - 1, 0) if way == 0 else jnp.minimum(z + d + 1, 3)
            p = self.piece(j, zz, at.y)
            pl.when(has)(functools.partial(arrived, p, self.zs.at[i, d, way]))
            if d < 2 and way == 0:
                self.send(p, p, self.zs.at[i, d + 1, 0], at.up, has & (z < 3))
            if d < 2 and way == 1:
                self.send(p, p, self.zs.at[i, d + 1, 1], at.down, has & (z > 0))
            self.send(p, p, self.ys.at[i, zz], at.yn, has)
            if len(blocks) == 2:
                self.send(p, p, self.xs.at[i, zz, at.y], at.xn, has)
            self.send(p, p, self.cs.at[j, zz, at.y], at.sib, has)

    def across(self, i):
        at, blocks = self.at, GATHER_ITEMS[i]
        j, yy = at.mine(blocks), 1 - at.y
        for dz in range(4):
            zz = (at.z + dz) % 4
            p = self.piece(j, zz, yy)
            arrived(p, self.ys.at[i, zz])
            if len(blocks) == 2:
                self.send(p, p, self.xs.at[i, zz, yy], at.xn)
            self.send(p, p, self.cs.at[j, zz, yy], at.sib)

    def handed(self, i):
        if len(GATHER_ITEMS[i]) == 2:
            j = self.at.theirs(GATHER_ITEMS[i])
            for zz, yy in self.others:
                p = self.piece(j, zz, yy)
                arrived(p, self.xs.at[i, zz, yy])
                self.send(p, p, self.cs.at[j, zz, yy], self.at.sib)

    def shared(self, i):
        for j in GATHER_ITEMS[i]:
            for zz, yy in self.others:
                arrived(self.w.at[j, zz, yy, self.other, :], self.cs.at[j, zz, yy])

    def finish(self):
        for cond, copy in self.sends:
            if cond is None:
                copy.wait_send()
            else:
                pl.when(cond)(copy.wait_send)


def forward_kernel(
    w_qkv, w_out, w_up, w_down, vectors, tok, flags,
    lo_h, w_h, pv_h, e1_h, proj_h, probs_h, att_h, mid_h, e2_h, act_h, dg_h,
    w, tile, tiles, pv, fcol, e1, proj, probs, att, mid, e2, act, dg, lo, zs, ys, xs, cs, vs, save_sem, snd,
):
    at = Place()
    fs = at.z * 2 + at.y
    comm = Gatherer(at, w, zs, ys, xs, cs, snd)
    barrier = pltpu.get_barrier_semaphore()
    peers = [at.sib, at.xn] + [at.dev(at.x, yy, zz, at.c) for zz, yy in comm.others]
    for peer in peers:
        pl.semaphore_signal(barrier, inc=1, device_id=peer, device_id_type=MESH)
    vector_tile(vectors, tile)
    tiles[fs] = tile[...]
    for k in range(3):
        w[k, at.z, at.y] = w_qkv[:, k * CW : (k + 1) * CW].astype(BF)
    w[3, at.z, at.y] = w_out[...].astype(BF)
    for k in range(4):
        w[4 + k, at.z, at.y] = w_up[:, k * CW : (k + 1) * CW].astype(BF)
    for k in range(4):
        w[8 + k, at.z, at.y] = w_down[k * RU : (k + 1) * RU, :].astype(BF)
    pl.semaphore_wait(barrier, len(peers))
    for zz, yy in comm.others:
        comm.send(tile, tiles.at[fs], vs.at[fs], at.dev(at.x, yy, zz, at.c))
    saves = []

    def save(src, dst):
        copy = pltpu.make_async_copy(src, dst, save_sem.at[len(saves)])
        copy.start()
        saves.append(copy)

    def vectors_in():
        for zz, yy in comm.others:
            arrived(tiles.at[zz * 2 + yy], vs.at[zz * 2 + yy])
        vector_rows(tiles, pv)
        save(pv, pv_h)

    steps = [(-1, lambda: flag_column(flags, fcol)), (-1, vectors_in)]
    steps += [(-1, lambda i=i: norm_one(tok, fcol, pv, e1, i)) for i in range(4)]
    steps += [(0, lambda j=j, i=i: project_part(e1, w, proj, j, i)) for j in range(2) for i in range(2)]
    steps += [(1, lambda i=i: project_part(e1, w, proj, 2, i)) for i in range(2)]
    steps += [(1, lambda: save(e1, e1_h)), (1, lambda: save(proj, proj_h))]
    steps += [(1, lambda b=b, k=k: attend(proj, att, probs, b, k)) for b in range(2) for k in range(2)]
    steps += [(1, lambda: save(probs, probs_h))]
    steps += [(2, lambda i=i: norm_two(tok, fcol, pv, att, w, mid, e2, i)) for i in range(2)]
    steps += [(2, lambda: save(att, att_h)), (2, lambda: save(mid, mid_h)), (2, lambda: save(e2, e2_h))]
    for k, need in enumerate((2, 3, 3, 4)):
        steps += [(need, lambda k=k, i=i: rise(e2, w, act, dg, k, i)) for i in range(4)]
        steps += [(need, lambda k=k: save(act.at[k], act_h.at[k])), (need, lambda k=k: save(dg.at[k], dg_h.at[k]))]
    steps += [(7, lambda i=i: lower(act, w, mid, lo, i)) for i in range(2)]
    steps += [(7, lambda: save(lo, lo_h))]
    there = -1

    def fill(count):
        while steps and count and steps[0][0] <= there:
            steps.pop(0)[1]()
            count -= 1

    n, lead = len(GATHER_ITEMS), LEAD
    for i in range(lead):
        comm.start(i)
    for t in range(n + 5):
        each = EACH[t]
        if t + lead < n:
            comm.start(t + lead)
        for d in range(3):
            if 0 <= t - d < n:
                comm.hop(t - d, d)
                fill(each if t else 0)
        for stage, lag in ((comm.across, 3), (comm.handed, 4), (comm.shared, 5)):
            if 0 <= t - lag < n:
                stage(t - lag)
                if lag == 5:
                    there = t - lag
                    for j in GATHER_ITEMS[there]:
                        save(w.at[j], w_h.at[j])
                fill(each)
    fill(len(steps))
    comm.finish()
    for copy in saves:
        copy.wait()


def forward(w_qkv, w_out, w_up, w_down, vectors, tokens, flags):
    n = len(GATHER_ITEMS)
    vmem, anywhere = pl.BlockSpec(memory_space=pltpu.VMEM), pl.BlockSpec(memory_space=pl.ANY)
    dma = pltpu.SemaphoreType.DMA
    whole, three, four = (ROWS, CW), (3, ROWS, CW), (4, ROWS, CW)
    shapes = [
        (whole, BF), ((BLOCKS, 4, 2, RU, CW), BF), ((16, CW), F32), (whole, BF), (three, BF), ((4, 8, IMAGE, IMAGE), BF), (whole, BF), (whole, F32),
        (whole, BF), (four, BF), (four, BF),
    ]
    return pl.pallas_call(
        forward_kernel,
        out_shape=[jax.ShapeDtypeStruct(s, t) for s, t in shapes],
        in_specs=[vmem] * 7,
        out_specs=[anywhere] * len(shapes),
        scratch_shapes=[
            pltpu.VMEM((BLOCKS, 4, 2, RU, CW), BF),
            pltpu.VMEM((16, 128), BF),
            pltpu.VMEM((8, 16, 128), BF),
            pltpu.VMEM((16, CW), F32),
            pltpu.VMEM((ROWS, 1), F32),
            pltpu.VMEM(whole, BF),
            pltpu.VMEM(three, BF),
            pltpu.VMEM((4, 8, IMAGE, IMAGE), BF),
            pltpu.VMEM(whole, BF),
            pltpu.VMEM(whole, F32),
            pltpu.VMEM(whole, BF),
            pltpu.VMEM(four, BF),
            pltpu.VMEM(four, BF),
            pltpu.VMEM(whole, BF),
            dma((n, 3, 2)),
            dma((n, 4)),
            dma((n, 4, 2)),
            dma((BLOCKS, 4, 2)),
            dma((8,)),
            dma((32,)),
            dma,
        ],
        compiler_params=pltpu.CompilerParams(collective_id=0, has_side_effects=True, vmem_limit_bytes=VMEM_LIMIT),
        name="forward",
    )(w_qkv, w_out, w_up, w_down, vectors, tokens, flags)


def grad_out_rows(cot, fcol, counts, r, b):
    weight = float(IMAGE) / jnp.full((1, 1), counts[b], jnp.int32).astype(F32)
    return cot[r, :].astype(F32) * (fcol[r, :] * weight)


def grad_low_part(cot, fcol, counts, gl, b):
    for k in range(4):
        r = pl.ds(b * IMAGE + k * 64, 64)
        gl[r, :] = grad_out_rows(cot, fcol, counts, r, b).astype(BF)


def grad_down_part(act, gl, g, s):
    d = dot(act[s // 2, :, (s % 2) * 384 : (s % 2) * 384 + 384], gl[...], 0, 0).astype(BF)
    for k in range(4):
        g[8 + k, s // 2, s % 2] = d[k * RU : (k + 1) * RU]


def grad_rising_part(gl, w, dg, s):
    lanes = slice((s % 2) * 384, (s % 2) * 384 + 384)
    grad = dot(gl[...], down_rows(w, s, 0), 1, 1)
    dg[s // 2, :, lanes] = (grad * dg[s // 2, :, lanes].astype(F32)).astype(BF)


def weight_grad_part(left, right, g, j, i):
    d = dot(left[:, i * 384 : i * 384 + 384], right[...], 0, 0).astype(BF)
    g[j, 2 * i : 2 * i + 2] = d.reshape(2, 2, RU, CW)


def norm_back_rows(grad, n, inverse, gain):
    scaled = grad * gain
    first = jnp.mean(scaled, axis=-1, keepdims=True)
    second = jnp.mean(scaled * n, axis=-1, keepdims=True)
    return inverse * (scaled - first - n * second)


def row_sum(values):
    return jnp.sum(values, axis=0, keepdims=True)


def back_two_part(gr, w, mid, pv, cot, fcol, counts, gm, ml, vec, i, rows=128):
    r = part(i, rows)
    grad = sum(dot(gr[k, r, :], matrix(w, k), 1, 1) for k in range(4))
    n, inverse = standardize(mid[r, :])
    total = grad_out_rows(cot, fcol, counts, r, i * rows // IMAGE) + norm_back_rows(grad, n, inverse, pv[2:3, :])
    gm[r, :] = total
    ml[r, :] = total.astype(BF)
    vec[0, 2:3, :] += row_sum(grad * n)
    vec[0, 3:4, :] += row_sum(grad)


def grad_attended_part(ml, w, ga, i):
    r = part(i, 256)
    ga[r, :] = dot(ml[r, :], matrix(w, 4), 1, 1).astype(BF)


def attend_back(proj, probs, ga, dproj, b, group):
    rows = part(b, IMAGE)

    def lanes(t):
        return slice(group * 384 + t * 128, group * 384 + t * 128 + 128)

    acc = [[None] * 3 for _ in range(3)]

    def add(k, t, value):
        acc[k][t] = value if acc[k][t] is None else acc[k][t] + value

    for h, (first, tiles) in enumerate(head_lanes()):
        masks = {t: lane_mask(first, t) for t in tiles}
        low = probs[2 * b + group, h]
        grad = sum(dot(proj[2, rows, lanes(t)], ga[rows, lanes(t)] * masks[t], 1, 1) for t in tiles)
        p = low.astype(F32)
        delta = jnp.sum(grad * p, axis=0, keepdims=True)
        raw = (p * ((grad - delta) * FACTOR)).astype(BF)
        for t in tiles:
            add(0, t, dot(raw, proj[1, rows, lanes(t)] * masks[t], 0, 0))
            add(1, t, dot(raw, proj[0, rows, lanes(t)] * masks[t]))
            add(2, t, dot(low, ga[rows, lanes(t)] * masks[t]))
    for k in range(3):
        for t in range(3):
            dproj[k, rows, lanes(t)] = acc[k][t].astype(BF)


def back_one_part(dproj, w, tok, fcol, pv, gm, tg, vec, i, rows=128):
    r = part(i, rows)
    grad = sum(dot(dproj[k, r, :], matrix(w, k), 1, 1) for k in range(3))
    n, inverse = standardize(hidden_rows(tok, fcol, pv, r))
    total = norm_back_rows(grad, n, inverse, pv[0:1, :]) + gm[r, :]
    on = fcol[r, :] > 0.5
    tg[r, :] = jnp.where(on, 0.0, total).astype(BF)
    vec[0, 0:1, :] += row_sum(grad * n)
    vec[0, 1:2, :] += row_sum(grad)
    vec[0, 4:5, :] += row_sum(jnp.where(on, total, 0.0))


PLAN_END = []


class Task:
    def __init__(self, name, time, needs, sends=(), rank=0):
        self.name, self.time, self.needs, self.sends, self.rank = name, time, tuple(needs), tuple(sends), rank


def plan(tasks, rates, window, arrive, sent, issue=0.1):
    now = 0.0
    links = {name: dict(active={}, queue=[], over=[], late=[], last=0.0) for name in rates}
    done, left, order, count = {}, list(tasks), [], 0

    def advance(to):
        for name, link in links.items():
            at = link["last"]
            while link["active"]:
                share = rates[name] / len(link["active"])
                token = min(link["active"], key=lambda q: link["active"][q])
                rest = link["active"][token]
                end = at + rest / share
                if end > to + 1e-9:
                    for q in link["active"]:
                        link["active"][q] -= (to - at) * share
                    at = to
                    break
                for q in link["active"]:
                    link["active"][q] -= rest
                del link["active"][token]
                at = end
                done[token] = end + arrive
                link["late"].append((end + sent, token))
            link["last"] = max(at, to)

    while left or any(link["queue"] or link["active"] for link in links.values()):
        advance(now)
        moved = False
        for name, link in links.items():
            link["over"] += [q[1] for q in link["late"] if q[0] <= now]
            link["late"] = [q for q in link["late"] if q[0] > now]
            while link["queue"] and len(link["active"]) + len(link["late"]) < window[name]:
                link["queue"].sort()
                _, _, token, size = link["queue"].pop(0)
                order.append(("issue", token, link["over"]))
                link["over"] = []
                now += issue
                advance(now)
                link["active"][token] = size
                moved = True
        ready = [q for q in left if all(done.get(need, 1e18) <= now for need in q.needs)]
        if ready:
            task = min(ready, key=lambda q: q.rank)
            left.remove(task)
            order.append(("run", task.name))
            now += task.time
            advance(now)
            done[task.name] = now
            for name, size, token, rank in task.sends:
                count += 1
                links[name]["queue"].append((rank, count, token, size))
            moved = True
        if not moved:
            times = [v for v in done.values() if v > now]
            for name, link in links.items():
                times += [q[0] for q in link["late"] if q[0] > now]
                if link["active"]:
                    times.append(link["last"] + min(link["active"].values()) * len(link["active"]) / rates[name])
            now = max(min(times), now) + 1e-6
    PLAN_END.append(now)
    order.append(("waits", [t for link in links.values() for t in link["over"] + [q[1] for q in link["late"]]]))
    return order


ARRIVE, SENT, ISSUE = 2.5, 1.5, 0.06
RATES = dict(c=350e3, x=45e3, y=45e3, z=45e3, w=45e3, v=45e3)
WINDOW = dict(c=6, x=5, y=6, z=5, w=4, v=6)
REDUCE_ITEMS = (
    ((2,), 3), ((6,), 1), ((5,), 1), ((3, 8), 3), ((1, 0), 3), ((11,), 3), ((10, 4), 1), ((7,), 3), ((9,), 1)
)
SLOT = {blocks: k for k, (blocks, _) in enumerate(REDUCE_ITEMS)}
PAIR_SLOT = {blocks: k for k, blocks in enumerate(b for b, _ in REDUCE_ITEMS if len(b) == 2)}


def reduce_items():
    return [(blocks, k * (H // parts), H // parts) for blocks, parts in REDUCE_ITEMS for k in range(parts)]


def reduce_tasks(items, made):
    tasks = []
    for i, (blocks, _, rows) in enumerate(items):
        pair, size, add = len(blocks) == 2, rows * CW * 2, 0.04 * rows / H
        needs = [token for j in blocks for token in made[j]]
        to_sib = [("c", 8 * size, ("mine", i), i)]
        to_y = [("y", 2 * size, ("y0", i), i), ("y", 2 * size, ("y1", i), i)]
        if pair:
            to_x = [("x", 4 * size, ("x0", i), i), ("x", 4 * size, ("x1", i), i)]
            tasks.append(Task(("A", i), 0.05, needs, [("c", 8 * size, ("theirs", i), i)] + to_sib, i))
            tasks.append(Task(("Bt", i), 8 * add, [("theirs", i)], to_x, i))
            tasks.append(Task(("Bm", i), 8 * add, [("mine", i)], [], i))
            tasks.append(Task(("C", i), 8 * add, [("x0", i), ("x1", i), ("Bm", i)], to_y, i))
        else:
            tasks.append(Task(("A", i), 0.05, needs, to_sib, i))
            tasks.append(Task(("Bm", i), 8 * add, [("mine", i)], to_y, i))
        tasks.append(Task(("D", i), 4 * add, [("y0", i), ("y1", i)], [("z", 3 * size, ("za", i), i)], i))
        tasks.append(Task(("E1", i), 3 * add, [("za", i)], [("w", 2 * size, ("zb", i), i - 50)], i))
        tasks.append(Task(("E2", i), 2 * add, [("zb", i)], [("v", size, ("zc", i), i - 50)], i))
        tasks.append(Task(("E3", i), add, [("zc", i)], [("x", size, ("xf", i), i - 100)], i))
        finals = [("f%d" % k, i) for k in range(len(blocks))]
        tasks.append(Task(("G", i), 2 * add, [("xf", i)], [("c", size, f, i) for f in finals], i))
        tasks.append(Task(("H", i), 0.05, finals, [], i))
    return tasks


def vector_tasks(made):
    size = 8 * CW * 4
    return [
        Task(("V0", 0), 0.05, made, [("c", size, ("vc", 0), -200)], -200),
        Task(("V1", 0), 0.05, [("vc", 0)], [("x", size, ("vx", 0), -200)], -200),
        Task(("V2", 0), 0.05, [("vx", 0)], [("y", size, ("vy", 0), -200)], -200),
        Task(("V3", 0), 0.05, [("vy", 0)], [("z", size, ("vz%d" % d, 0), -200) for d in (1, 2, 3)], -200),
        Task(("V4", 0), 0.05, [("vz%d" % d, 0) for d in (1, 2, 3)], [], -200),
    ]


class Sender:
    def __init__(self, sems, window):
        self.sems, self.queued, self.under_way = sems, {}, {}
        self.free, first = {}, 0
        for name, slots in window.items():
            self.free[name] = list(range(first, first + slots))
            first += slots

    def put(self, token, link, src, dst, sem, to, cond=None):
        self.queued[token] = (link, src, dst, sem, to, cond)

    def issue(self, token, over):
        self.wait(over)
        link, src, dst, sem, to, cond = self.queued.pop(token)
        slot = self.free[link].pop(0)
        copy = pltpu.make_async_remote_copy(
            src_ref=src, dst_ref=dst, send_sem=self.sems.at[slot], recv_sem=sem, device_id=to, device_id_type=MESH
        )
        if cond is None:
            copy.start()
        else:
            pl.when(cond)(copy.start)
        self.under_way[token] = (link, slot, copy, cond)

    def wait(self, tokens):
        for token in tokens:
            link, slot, copy, cond = self.under_way.pop(token)
            self.free[link].append(slot)
            if cond is None:
                copy.wait_send()
            else:
                pl.when(cond)(copy.wait_send)


class Reducer:
    def __init__(self, at, items, sender, g, fin, sr, xr, yr, zr, xf, vec, vr, sems):
        self.at, self.items, self.sender = at, items, sender
        self.g, self.fin, self.sr, self.xr, self.yr, self.zr, self.xf = g, fin, sr, xr, yr, zr, xf
        self.vec, self.vr = vec, vr
        self.ssem, self.xsem, self.ysem, self.zsem, self.xfsem, self.fsem, self.vsem = sems

    def run(self, op, i):
        if op[0] == "V":
            return self.vectors(op)
        at, g, y, z = self.at, self.g, self.at.y, self.at.z
        blocks, first, count = self.items[i]
        pair, key, m = len(blocks) == 2, SLOT[blocks], self.at.mine(blocks)
        xkey = PAIR_SLOT.get(blocks)
        loc = pl.ds(first, count)
        own_rows = pl.ds(pl.multiple_of(at.c * H + first, 16), count)
        sib_rows = pl.ds(pl.multiple_of((1 - at.c) * H + first, 16), count)

        def add_shards(j, src):
            def body(k, _):
                d = g.at[j, k // 2, k % 2, own_rows, :]
                add_into(d, d, src.at[k // 2, k % 2, loc, :])
                return 0

            lax.fori_loop(0, 8, body, 0)

        def to_y():
            for q in range(2):
                two = pl.ds(2 * q, 2)
                self.sender.put(
                    ("y%d" % q, i), "y", g.at[m, two, 1 - y, own_rows, :], self.yr.at[key, two, loc, :],
                    self.ysem.at[i, q], at.yn,
                )

        if op == "A":
            if pair:
                t = at.theirs(blocks)
                self.sender.put(
                    ("theirs", i), "c", g.at[t, :, :, sib_rows, :], self.sr.at[t, :, :, loc, :], self.ssem.at[i, 1], at.sib
                )
            self.sender.put(
                ("mine", i), "c", g.at[m, :, :, sib_rows, :], self.sr.at[m, :, :, loc, :], self.ssem.at[i, 0], at.sib
            )
        elif op == "Bm":
            arrived(self.sr.at[m, :, :, loc, :], self.ssem.at[i, 0])
            add_shards(m, self.sr.at[m])
            if not pair:
                to_y()
        elif op == "Bt":
            t = at.theirs(blocks)
            arrived(self.sr.at[t, :, :, loc, :], self.ssem.at[i, 1])
            add_shards(t, self.sr.at[t])
            for q in range(2):
                two = pl.ds(2 * q, 2)
                self.sender.put(
                    ("x%d" % q, i), "x", g.at[t, two, :, own_rows, :], self.xr.at[xkey, two, :, loc, :],
                    self.xsem.at[i, q], at.xn,
                )
        elif op == "C":
            for q in range(2):
                arrived(self.xr.at[xkey, pl.ds(2 * q, 2), :, loc, :], self.xsem.at[i, q])
            add_shards(m, self.xr.at[xkey])
            to_y()
        elif op == "D":
            for q in range(2):
                arrived(self.yr.at[key, pl.ds(2 * q, 2), loc, :], self.ysem.at[i, q])

            def body(k, _):
                d = g.at[m, k, y, own_rows, :]
                add_into(d, d, self.yr.at[key, k, loc, :])
                return 0

            lax.fori_loop(0, 4, body, 0)
            self.sender.put(
                ("za", i), "z", g.at[m, pl.ds(1 - z // 3, 3), y, own_rows, :], self.zr.at[key, pl.ds(0, 3), loc, :],
                self.zsem.at[i, 0], at.inner, at.end,
            )
        elif op == "E1":

            @pl.when(at.mid)
            def _():
                arrived(self.zr.at[key, pl.ds(0, 3), loc, :], self.zsem.at[i, 0])
                for k in range(3):
                    d = g.at[m, 2 - z + k, y, own_rows, :]
                    add_into(d, d, self.zr.at[key, k, loc, :])

            self.sender.put(
                ("zb", i), "w", g.at[m, pl.ds(2 * (2 - z), 2), y, own_rows, :], self.zr.at[key, pl.ds(3, 2), loc, :],
                self.zsem.at[i, 1], at.inner, at.mid,
            )
        elif op == "E2":

            @pl.when(at.mid)
            def _():
                arrived(self.zr.at[key, pl.ds(3, 2), loc, :], self.zsem.at[i, 1])
                for k in range(2):
                    d = g.at[m, 2 * (z - 1) + k, y, own_rows, :]
                    add_into(d, d, self.zr.at[key, 3 + k, loc, :])

            self.sender.put(
                ("zc", i), "v", g.at[m, 3 * (z - 1), y, own_rows, :], self.zr.at[key, 0, loc, :],
                self.zsem.at[i, 2], at.outer, at.mid,
            )
        elif op == "E3":
            d = g.at[m, z, y, own_rows, :]

            @pl.when(at.end)
            def _():
                arrived(self.zr.at[key, 0, loc, :], self.zsem.at[i, 2])
                add_into(d, d, self.zr.at[key, 0, loc, :])

            self.sender.put(("xf", i), "x", d, self.xf.at[key, loc, :], self.xfsem.at[i], at.xn)
        elif op == "G":
            arrived(self.xf.at[key, loc, :], self.xfsem.at[i])
            d = g.at[m, z, y, own_rows, :]
            if pair:
                self.fin[m, own_rows, :] = d[...]
                self.fin[at.theirs(blocks), own_rows, :] = self.xf[key, loc, :]
            else:
                add_into(self.fin.at[m, own_rows, :], d, self.xf.at[key, loc, :])
            for k, j in enumerate((m, at.theirs(blocks)) if pair else blocks):
                f = self.fin.at[j, own_rows, :]
                self.sender.put(("f%d" % k, i), "c", f, f, self.fsem.at[i, k], at.sib)
        elif op == "H":
            for k, j in enumerate((m, at.theirs(blocks)) if pair else blocks):
                arrived(self.fin.at[j, sib_rows, :], self.fsem.at[i, k])

    def vectors(self, op):
        at, vec, vr, vsem = self.at, self.vec, self.vr, self.vsem
        if op == "V0":
            self.sender.put(("vc", 0), "c", vec.at[0], vr.at[0], vsem.at[0], at.sib)
        elif op == "V1":
            arrived(vr.at[0], vsem.at[0])
            vec[1] = vec[0] + vr[0]
            self.sender.put(("vx", 0), "x", vec.at[1], vr.at[1], vsem.at[1], at.xn)
        elif op == "V2":
            arrived(vr.at[1], vsem.at[1])
            vec[2] = vec[1] + vr[1]
            self.sender.put(("vy", 0), "y", vec.at[2], vr.at[2], vsem.at[2], at.yn)
        elif op == "V3":
            arrived(vr.at[2], vsem.at[2])
            vec[3] = vec[2] + vr[2]
            vr[3 + at.z] = vec[3]
            for d, to in ((1, at.up), (2, at.far), (3, at.down)):
                self.sender.put(("vz%d" % d, 0), "z", vec.at[3], vr.at[3 + at.z], vsem.at[3 + at.z], to)
        else:
            for d in (1, 2, 3):
                arrived(vr.at[3 + (at.z + d) % 4], vsem.at[3 + (at.z + d) % 4])
            vec[4] = ((vr[3] + vr[4]) + vr[5]) + vr[6]


def reduce_barrier(at):
    barrier = pltpu.get_barrier_semaphore()
    peers = [at.sib, at.xn, at.yn, at.up, at.far, at.down]
    for peer in peers:
        pl.semaphore_signal(barrier, inc=1, device_id=peer, device_id_type=MESH)
    pl.semaphore_wait(barrier, len(peers))


def reduce_scratch(n):
    dma = pltpu.SemaphoreType.DMA
    return [
        pltpu.VMEM((BLOCKS, 4, 2, H, CW), BF),
        pltpu.VMEM((len(PAIR_SLOT), 4, 2, H, CW), BF),
        pltpu.VMEM((len(SLOT), 4, H, CW), BF),
        pltpu.VMEM((len(SLOT), 5, H, CW), BF),
        pltpu.VMEM((len(SLOT), H, CW), BF),
        pltpu.VMEM((5, 8, CW), F32),
        pltpu.VMEM((7, 8, CW), F32),
        dma((n, 2)),
        dma((n, 2)),
        dma((n, 2)),
        dma((n, 3)),
        dma((n,)),
        dma((n, 2)),
        dma((7,)),
        dma((sum(WINDOW.values()),)),
    ]


LOADS = ("act", "cot", "dg", "d0", "d1", "d2", "d3", "e2", "mid", "out", "att", "proj", "probs", "e1", "tok")


def backward_tasks():
    rows = [(("gl", b), 0.5, []) for b in range(2)]
    low = [("gl", b) for b in range(2)]
    rows += [(("gd", s), 0.45, low) for s in range(8)]
    rows += [(("gr", s), 0.6, low) for s in range(8)]
    rows += [(("gu", k, i), 0.6, [("gr", 2 * k), ("gr", 2 * k + 1)]) for k in range(4) for i in range(2)]
    rows += [(("b2", b), 2.4, [("gr", s) for s in range(8)]) for b in range(2)]
    two = [("b2", b) for b in range(2)]
    rows += [(("go", i), 0.75, two) for i in range(2)]
    rows += [(("ga", b), 0.75, [("b2", b)]) for b in range(2)]
    rows += [(("ab", b, k), 3.4, [("ga", b)]) for b in range(2) for k in range(2)]
    heads = [("ab", b, k) for b in range(2) for k in range(2)]
    rows += [(("gq", j, i), 0.7, heads) for j in range(3) for i in range(2)]
    rows += [(("b1", b), 2.1, heads) for b in range(2)]
    made = [[("gq", j, i) for i in range(2)] for j in range(3)]
    made += [[("go", i) for i in range(2)]]
    made += [[("gu", k, i) for i in range(2)] for k in range(4)]
    made += [[("gd", s) for s in range(8)]] * 4
    tasks = [Task(name, time, needs, (), 1000 + k) for k, (name, time, needs) in enumerate(rows)]
    return tasks, made, [("b1", b) for b in range(2)]


def backward_kernel(
    items, order,
    flags, counts, pv, act_h, cot_h, dg_h, w_h, e2_h, mid_h, att_h, proj_h, probs_h, e1_h, tok_h,
    tg_h, fin, vec_out,
    act, cot, dg, w, e2, mid, att, proj, probs, e1, tok, fcol, gl, gm, ml, g, load_sem, tg_sem, *reduce_refs,
):
    at = Place()
    source = dict(act=act_h, cot=cot_h, dg=dg_h, e2=e2_h, mid=mid_h, att=att_h, proj=proj_h, probs=probs_h, e1=e1_h, tok=tok_h)
    target = dict(act=act, cot=cot, dg=dg, e2=e2, mid=mid, att=att, proj=proj, probs=probs, e1=e1, tok=tok)
    loads = {}

    def load(name, src, dst):
        loads[name] = pltpu.make_async_copy(src, dst, load_sem.at[len(loads)])
        loads[name].start()

    def need(*names):
        for name in names:
            if loads[name] is not None:
                loads[name].wait()
                loads[name] = None

    for name in LOADS:
        if name in source:
            load(name, source[name], target[name])
        elif name == "out":
            load(name, w_h.at[3], w.at[4])
        else:
            load(name, w_h.at[8 + int(name[1])], w.at[int(name[1])])
    vec = reduce_refs[5]
    vec[0] = jnp.zeros((8, CW), F32)
    flag_column(flags, fcol)
    reduce_barrier(at)
    sender = Sender(reduce_refs[-1], WINDOW)
    steps = Reducer(at, items, sender, g, fin, *reduce_refs[:7], reduce_refs[7:14])
    dproj, ga, tg = act, gl, ml

    def compute(op, *k):
        if op == "gl":
            need("cot")
            grad_low_part(cot, fcol, counts, gl, *k)
        elif op == "gd":
            need("act")
            grad_down_part(act, gl, g, *k)
        elif op == "gr":
            need("dg", "d0", "d1", "d2", "d3")
            grad_rising_part(gl, w, dg, *k)
            if k[0] == 7:
                for j in range(4):
                    load("u%d" % j, w_h.at[4 + j], w.at[j])
        elif op == "gu":
            need("e2")
            weight_grad_part(e2, dg.at[k[0]], g, 4 + k[0], k[1])
        elif op == "b2":
            need("mid", "u0", "u1", "u2", "u3")
            back_two_part(dg, w, mid, pv, cot, fcol, counts, gm, ml, vec, *k, rows=IMAGE)
            if k[0] == 1:
                for j in range(3):
                    load("q%d" % j, w_h.at[j], w.at[j])
        elif op == "go":
            need("att")
            weight_grad_part(att, ml, g, 3, *k)
        elif op == "ga":
            need("out")
            grad_attended_part(ml, w, ga, *k)
        elif op == "ab":
            need("proj", "probs")
            attend_back(proj, probs, ga, dproj, *k)
        elif op == "gq":
            need("e1")
            weight_grad_part(e1, dproj.at[k[0]], g, *k)
        elif op == "b1":
            need("tok", "q0", "q1", "q2")
            back_one_part(dproj, w, tok, fcol, pv, gm, tg, vec, *k, rows=IMAGE)
            if k[0] == 1:
                pltpu.make_async_copy(tg, tg_h, tg_sem).start()

    for entry in order:
        if entry[0] == "issue":
            sender.issue(entry[1], entry[2])
        elif entry[0] == "waits":
            sender.wait(entry[1])
        elif entry[1][0][0].isupper():
            steps.run(*entry[1])
        else:
            compute(*entry[1])
    pltpu.make_async_copy(tg, tg_h, tg_sem).wait()
    vec_out[...] = vec[4]


def backward(flags, counts, pv, act, cot, dg, w, e2, mid, att, proj, probs, e1, tok):
    items = reduce_items()
    steps, made, vector_made = backward_tasks()
    order = plan(steps + reduce_tasks(items, made) + vector_tasks(vector_made), RATES, WINDOW, ARRIVE, SENT, ISSUE)
    vmem, anywhere = pl.BlockSpec(memory_space=pltpu.VMEM), pl.BlockSpec(memory_space=pl.ANY)
    whole, three, four = (ROWS, CW), (3, ROWS, CW), (4, ROWS, CW)
    dma = pltpu.SemaphoreType.DMA
    return pl.pallas_call(
        functools.partial(backward_kernel, items, order),
        out_shape=[
            jax.ShapeDtypeStruct(whole, BF),
            jax.ShapeDtypeStruct((BLOCKS, RU, CW), BF),
            jax.ShapeDtypeStruct((8, CW), F32),
        ],
        in_specs=[vmem, pl.BlockSpec(memory_space=pltpu.SMEM), vmem] + [anywhere] * 11,
        out_specs=[anywhere, vmem, vmem],
        scratch_shapes=[
            pltpu.VMEM(four, BF),
            pltpu.VMEM(whole, BF),
            pltpu.VMEM(four, BF),
            pltpu.VMEM((5, 4, 2, RU, CW), BF),
            pltpu.VMEM(whole, BF),
            pltpu.VMEM(whole, F32),
            pltpu.VMEM(whole, BF),
            pltpu.VMEM(three, BF),
            pltpu.VMEM((4, 8, IMAGE, IMAGE), BF),
            pltpu.VMEM(whole, BF),
            pltpu.VMEM(whole, BF),
            pltpu.VMEM((ROWS, 1), F32),
            pltpu.VMEM(whole, BF),
            pltpu.VMEM(whole, F32),
            pltpu.VMEM(whole, BF),
            pltpu.VMEM((BLOCKS, 4, 2, RU, CW), BF),
            dma((24,)),
            dma,
        ]
        + reduce_scratch(len(items)),
        compiler_params=pltpu.CompilerParams(collective_id=1, has_side_effects=True, vmem_limit_bytes=VMEM_LIMIT),
        name="backward",
    )(flags, counts, pv, act, cot, dg, w, e2, mid, att, proj, probs, e1, tok)


def adam_kernel(fin, vec, fs, *refs):
    states, vecs, outs, vec_outs = refs[:12], refs[12:15], refs[15:27], refs[27:31]
    ins, news, in_sem, out_sem = refs[31:]

    def block(ref, j):
        if j < 3:
            return ref.at[:, pl.ds(j * CW, CW)]
        if j == 3:
            return ref
        if j < 8:
            return ref.at[:, pl.ds((j - 4) * CW, CW)]
        return ref.at[pl.ds((j - 8) * RU, RU), :]

    matrix_of = [0] * 3 + [1] + [2] * 4 + [3] * 4
    loads, saves = [], []
    for j in range(BLOCKS):
        three = [
            pltpu.make_async_copy(block(states[3 * matrix_of[j] + k], j), ins.at[j, k], in_sem.at[j, k]) for k in range(3)
        ]
        for copy in three:
            copy.start()
        loads.append(three)
    column = lax.broadcasted_iota(jnp.int32, (RU, CW), 1) == lax.broadcasted_iota(jnp.int32, (RU, CW), 0) + fs[0] * RU
    grad = lax.dot_general(
        vec[...], column.astype(F32), (((1,), (1,)), ((), ())), preferred_element_type=F32,
        precision=lax.Precision.HIGHEST,
    )
    first, second, new = adamw(vecs[0][...], grad[0:5], vecs[1][...], vecs[2][...], RATE_VECTORS)
    vec_outs[0][...] = first
    vec_outs[1][0:2, :] = second[0:2]
    vec_outs[1][2:3, :] = second[4:5]
    vec_outs[2][...] = second[2:4]
    vec_outs[3][...] = new
    for j in range(BLOCKS):
        rate = (RATE_QKV, RATE_OUT, RATE_UP, RATE_DOWN)[matrix_of[j]]
        for copy in loads[j]:
            copy.wait()

        def rows(i, _, j=j, rate=rate):
            r = part(i, 16)
            result = adamw(ins[j, 0, r, :], fin[j, r, :].astype(F32), ins[j, 1, r, :], ins[j, 2, r, :], rate)
            for k in range(3):
                news[j, k, r, :] = result[k]
            return 0

        lax.fori_loop(0, RU // 16, rows, 0)
        for k in range(3):
            copy = pltpu.make_async_copy(news.at[j, k], block(outs[3 * matrix_of[j] + k], j), out_sem.at[j, k])
            copy.start()
            saves.append(copy)
    for copy in saves:
        copy.wait()


def adam(fin, vec, fs, states, vecs):
    vmem, anywhere = pl.BlockSpec(memory_space=pltpu.VMEM), pl.BlockSpec(memory_space=pl.ANY)
    dma = pltpu.SemaphoreType.DMA
    return pl.pallas_call(
        adam_kernel,
        out_shape=[jax.ShapeDtypeStruct(s.shape, F32) for s in states]
        + [jax.ShapeDtypeStruct((n, RU), F32) for n in (5, 3, 2, 5)],
        in_specs=[vmem, vmem, pl.BlockSpec(memory_space=pltpu.SMEM)] + [anywhere] * 12 + [vmem] * 3,
        out_specs=[anywhere] * 12 + [vmem] * 4,
        scratch_shapes=[
            pltpu.VMEM((BLOCKS, 3, RU, CW), F32),
            pltpu.VMEM((BLOCKS, 3, RU, CW), F32),
            dma((BLOCKS, 3)),
            dma((BLOCKS, 3)),
        ],
        compiler_params=pltpu.CompilerParams(vmem_limit_bytes=VMEM_LIMIT),
        name="adam",
    )(fin, vec, fs, *states, *vecs)


def on_device_plain(
    tokens,
    mask_flags,
    mask_counts,
    cotangent,
    w_qkv,
    w_out,
    w_up,
    w_down,
    vectors,
    first_qkv,
    first_out,
    first_up,
    first_down,
    first_vectors,
    second_qkv,
    second_out,
    second_up,
    second_down,
    second_vectors,
):
    rows, width = tokens.shape
    images = mask_counts.shape[0]
    length = rows // images
    factor = HEAD_DIM ** (-0.5)
    attn_shards = (
        w_qkv.astype(jnp.bfloat16),
        w_out.astype(jnp.bfloat16),
        vectors.astype(jnp.bfloat16),
    )
    mlp_shards = (w_up.astype(jnp.bfloat16), w_down.astype(jnp.bfloat16))
    full_qkv, full_out, full_vec = (
        lax.all_gather(attn_shards[0], "fsdp", axis=0, tiled=True),
        lax.all_gather(attn_shards[1], "fsdp", axis=0, tiled=True),
        lax.all_gather(attn_shards[2], "fsdp", axis=0, tiled=True),
    )
    full_up, full_down = (
        lax.all_gather(mlp_shards[0], "fsdp", axis=0, tiled=True),
        lax.all_gather(mlp_shards[1], "fsdp", axis=0, tiled=True),
    )
    params = full_vec.astype(jnp.float32)
    masked = (mask_flags == 1)[:, None]
    hidden = jnp.where(masked, params[:, 4][None, :], tokens.astype(jnp.float32))
    normed_one, inverse_one = standardize(hidden)
    entry_one = (normed_one * params[:, 0] + params[:, 1]).astype(jnp.bfloat16)
    project = jnp.dot(entry_one, full_qkv, preferred_element_type=jnp.float32).astype(jnp.bfloat16)
    split = project.reshape(images, length, 3, HEADS, HEAD_DIM)
    queries = split[:, :, 0]
    keys = split[:, :, 1]
    values = split[:, :, 2]
    scores = (
        jnp.einsum("bqhd,bkhd->bhqk", queries, keys, preferred_element_type=jnp.float32) * factor
    )
    top = jnp.max(scores, axis=-1, keepdims=True)
    total = jnp.sum(jnp.exp(scores - top), axis=-1, keepdims=True)
    logsum = top + jnp.log(total)
    probs_low = jnp.exp(scores - logsum).astype(jnp.bfloat16)
    mixed = jnp.einsum("bhqk,bkhd->bqhd", probs_low, values, preferred_element_type=jnp.float32)
    attended = mixed.astype(jnp.bfloat16).reshape(rows, width)
    middle = hidden + jnp.dot(attended, full_out, preferred_element_type=jnp.float32)
    normed_two, inverse_two = standardize(middle)
    entry_two = (normed_two * params[:, 2] + params[:, 3]).astype(jnp.bfloat16)
    rising = jnp.dot(entry_two, full_up, preferred_element_type=jnp.float32)
    activated, gelu_pull = jax.vjp(gelu_exact, rising)
    active = activated.astype(jnp.bfloat16)
    layer_out = (middle + jnp.dot(active, full_down, preferred_element_type=jnp.float32)).astype(
        jnp.bfloat16
    )
    row_weight = jnp.repeat(
        length / mask_counts.astype(jnp.float32), length, total_repeat_length=rows
    )
    grad_out = (
        cotangent.astype(jnp.float32) * (row_weight * mask_flags.astype(jnp.float32))[:, None]
    )
    back_up, back_down = (
        lax.all_gather(mlp_shards[0], "fsdp", axis=0, tiled=True),
        lax.all_gather(mlp_shards[1], "fsdp", axis=0, tiled=True),
    )
    back_qkv, back_out, back_vec = (
        lax.all_gather(attn_shards[0], "fsdp", axis=0, tiled=True),
        lax.all_gather(attn_shards[1], "fsdp", axis=0, tiled=True),
        lax.all_gather(attn_shards[2], "fsdp", axis=0, tiled=True),
    )
    gains = back_vec.astype(jnp.float32)
    grad_low = grad_out.astype(jnp.bfloat16)
    grad_down = jnp.einsum("tf,td->fd", active, grad_low, preferred_element_type=jnp.float32)
    grad_active = jnp.einsum("td,fd->tf", grad_low, back_down, preferred_element_type=jnp.float32)
    grad_rising = gelu_pull(grad_active)[0].astype(jnp.bfloat16)
    grad_up = jnp.einsum("td,tf->df", entry_two, grad_rising, preferred_element_type=jnp.float32)
    grad_entry_two = jnp.einsum(
        "tf,df->td", grad_rising, back_up, preferred_element_type=jnp.float32
    )
    mlp_sums = (
        lax.psum_scatter(grad_up, "fsdp", scatter_dimension=0, tiled=True),
        lax.psum_scatter(grad_down, "fsdp", scatter_dimension=0, tiled=True),
    )
    back_two, gain_two, bias_two = norm_back(grad_entry_two, normed_two, inverse_two, gains[:, 2])
    grad_middle = grad_out + back_two
    middle_low = grad_middle.astype(jnp.bfloat16)
    grad_wout = jnp.einsum("tc,td->cd", attended, middle_low, preferred_element_type=jnp.float32)
    grad_attended = jnp.einsum(
        "td,cd->tc", middle_low, back_out, preferred_element_type=jnp.float32
    )
    grad_attended = grad_attended.astype(jnp.bfloat16).reshape(images, length, HEADS, HEAD_DIM)
    again_scores = (
        jnp.einsum("bqhd,bkhd->bhqk", queries, keys, preferred_element_type=jnp.float32) * factor
    )
    probs = jnp.exp(again_scores - logsum)
    again_low = probs.astype(jnp.bfloat16)
    grad_values = jnp.einsum(
        "bhqk,bqhd->bkhd", again_low, grad_attended, preferred_element_type=jnp.float32
    )
    grad_probs = jnp.einsum(
        "bqhd,bkhd->bhqk", grad_attended, values, preferred_element_type=jnp.float32
    )
    grad_scores = probs * (grad_probs - jnp.sum(grad_probs * probs, axis=-1, keepdims=True))
    grad_raw = (grad_scores * factor).astype(jnp.bfloat16)
    grad_queries = jnp.einsum("bhqk,bkhd->bqhd", grad_raw, keys, preferred_element_type=jnp.float32)
    grad_keys = jnp.einsum("bhqk,bqhd->bkhd", grad_raw, queries, preferred_element_type=jnp.float32)
    grad_project = (
        jnp.stack([grad_queries, grad_keys, grad_values], axis=2)
        .reshape(rows, 3 * width)
        .astype(jnp.bfloat16)
    )
    grad_qkv = jnp.einsum("td,te->de", entry_one, grad_project, preferred_element_type=jnp.float32)
    grad_entry_one = jnp.einsum(
        "te,de->td", grad_project, back_qkv, preferred_element_type=jnp.float32
    )
    back_one, gain_one, bias_one = norm_back(grad_entry_one, normed_one, inverse_one, gains[:, 0])
    grad_hidden = back_one + grad_middle
    token_grad = jnp.where(masked, 0.0, grad_hidden).astype(jnp.bfloat16)
    grad_mask = jnp.sum(jnp.where(masked, grad_hidden, 0.0), axis=0)
    grad_vec = jnp.stack([gain_one, bias_one, gain_two, bias_two, grad_mask], axis=1)
    attn_sums = (
        lax.psum_scatter(grad_qkv, "fsdp", scatter_dimension=0, tiled=True),
        lax.psum_scatter(grad_wout, "fsdp", scatter_dimension=0, tiled=True),
        lax.psum_scatter(grad_vec, "fsdp", scatter_dimension=0, tiled=True),
    )
    sum_qkv, sum_out, sum_vec, sum_up, sum_down = (
        lax.psum(attn_sums[0].astype(jnp.bfloat16), "dp").astype(jnp.float32),
        lax.psum(attn_sums[1].astype(jnp.bfloat16), "dp").astype(jnp.float32),
        lax.psum(attn_sums[2].astype(jnp.bfloat16), "dp").astype(jnp.float32),
        lax.psum(mlp_sums[0].astype(jnp.bfloat16), "dp").astype(jnp.float32),
        lax.psum(mlp_sums[1].astype(jnp.bfloat16), "dp").astype(jnp.float32),
    )
    qkv_first, qkv_second, qkv_new = adamw(w_qkv, sum_qkv, first_qkv, second_qkv, RATE_QKV)
    out_first, out_second, out_new = adamw(w_out, sum_out, first_out, second_out, RATE_OUT)
    up_first, up_second, up_new = adamw(w_up, sum_up, first_up, second_up, RATE_UP)
    down_first, down_second, down_new = adamw(w_down, sum_down, first_down, second_down, RATE_DOWN)
    vec_first, vec_second, vec_new = adamw(
        vectors, sum_vec, first_vectors, second_vectors, RATE_VECTORS
    )
    second_front = jnp.concatenate([vec_second[:, 0:2], vec_second[:, 4:5]], axis=1)
    second_later = vec_second[:, 2:4]
    return (
        layer_out,
        token_grad,
        qkv_first,
        out_first,
        up_first,
        down_first,
        vec_first,
        qkv_second,
        out_second,
        up_second,
        down_second,
        second_front,
        second_later,
        qkv_new,
        out_new,
        up_new,
        down_new,
        vec_new,
    )


def on_device_fast(
    tokens,
    mask_flags,
    mask_counts,
    cotangent,
    w_qkv,
    w_out,
    w_up,
    w_down,
    vectors,
    first_qkv,
    first_out,
    first_up,
    first_down,
    first_vectors,
    second_qkv,
    second_out,
    second_up,
    second_down,
    second_vectors,
):
    flags = mask_flags.reshape(1, ROWS)
    layer_out, w, pv, e1, proj, probs, att, mid, e2, act, dg = forward(
        w_qkv, w_out, w_up, w_down, vectors.T, tokens, flags
    )
    token_grad, sums, sum_vec = backward(
        flags, mask_counts, pv, act, cotangent, dg, w, e2, mid, att, proj, probs, e1, tokens
    )
    states = (
        w_qkv, first_qkv, second_qkv, w_out, first_out, second_out,
        w_up, first_up, second_up, w_down, first_down, second_down,
    )
    fs = lax.axis_index("fsdp").astype(jnp.int32).reshape(1)
    new = adam(sums, sum_vec, fs, states, (vectors.T, first_vectors.T, second_vectors.T))
    new_w, new_first, new_second = [[new[3 * m + k] for m in range(4)] for k in (2, 0, 1)]
    vec_first, second_front, second_later, vec_new = [v.T for v in new[12:]]
    return (
        layer_out, token_grad, *new_first, vec_first, *new_second, second_front, second_later, *new_w, vec_new
    )


def solution(mesh):
    placed = (
        P(("dp", "fsdp"), None),
        P(("dp", "fsdp")),
        P(("dp", "fsdp")),
        P(("dp", "fsdp"), None),
        P("fsdp", None),
        P("fsdp", None),
        P("fsdp", None),
        P("fsdp", None),
        P("fsdp", None),
        P("fsdp", None),
        P("fsdp", None),
        P("fsdp", None),
        P("fsdp", None),
        P("fsdp", None),
        P("fsdp", None),
        P("fsdp", None),
        P("fsdp", None),
        P("fsdp", None),
        P("fsdp", None),
    )
    shape = dict(mesh.shape)
    fast = shape["dp"] == 4 and shape["fsdp"] == 8
    return jax.shard_map(
        on_device_fast if fast else on_device_plain,
        mesh=mesh,
        in_specs=placed,
        out_specs=(
            P(("dp", "fsdp"), None),
            P(("dp", "fsdp"), None),
            P("fsdp", None),
            P("fsdp", None),
            P("fsdp", None),
            P("fsdp", None),
            P("fsdp", None),
            P("fsdp", None),
            P("fsdp", None),
            P("fsdp", None),
            P("fsdp", None),
            P("fsdp", None),
            P("fsdp", None),
            P("fsdp", None),
            P("fsdp", None),
            P("fsdp", None),
            P("fsdp", None),
            P("fsdp", None),
        ),
        check_vma=False,
    )
```

```python
import functools

import jax
import jax.numpy as jnp
from jax import lax
from jax.experimental import pallas as pl
from jax.experimental.pallas import tpu as pltpu
from jax.sharding import PartitionSpec as P

HEADS = 16
HEAD_DIM = 48
STEP = 10


EPS_NORM = 1e-06
BETA_ONE = 0.5
BETA_TWO = 0.5
ADAM_EPS = 1e-08
DECAY = 0.01
RATE_QKV = 0.02
RATE_OUT = 0.1
RATE_UP = 0.02
RATE_DOWN = 0.01
RATE_VECTORS = 0.2

BF = jnp.bfloat16
F32 = jnp.float32
MESH = pl.DeviceIdType.MESH

RU, CW, H = 96, 768, 48
BLOCKS = 12
GATHER_ITEMS = (
    ((0, 1), 1, False), ((2,), 1, False), ((3, 4), 1, False), ((11,), 1, False), ((7, 10), 1, True), ((5,), 1, True),
    ((6, 8), 1, False), ((9,), 1, True),
)
GATHER_RATES = dict(u=46e3, d=46e3, y=46e3, x=46e3, c=280e3)
GATHER_WINDOW = dict(u=2, d=2, y=4, x=8, c=6)
GATHER_ISSUE = 0.2
VMEM_LIMIT = 62 * 2**20


def standardize(values):
    mean = jnp.mean(values, axis=-1, keepdims=True)
    centred = values - mean
    inverse = lax.rsqrt(jnp.mean(centred * centred, axis=-1, keepdims=True) + EPS_NORM)
    return (centred * inverse, inverse)


def norm_back(grad, normed, inverse, gain):
    scaled = grad * gain[None, :]
    first = jnp.mean(scaled, axis=-1, keepdims=True)
    second = jnp.mean(scaled * normed, axis=-1, keepdims=True)
    return (
        inverse * (scaled - first - normed * second),
        jnp.sum(grad * normed, axis=0),
        jnp.sum(grad, axis=0),
    )


def gelu_exact(values):
    return jax.nn.gelu(values, approximate=False)


def adamw(weight, grad, first, second, rate):
    new_first = BETA_ONE * first + (1.0 - BETA_ONE) * grad
    new_second = BETA_TWO * second + (1.0 - BETA_TWO) * grad * grad
    fix_one = 1.0 - BETA_ONE**STEP
    fix_two = 1.0 - BETA_TWO**STEP
    ratio = new_first / fix_one / (jnp.sqrt(new_second / fix_two) + ADAM_EPS)
    return (new_first, new_second, weight - rate * (ratio + DECAY * weight))


class Place:
    def __init__(self):
        dp, fs = lax.axis_index("dp"), lax.axis_index("fsdp")
        self.x, self.c = dp // 2, dp % 2
        self.z, self.y = fs // 2, fs % 2
        x, y, z, c = self.x, self.y, self.z, self.c
        self.sib = self.dev(x, y, z, 1 - c)
        self.xn = self.dev(1 - x, y, z, c)
        self.xn_sib = self.dev(1 - x, y, z, 1 - c)
        self.yn = self.dev(x, 1 - y, z, c)
        self.end = (z == 0) | (z == 3)
        self.mid = (z == 1) | (z == 2)
        self.inner = self.dev(x, y, z + 1 - 2 * (z // 2), c)
        self.outer = self.dev(x, y, (z + 3 + 2 * (z // 2)) % 4, c)
        self.up = self.dev(x, y, (z + 1) % 4, c)
        self.down = self.dev(x, y, (z + 3) % 4, c)
        self.far = self.dev(x, y, (z + 2) % 4, c)

    def dev(self, x, y, z, c):
        return (x * 2 + c, z * 2 + y)

    def mine(self, blocks):
        return blocks[0] if len(blocks) == 1 else blocks[0] + self.x * (blocks[1] - blocks[0])

    def theirs(self, blocks):
        return blocks[1] + self.x * (blocks[0] - blocks[1])


def arrived(ref, sem):
    pltpu.make_async_copy(ref, ref, sem).wait()


def add_into(dst, left, right):
    for row in range(0, dst.shape[-2], 16):
        dst[row : row + 16] = (left[row : row + 16].astype(F32) + right[row : row + 16].astype(F32)).astype(BF)


ROWS, IMAGE = 512, 256
FACTOR = HEAD_DIM**-0.5
LOG2E = 1.4426950408889634


def dot(left, right, over_left=1, over_right=0):
    return lax.dot_general(left, right, (((over_left,), (over_right,)), ((), ())), preferred_element_type=F32)


def matrix(w, j):
    return w[j].reshape(CW, CW)


def down_rows(w, s, first=8):
    return jnp.concatenate([w[first + k, s // 2, s % 2] for k in range(4)], axis=0)


def part(i, rows):
    return pl.ds(pl.multiple_of(i * rows, rows), rows)


def flag_column(flags, fcol):
    spot = lax.broadcasted_iota(jnp.int32, (IMAGE, IMAGE), 0) == lax.broadcasted_iota(jnp.int32, (IMAGE, IMAGE), 1)
    for b in range(2):
        row = jnp.broadcast_to((flags[:, b * IMAGE : (b + 1) * IMAGE] == 1).astype(F32), (8, IMAGE)).astype(BF)
        fcol[b * IMAGE : (b + 1) * IMAGE, :] = dot(spot.astype(F32).astype(BF), row, 1, 1)[:, 0:1]


def vector_tile(vectors, tile):
    tile[...] = jnp.zeros_like(tile)
    tile[0:5, 0:RU] = vectors[...].astype(BF)


def spread(s):
    row = lax.broadcasted_iota(jnp.int32, (128, CW), 0)
    column = lax.broadcasted_iota(jnp.int32, (128, CW), 1)
    return ((row < RU) & (column == row + s * RU)).astype(F32).astype(BF)


def vector_rows(tiles, pv):
    total = dot(tiles[0], spread(0))
    for s in range(1, 8):
        total = total + dot(tiles[s], spread(s))
    pv[...] = total


def hidden_rows(tok, fcol, pv, r):
    return jnp.where(fcol[r, :] > 0.5, pv[4:5, :], tok[r, :].astype(F32))


def norm_one(tok, fcol, pv, e1, i, rows=128):
    for k in range(rows // 64):
        r = pl.ds(pl.multiple_of(i * rows + k * 64, 64), 64)
        n, _ = standardize(hidden_rows(tok, fcol, pv, r))
        e1[r, :] = (n * pv[0:1, :] + pv[1:2, :]).astype(BF)


def project_part(e1, w, proj, j, i):
    r = part(i, 256)
    proj[j, r, :] = dot(e1[r, :], matrix(w, j)).astype(BF)


def head_lanes():
    return [(h * HEAD_DIM, range(h * HEAD_DIM // 128, (h * HEAD_DIM + HEAD_DIM - 1) // 128 + 1)) for h in range(8)]


def lane_mask(first, t):
    lane = lax.broadcasted_iota(jnp.int32, (1, 128), 1) + t * 128
    return ((lane >= first) & (lane < first + HEAD_DIM)).astype(F32).astype(BF)


def attend(proj, att, probs, b, group):
    rows = part(b, IMAGE)

    def lanes(t):
        return slice(group * 384 + t * 128, group * 384 + t * 128 + 128)

    acc = [None] * 3
    for h, (first, tiles) in enumerate(head_lanes()):
        masks = {t: lane_mask(first, t) for t in tiles}
        s = sum(dot(proj[1, rows, lanes(t)], proj[0, rows, lanes(t)] * masks[t], 1, 1) for t in tiles)
        top = jnp.max(s, axis=0, keepdims=True)
        e = jnp.exp2((s - top) * (FACTOR * LOG2E))
        p = (e * (1.0 / jnp.sum(e, axis=0, keepdims=True))).astype(BF)
        probs[2 * b + group, h] = p
        for t in tiles:
            o = dot(p, proj[2, rows, lanes(t)] * masks[t], 0, 0)
            acc[t] = o if acc[t] is None else acc[t] + o
    for t in range(3):
        att[rows, lanes(t)] = acc[t].astype(BF)


def norm_two(tok, fcol, pv, att, w, mid, e2, i):
    r = part(i, 256)
    v = hidden_rows(tok, fcol, pv, r) + dot(att[r, :], matrix(w, 3))
    mid[r, :] = v
    n, _ = standardize(v)
    e2[r, :] = (n * pv[2:3, :] + pv[3:4, :]).astype(BF)


def rise(e2, w, act, dg, k, i, rows=128):
    r = part(i, rows)
    v = dot(e2[r, :], matrix(w, 4 + k))
    cdf = 0.5 * (1.0 + lax.erf(v * 0.7071067811865476))
    act[k, r, :] = (v * cdf).astype(BF)
    dg[k, r, :] = (cdf + v * (jnp.exp2(v * v * (-0.5 * LOG2E)) * 0.3989422804014327)).astype(BF)


def lower(act, w, mid, out, i, first=8):
    r = part(i, 256)
    total = mid[r, :]
    for s in range(8):
        total = total + dot(act[s // 2, r, (s % 2) * 384 : (s % 2) * 384 + 384], down_rows(w, s, first))
    out[r, :] = total.astype(BF)


PLAN_END = []


class Task:
    def __init__(self, name, time, needs, sends=(), rank=0):
        self.name, self.time, self.needs, self.sends, self.rank = name, time, tuple(needs), tuple(sends), rank


def plan(tasks, rates, window, arrive, sent, issue=0.1):
    now = 0.0
    links = {name: dict(active={}, queue=[], over=[], late=[], last=0.0) for name in rates}
    done, left, order, count = {}, list(tasks), [], 0

    def advance(to):
        for name, link in links.items():
            at = link["last"]
            while link["active"]:
                token, rest = next(iter(link["active"].items()))
                end = at + rest / rates[name]
                if end > to + 1e-9:
                    link["active"][token] -= (to - at) * rates[name]
                    at = to
                    break
                del link["active"][token]
                at = end
                done[token] = end + arrive
                link["late"].append((end + sent, token))
            link["last"] = max(at, to)

    while left or any(link["queue"] or link["active"] for link in links.values()):
        advance(now)
        moved = False
        for name, link in links.items():
            link["over"] += [q[1] for q in link["late"] if q[0] <= now]
            link["late"] = [q for q in link["late"] if q[0] > now]
            while link["queue"] and len(link["active"]) + len(link["late"]) < window[name]:
                link["queue"].sort()
                _, _, token, size = link["queue"].pop(0)
                order.append(("issue", token, link["over"]))
                link["over"] = []
                now += issue
                advance(now)
                link["active"][token] = size
                moved = True
        ready = [q for q in left if all(done.get(need, 1e18) <= now for need in q.needs)]
        if ready:
            task = min(ready, key=lambda q: q.rank)
            left.remove(task)
            order.append(("run", task.name))
            now += task.time
            advance(now)
            done[task.name] = now
            for name, size, token, rank in task.sends:
                count += 1
                links[name]["queue"].append((rank, count, token, size))
            moved = True
        if not moved:
            times = [v for v in done.values() if v > now]
            for name, link in links.items():
                times += [q[0] for q in link["late"] if q[0] > now]
                if link["active"]:
                    times.append(link["last"] + next(iter(link["active"].values())) / rates[name])
            now = max(min(times), now) + 1e-6
    PLAN_END.append(now)
    order.append(("waits", [t for link in links.values() for t in link["over"] + [q[1] for q in link["late"]]]))
    return order


ARRIVE, SENT, ISSUE = 1.5, 1.0, 0.06


class Sender:
    def __init__(self, sems, window):
        self.sems, self.queued, self.under_way = sems, {}, {}
        self.free, first = {}, 0
        for name, slots in window.items():
            self.free[name] = list(range(first, first + slots))
            first += slots

    def put(self, token, link, src, dst, sem, to, cond=None):
        self.queued[token] = (link, src, dst, sem, to, cond)

    def issue(self, token, over):
        self.wait(over)
        link, src, dst, sem, to, cond = self.queued.pop(token)
        slot = self.free[link].pop(0)
        copy = pltpu.make_async_remote_copy(
            src_ref=src, dst_ref=dst, send_sem=self.sems.at[slot], recv_sem=sem, device_id=to, device_id_type=MESH
        )
        if cond is None:
            copy.start()
        else:
            pl.when(cond)(copy.start)
        self.under_way[token] = (link, slot, copy, cond)

    def wait(self, tokens):
        for token in tokens:
            link, slot, copy, cond = self.under_way.pop(token)
            self.free[link].append(slot)
            if cond is None:
                copy.wait_send()
            else:
                pl.when(cond)(copy.wait_send)


def grad_out_rows(cot, fcol, counts, r, b):
    weight = float(IMAGE) / jnp.full((1, 1), counts[b], jnp.int32).astype(F32)
    return cot[r, :].astype(F32) * (fcol[r, :] * weight)


def grad_low_part(cot, fcol, counts, gl, b):
    for k in range(4):
        r = pl.ds(b * IMAGE + k * 64, 64)
        gl[r, :] = grad_out_rows(cot, fcol, counts, r, b).astype(BF)


def grad_down_part(act, gl, g, s):
    d = dot(act[s // 2, :, (s % 2) * 384 : (s % 2) * 384 + 384], gl[...], 0, 0).astype(BF)
    for k in range(4):
        g[k, s // 2, s % 2] = d[k * RU : (k + 1) * RU]


def grad_rising_part(gl, w, dg, s):
    lanes = slice((s % 2) * 384, (s % 2) * 384 + 384)
    grad = dot(gl[...], down_rows(w, s, 0), 1, 1)
    dg[s // 2, :, lanes] = (grad * dg[s // 2, :, lanes].astype(F32)).astype(BF)


def weight_grad_part(left, right, g, j, i):
    d = dot(left[:, i * 384 : i * 384 + 384], right[...], 0, 0).astype(BF)
    g[j, 2 * i : 2 * i + 2] = d.reshape(2, 2, RU, CW)


def norm_back_rows(grad, n, inverse, gain):
    scaled = grad * gain
    first = jnp.mean(scaled, axis=-1, keepdims=True)
    second = jnp.mean(scaled * n, axis=-1, keepdims=True)
    return inverse * (scaled - first - n * second)


def row_sum(values):
    return jnp.sum(values, axis=0, keepdims=True)


def back_two_part(gr, w, mid, pv, cot, fcol, counts, gm, ml, vec, i, rows=128):
    r = part(i, rows)
    grad = sum(dot(gr[k, r, :], matrix(w, k), 1, 1) for k in range(4))
    n, inverse = standardize(mid[r, :])
    total = grad_out_rows(cot, fcol, counts, r, i * rows // IMAGE) + norm_back_rows(grad, n, inverse, pv[2:3, :])
    gm[r, :] = total
    ml[r, :] = total.astype(BF)
    vec[0, 2:3, :] += row_sum(grad * n)
    vec[0, 3:4, :] += row_sum(grad)


def grad_attended_part(ml, w, ga, i):
    r = part(i, 256)
    ga[r, :] = dot(ml[r, :], matrix(w, 4), 1, 1).astype(BF)


def attend_back(proj, probs, ga, dproj, b, group):
    rows = part(b, IMAGE)

    def lanes(t):
        return slice(group * 384 + t * 128, group * 384 + t * 128 + 128)

    acc = [[None] * 3 for _ in range(3)]

    def add(k, t, value):
        acc[k][t] = value if acc[k][t] is None else acc[k][t] + value

    for h, (first, tiles) in enumerate(head_lanes()):
        masks = {t: lane_mask(first, t) for t in tiles}
        low = probs[2 * b + group, h]
        grad = sum(dot(proj[2, rows, lanes(t)], ga[rows, lanes(t)] * masks[t], 1, 1) for t in tiles)
        p = low.astype(F32)
        delta = jnp.sum(grad * p, axis=0, keepdims=True)
        raw = (p * ((grad - delta) * FACTOR)).astype(BF)
        for t in tiles:
            add(0, t, dot(raw, proj[1, rows, lanes(t)] * masks[t], 0, 0))
            add(1, t, dot(raw, proj[0, rows, lanes(t)] * masks[t]))
            add(2, t, dot(low, ga[rows, lanes(t)] * masks[t]))
    for k in range(3):
        for t in range(3):
            dproj[k, rows, lanes(t)] = acc[k][t].astype(BF)


def back_one_part(dproj, w, tok, fcol, pv, gm, tg, vec, i, rows=128):
    r = part(i, rows)
    grad = sum(dot(dproj[k, r, :], matrix(w, k), 1, 1) for k in range(3))
    n, inverse = standardize(hidden_rows(tok, fcol, pv, r))
    total = norm_back_rows(grad, n, inverse, pv[0:1, :]) + gm[r, :]
    on = fcol[r, :] > 0.5
    tg[r, :] = jnp.where(on, 0.0, total).astype(BF)
    vec[0, 0:1, :] += row_sum(grad * n)
    vec[0, 1:2, :] += row_sum(grad)
    vec[0, 4:5, :] += row_sum(jnp.where(on, total, 0.0))


class Gatherer:
    def __init__(self, at, items, w, sender, cast, zs, ys, xs, cs):
        self.at, self.items, self.w, self.sender, self.cast = at, items, w, sender, cast
        self.zs, self.ys, self.xs, self.cs = zs, ys, xs, cs
        self.others = [((at.z + dz) % 4, (at.y + dy) % 2) for dz in range(4) for dy in range(2) if dz + dy > 0]

    def run(self, op, i):
        at, z, y = self.at, self.at.z, self.at.y
        blocks, y_first, first, count = self.items[i]
        pair, j = len(blocks) == 2, at.mine(blocks)
        rows = pl.ds(pl.multiple_of(at.c * H + first, 16), count)
        sib_rows = pl.ds(pl.multiple_of((1 - at.c) * H + first, 16), count)

        def send(name, link, p, sem, to, cond=None):
            self.sender.put((name, i), link, p, p, sem, to, cond)

        def share(k, t):
            send("c%d" % k, "c", self.w.at[t, :, :, rows, :], self.cs.at[i, k], at.sib)

        def start_z(p):
            send("u0", "u", p, self.zs.at[i, 0, 0], at.up, z < 3)
            send("d0", "d", p, self.zs.at[i, 0, 1], at.down, z > 0)

        if op == "S":
            for t in blocks:
                self.cast(t, first, count)
            p = self.w.at[j, z, y, rows, :]
            send("yo", "y", p, self.ys.at[i, z], at.yn)
            if not y_first:
                start_z(p)
        elif op == "Y":
            p = self.w.at[j, z, 1 - y, rows, :]
            arrived(p, self.ys.at[i, z])
            start_z(self.w.at[j, z, :, rows, :])
            if pair:
                send("xq", "x", p, self.xs.at[i, z], at.xn)
        elif op[0] == "P":
            d = int(op[1])
            for way in (0, 1):
                has = (z - d - 1 >= 0) if way == 0 else (z + d + 1 <= 3)
                zz = jnp.maximum(z - d - 1, 0) if way == 0 else jnp.minimum(z + d + 1, 3)
                p = self.w.at[j, zz, :, rows, :] if y_first else self.w.at[j, zz, y, rows, :]
                pl.when(has)(functools.partial(arrived, p, self.zs.at[i, d, way]))
                if d < 2 and way == 0:
                    send("u%d" % (d + 1), "u", p, self.zs.at[i, d + 1, 0], at.up, has & (z < 3))
                if d < 2 and way == 1:
                    send("d%d" % (d + 1), "d", p, self.zs.at[i, d + 1, 1], at.down, has & (z > 0))
                name = "ab"[way] + op[1]
                if not y_first:
                    send("y" + name, "y", p, self.ys.at[i, zz], at.yn, has)
                if pair:
                    send("x" + name, "x", p, self.xs.at[i, zz], at.xn, has)
            if y_first and d == 2:
                share(0, j)
        elif op == "Q":
            for zz in range(4):
                arrived(self.w.at[j, zz, 1 - y, rows, :], self.ys.at[i, zz])
            if pair:
                send("xq", "x", self.w.at[j, :, 1 - y, rows, :], self.xs.at[i, 4], at.xn)
            share(0, j)
        elif op == "X":
            t = at.theirs(blocks)
            for dz in (1, 2, 3):
                zz = (z + dz) % 4
                p = self.w.at[t, zz, :, rows, :] if y_first else self.w.at[t, zz, y, rows, :]
                arrived(p, self.xs.at[i, zz])
            if y_first:
                arrived(self.w.at[t, z, 1 - y, rows, :], self.xs.at[i, z])
            else:
                arrived(self.w.at[t, :, 1 - y, rows, :], self.xs.at[i, 4])
            share(1, t)
        else:
            for k, t in enumerate((j, at.theirs(blocks)) if pair else (j,)):
                arrived(self.w.at[t, :, :, sib_rows, :], self.cs.at[i, k])


def gather_items():
    return [
        (blocks, y_first, k * (H // parts), H // parts) for blocks, parts, y_first in GATHER_ITEMS for k in range(parts)
    ]


def gather_tasks(items):
    tasks, there = [], [[] for _ in range(BLOCKS)]
    for i, (blocks, y_first, _, rows) in enumerate(items):
        pair, size = len(blocks) == 2, rows * CW * 2
        wide = size * (2 if y_first else 1)
        to_z = [("u", wide, ("u0", i), i), ("d", wide, ("d0", i), i)]
        to_sib = [("c", 8 * size, ("c0", i), i)]
        tasks.append(Task(("S", i), 0.15 * len(blocks), [], [("y", size, ("yo", i), i)] + ([] if y_first else to_z), i))
        if y_first:
            to_x = [("x", size, ("xq", i), i)] if pair else []
            tasks.append(Task(("Y", i), 0.05, [("yo", i)], to_z + to_x, i))
        across, handed = [("yo", i)], [("xq", i)]
        for d, part_of in enumerate((0.75, 0.5, 0.25)):
            sends = []
            for way in "ab":
                if d < 2:
                    name = "ud"[way == "b"] + str(d + 1)
                    sends.append((name[0], wide, (name, i), i))
                if not y_first:
                    sends.append(("y", part_of * size, ("y%s%d" % (way, d), i), i))
                    across.append(("y%s%d" % (way, d), i))
                if pair:
                    sends.append(("x", part_of * wide, ("x%s%d" % (way, d), i), i))
                    handed.append(("x%s%d" % (way, d), i))
            if y_first and d == 2:
                sends += to_sib
            tasks.append(Task(("P%d" % d, i), 0.1, [("u%d" % d, i), ("d%d" % d, i)], sends, i))
        if not y_first:
            to_x = [("x", 4 * size, ("xq", i), i)] if pair else []
            tasks.append(Task(("Q", i), 0.1, across, to_x + to_sib, i))
        if pair:
            tasks.append(Task(("X", i), 0.1, handed, [("c", 8 * size, ("c1", i), i)], i))
        tasks.append(Task(("C", i), 0.1, [("c%d" % k, i) for k in range(len(blocks))], [], i))
        for j in blocks:
            there[j].append(("C", i))
    return tasks, there


def forward_kernel(
    items, order,
    w_qkv, w_out, w_up, w_down, vectors, tok, flags, counts, cot,
    w_h, pv_h, e1_h, proj_h, probs_h, att_h, mid_h, e2_h, act_h, dg_h, gl_h, gd_h,
    w, own, tile, tiles, pv, fcol, e1, proj, probs, att, mid, e2, act, dg, gl, gd, zs, ys, xs, cs, vs, save_sem, tile_sem, own_sem, send_sem,
):
    at = Place()
    fs = at.z * 2 + at.y
    sender = Sender(send_sem, GATHER_WINDOW)
    loads = []
    mine = pl.ds(pl.multiple_of(at.c * H, H), H)
    parts = [(w_qkv.at[mine, pl.ds(k * CW, CW)]) for k in range(3)] + [w_out.at[mine, :]]
    parts += [w_up.at[mine, pl.ds(k * CW, CW)] for k in range(4)]
    parts += [w_down.at[pl.ds(pl.multiple_of(k * RU + at.c * H, H), H), :] for k in range(4)]
    for blocks, _, _ in GATHER_ITEMS:
        for j in blocks:
            loads.append(pltpu.make_async_copy(parts[j], own.at[j], own_sem.at[j]))
            loads[-1].start()
    order_of = [j for blocks, _, _ in GATHER_ITEMS for j in blocks]

    def cast(j, first, count):
        k = order_of.index(j)
        if loads[k] is not None:
            loads[k].wait()
            loads[k] = None
        rows = pl.ds(pl.multiple_of(at.c * H + first, 16), count)
        w[j, at.z, at.y, rows, :] = own[j, first : first + count, :].astype(BF)

    comm = Gatherer(at, items, w, sender, cast, zs, ys, xs, cs)
    barrier = pltpu.get_barrier_semaphore()
    peers = [at.sib, at.xn] + [at.dev(at.x, yy, zz, at.c) for zz, yy in comm.others]
    for peer in peers:
        pl.semaphore_signal(barrier, inc=1, device_id=peer, device_id_type=MESH)
    vector_tile(vectors, tile)
    tiles[fs] = tile[...]
    pl.semaphore_wait(barrier, len(peers))
    tile_sends = [
        pltpu.make_async_remote_copy(
            src_ref=tile, dst_ref=tiles.at[fs], send_sem=tile_sem.at[k], recv_sem=vs.at[fs],
            device_id=at.dev(at.x, yy, zz, at.c), device_id_type=MESH,
        )
        for k, (zz, yy) in enumerate(comm.others)
    ]
    for copy in tile_sends:
        copy.start()
    saves = []

    def save(src, dst):
        copy = pltpu.make_async_copy(src, dst, save_sem.at[len(saves)])
        copy.start()
        saves.append(copy)

    def vectors_in():
        for zz, yy in comm.others:
            arrived(tiles.at[zz * 2 + yy], vs.at[zz * 2 + yy])
        vector_rows(tiles, pv)
        save(pv, pv_h)

    def compute(op, *k):
        if op == "flags":
            flag_column(flags, fcol)
        elif op == "vectors":
            vectors_in()
        elif op == "one":
            norm_one(tok, fcol, pv, e1, *k)
        elif op == "project":
            project_part(e1, w, proj, *k)
        elif op == "attend":
            attend(proj, att, probs, *k)
        elif op == "two":
            norm_two(tok, fcol, pv, att, w, mid, e2, *k)
        elif op == "rise":
            rise(e2, w, act, dg, *k)
        elif op == "low":
            grad_low_part(cot, fcol, counts, gl, *k)
        elif op == "down":
            grad_down_part(act, gl, gd, *k)
        elif op == "whole":
            save(w.at[k[0]], w_h.at[k[0]])
        else:
            j = k[0]
            refs = dict(e1=(e1, e1_h), proj=(proj, proj_h), probs=(probs, probs_h), att=(att, att_h), mid=(mid, mid_h))
            refs.update(e2=(e2, e2_h), gl=(gl, gl_h), gd=(gd.at[j], gd_h.at[j]), act=(act.at[j], act_h.at[j]), dg=(dg.at[j], dg_h.at[j]))
            save(*refs[op[5:]])

    for entry in order:
        if entry[0] == "issue":
            sender.issue(entry[1], entry[2])
        elif entry[0] == "waits":
            sender.wait(entry[1])
        elif entry[1][0][0].isupper():
            comm.run(*entry[1])
        else:
            compute(*entry[1])
    for copy in tile_sends:
        copy.wait_send()
    for copy in saves:
        copy.wait()


def forward_tasks(there):
    rows = [(("flags",), 0.3, []), (("vectors",), 0.8, [("u0", 1)])]
    rows += [(("one", i), 0.5, [("vectors",)]) for i in range(4)]
    rows += [(("low", b), 0.5, [("flags",)]) for b in range(2)]
    lows = [("low", b) for b in range(2)]
    ones = [("one", i) for i in range(4)] + [("flags",)]
    rows += [(("project", j, i), 0.55, there[j] + ones) for j in range(3) for i in range(2)]
    projected = [("project", j, i) for j in range(3) for i in range(2)]
    rows += [(("attend", b, k), 2.4, projected) for b in range(2) for k in range(2)]
    rows += [(("two", b), 1.2, there[3] + [("attend", b, k) for k in range(2)]) for b in range(2)]
    rows += [(("rise", k, i), 0.35, there[4 + k] + [("two", i // 2)]) for k in range(4) for i in range(4)]
    rows += [(("down", s), 0.45, lows + [("rise", s // 2, i) for i in range(4)]) for s in range(8)]
    two = [("two", b) for b in range(2)]
    heads = [("attend", b, k) for b in range(2) for k in range(2)]
    rows += [(("whole", j), 0.05, there[j]) for j in range(BLOCKS)]
    rows += [(("save e1", 0), 0.05, ones), (("save proj", 0), 0.05, projected), (("save probs", 0), 0.05, heads)]
    rows += [(("save att", 0), 0.05, heads), (("save mid", 0), 0.05, two), (("save e2", 0), 0.05, two)]
    for k in range(4):
        rows += [(("save " + n, k), 0.05, [("rise", k, i) for i in range(4)]) for n in ("act", "dg")]
    rows += [(("save gl", 0), 0.05, lows)]
    rows += [(("save gd", k), 0.05, [("down", s) for s in range(8)]) for k in range(4)]
    return [Task(name, time, needs, (), 1000 + k) for k, (name, time, needs) in enumerate(rows)]


def forward(w_qkv, w_out, w_up, w_down, vectors, tokens, flags, counts, cotangent):
    items = gather_items()
    n = len(items)
    tasks, there = gather_tasks(items)
    order = plan(tasks + forward_tasks(there), GATHER_RATES, GATHER_WINDOW, ARRIVE, SENT, GATHER_ISSUE)
    vmem, anywhere = pl.BlockSpec(memory_space=pltpu.VMEM), pl.BlockSpec(memory_space=pl.ANY)
    dma = pltpu.SemaphoreType.DMA
    whole, three, four = (ROWS, CW), (3, ROWS, CW), (4, ROWS, CW)
    shapes = [
        ((BLOCKS, 4, 2, RU, CW), BF), ((16, CW), F32), (whole, BF), (three, BF), ((4, 8, IMAGE, IMAGE), BF), (whole, BF), (whole, F32),
        (whole, BF), (four, BF), (four, BF), (whole, BF), ((4, 4, 2, RU, CW), BF),
    ]
    return pl.pallas_call(
        functools.partial(forward_kernel, items, order),
        out_shape=[jax.ShapeDtypeStruct(s, t) for s, t in shapes],
        in_specs=[anywhere] * 4 + [vmem] * 3 + [pl.BlockSpec(memory_space=pltpu.SMEM), vmem],
        out_specs=[anywhere] * len(shapes),
        scratch_shapes=[
            pltpu.VMEM((BLOCKS, 4, 2, RU, CW), BF),
            pltpu.VMEM((BLOCKS, H, CW), F32),
            pltpu.VMEM((16, 128), BF),
            pltpu.VMEM((8, 16, 128), BF),
            pltpu.VMEM((16, CW), F32),
            pltpu.VMEM((ROWS, 1), F32),
            pltpu.VMEM(whole, BF),
            pltpu.VMEM(three, BF),
            pltpu.VMEM((4, 8, IMAGE, IMAGE), BF),
            pltpu.VMEM(whole, BF),
            pltpu.VMEM(whole, F32),
            pltpu.VMEM(whole, BF),
            pltpu.VMEM(four, BF),
            pltpu.VMEM(four, BF),
            pltpu.VMEM(whole, BF),
            pltpu.VMEM((4, 4, 2, RU, CW), BF),
            dma((n, 3, 2)),
            dma((n, 4)),
            dma((n, 5)),
            dma((n, 2)),
            dma((8,)),
            dma((32,)),
            dma((8,)),
            dma((BLOCKS,)),
            dma((sum(GATHER_WINDOW.values()),)),
        ],
        compiler_params=pltpu.CompilerParams(collective_id=0, has_side_effects=True, vmem_limit_bytes=VMEM_LIMIT),
        name="forward",
    )(w_qkv, w_out, w_up, w_down, vectors, tokens, flags, counts, cotangent)


RATES = dict(c=350e3, x=45e3, y=45e3, z=45e3, w=45e3, v=45e3)
WINDOW = dict(c=8, x=8, y=3, z=4, w=6, v=3)
REDUCE_ITEMS = (
    ((2,), 3, False), ((11,), 1, False), ((7, 4), 3, False), ((5, 8), 1, False), ((3,), 1, False), ((10,), 1, True),
    ((9,), 1, False), ((1, 0), 3, True), ((6,), 1, False),
)
HALVES = 1
COMPUTE_RANK = 1000
SLOT = {blocks: k for k, (blocks, _, _) in enumerate(REDUCE_ITEMS)}
PAIR_SLOT = {blocks: k for k, blocks in enumerate(b for b, _, _ in REDUCE_ITEMS if len(b) == 2)}


def reduce_items():
    return [(blocks, direct, k * (H // parts), H // parts) for blocks, parts, direct in REDUCE_ITEMS for k in range(parts)]


def reduce_tasks(items, made):
    tasks = []
    for i, (blocks, direct, _, rows) in enumerate(items):
        pair, size, add = len(blocks) == 2, rows * CW * 2, 0.04 * rows / H
        needs = [token for j in blocks for token in made[j]]
        to_sib = [("c", 8 * size, ("mine", i), i)]
        halves = range(HALVES)
        to_y = [("y", 4 // HALVES * size, ("y%d" % q, i), i) for q in halves]
        if pair:
            to_x = [("x", 8 // HALVES * size, ("x%d" % q, i), i) for q in halves]
            tasks.append(Task(("A", i), 0.05, needs, [("c", 8 * size, ("theirs", i), i)] + to_sib, i))
            tasks.append(Task(("Bt", i), 8 * add, [("theirs", i)], to_x, i))
            tasks.append(Task(("Bm", i), 8 * add, [("mine", i)], [], i))
            tasks.append(Task(("C", i), 8 * add, [("x%d" % q, i) for q in halves] + [("Bm", i)], to_y, i))
        else:
            tasks.append(Task(("A", i), 0.05, needs, to_sib, i))
            tasks.append(Task(("Bm", i), 8 * add, [("mine", i)], to_y, i))
        tasks.append(Task(("D", i), 4 * add, [("y%d" % q, i) for q in halves], [("z", 3 * size, ("za", i), i)], i))
        tasks.append(Task(("E1", i), 3 * add, [("za", i)], [("w", 2 * size, ("zb", i), i - 50)], i))
        tasks.append(Task(("E2", i), 2 * add, [("zb", i)], [("v", size, ("zc", i), i - 50)], i))
        finals = [("x", size, ("xf", i), i - 100)]
        if direct:
            finals += [("x", size, ("xd", i), i - 100), ("c", size, ("cf", i), i - 100)]
        tasks.append(Task(("E3", i), add, [("zc", i)], finals, i))
        if direct:
            tasks.append(Task(("L", i), 4 * add, [("xf", i), ("xd", i), ("cf", i)], [], i))
            continue
        finals = [("f%d" % k, i) for k in range(len(blocks))]
        tasks.append(Task(("G", i), 2 * add, [("xf", i)], [("c", size, f, i) for f in finals], i))
        tasks.append(Task(("H", i), 0.05, finals, [], i))
    return tasks


def vector_tasks(made):
    size = 8 * CW * 4
    return [
        Task(("V0", 0), 0.05, made, [("c", size, ("vc", 0), -200)], -200),
        Task(("V1", 0), 0.05, [("vc", 0)], [("x", size, ("vx", 0), -200)], -200),
        Task(("V2", 0), 0.05, [("vx", 0)], [("y", size, ("vy", 0), -200)], -200),
        Task(("V3", 0), 0.05, [("vy", 0)], [("z", size, ("vz%d" % d, 0), -200) for d in (1, 2, 3)], -200),
        Task(("V4", 0), 0.05, [("vz%d" % d, 0) for d in (1, 2, 3)], [], -200),
    ]


class Reducer:
    def __init__(self, at, items, sender, g, fin, sr, xr, yr, zr, xf, xd, cf, vec, vr, sems):
        self.at, self.items, self.sender = at, items, sender
        self.g, self.fin, self.sr, self.xr, self.yr, self.zr, self.xf = g, fin, sr, xr, yr, zr, xf
        self.xd, self.cf = xd, cf
        self.vec, self.vr = vec, vr
        self.ssem, self.xsem, self.ysem, self.zsem, self.xfsem, self.fsem, self.vsem = sems

    def run(self, op, i):
        if op[0] == "V":
            return self.vectors(op)
        at, g, y, z = self.at, self.g, self.at.y, self.at.z
        blocks, direct, first, count = self.items[i]
        pair, key, m = len(blocks) == 2, SLOT[blocks], self.at.mine(blocks)
        xkey = PAIR_SLOT.get(blocks)
        loc = pl.ds(first, count)
        own_rows = pl.ds(pl.multiple_of(at.c * H + first, 16), count)
        sib_rows = pl.ds(pl.multiple_of((1 - at.c) * H + first, 16), count)

        def add_shards(j, src):
            def body(k, _):
                d = g.at[j, k // 2, k % 2, own_rows, :]
                add_into(d, d, src.at[k // 2, k % 2, loc, :])
                return 0

            lax.fori_loop(0, 8, body, 0)

        def to_y():
            for q in range(HALVES):
                two = pl.ds(4 // HALVES * q, 4 // HALVES)
                self.sender.put(
                    ("y%d" % q, i), "y", g.at[m, two, 1 - y, own_rows, :], self.yr.at[key, two, loc, :],
                    self.ysem.at[i, q], at.yn,
                )

        if op == "A":
            if pair:
                t = at.theirs(blocks)
                self.sender.put(
                    ("theirs", i), "c", g.at[t, :, :, sib_rows, :], self.sr.at[t, :, :, loc, :], self.ssem.at[i, 1], at.sib
                )
            self.sender.put(
                ("mine", i), "c", g.at[m, :, :, sib_rows, :], self.sr.at[m, :, :, loc, :], self.ssem.at[i, 0], at.sib
            )
        elif op == "Bm":
            arrived(self.sr.at[m, :, :, loc, :], self.ssem.at[i, 0])
            add_shards(m, self.sr.at[m])
            if not pair:
                to_y()
        elif op == "Bt":
            t = at.theirs(blocks)
            arrived(self.sr.at[t, :, :, loc, :], self.ssem.at[i, 1])
            add_shards(t, self.sr.at[t])
            for q in range(HALVES):
                two = pl.ds(4 // HALVES * q, 4 // HALVES)
                self.sender.put(
                    ("x%d" % q, i), "x", g.at[t, two, :, own_rows, :], self.xr.at[xkey, two, :, loc, :],
                    self.xsem.at[i, q], at.xn,
                )
        elif op == "C":
            for q in range(HALVES):
                arrived(self.xr.at[xkey, pl.ds(4 // HALVES * q, 4 // HALVES), :, loc, :], self.xsem.at[i, q])
            add_shards(m, self.xr.at[xkey])
            to_y()
        elif op == "D":
            for q in range(HALVES):
                arrived(self.yr.at[key, pl.ds(4 // HALVES * q, 4 // HALVES), loc, :], self.ysem.at[i, q])

            def body(k, _):
                d = g.at[m, k, y, own_rows, :]
                add_into(d, d, self.yr.at[key, k, loc, :])
                return 0

            lax.fori_loop(0, 4, body, 0)
            self.sender.put(
                ("za", i), "z", g.at[m, pl.ds(1 - z // 3, 3), y, own_rows, :], self.zr.at[key, pl.ds(0, 3), loc, :],
                self.zsem.at[i, 0], at.inner, at.end,
            )
        elif op == "L":
            for buffer, sem in ((self.xf, self.xfsem.at[i]), (self.xd, self.fsem.at[i, 0]), (self.cf, self.fsem.at[i, 1])):
                arrived(buffer.at[key, loc, :], sem)
            mine = g.at[m, z, y, own_rows, :]
            if pair:
                t = at.theirs(blocks)
                self.fin[m, own_rows, :] = mine[...]
                self.fin[m, sib_rows, :] = self.cf[key, loc, :]
                self.fin[t, own_rows, :] = self.xf[key, loc, :]
                self.fin[t, sib_rows, :] = self.xd[key, loc, :]
            else:
                add_into(self.fin.at[m, own_rows, :], mine, self.xf.at[key, loc, :])
                add_into(self.fin.at[m, sib_rows, :], self.cf.at[key, loc, :], self.xd.at[key, loc, :])
        elif op == "E1":

            @pl.when(at.mid)
            def _():
                arrived(self.zr.at[key, pl.ds(0, 3), loc, :], self.zsem.at[i, 0])
                for k in range(3):
                    d = g.at[m, 2 - z + k, y, own_rows, :]
                    add_into(d, d, self.zr.at[key, k, loc, :])

            self.sender.put(
                ("zb", i), "w", g.at[m, pl.ds(2 * (2 - z), 2), y, own_rows, :], self.zr.at[key, pl.ds(3, 2), loc, :],
                self.zsem.at[i, 1], at.inner, at.mid,
            )
        elif op == "E2":

            @pl.when(at.mid)
            def _():
                arrived(self.zr.at[key, pl.ds(3, 2), loc, :], self.zsem.at[i, 1])
                for k in range(2):
                    d = g.at[m, 2 * (z - 1) + k, y, own_rows, :]
                    add_into(d, d, self.zr.at[key, 3 + k, loc, :])

            self.sender.put(
                ("zc", i), "v", g.at[m, 3 * (z - 1), y, own_rows, :], self.zr.at[key, 0, loc, :],
                self.zsem.at[i, 2], at.outer, at.mid,
            )
        elif op == "E3":
            d = g.at[m, z, y, own_rows, :]

            @pl.when(at.end)
            def _():
                arrived(self.zr.at[key, 0, loc, :], self.zsem.at[i, 2])
                add_into(d, d, self.zr.at[key, 0, loc, :])

            self.sender.put(("xf", i), "x", d, self.xf.at[key, loc, :], self.xfsem.at[i], at.xn)
            if direct:
                self.sender.put(("xd", i), "x", d, self.xd.at[key, loc, :], self.fsem.at[i, 0], at.xn_sib)
                self.sender.put(("cf", i), "c", d, self.cf.at[key, loc, :], self.fsem.at[i, 1], at.sib)
        elif op == "G":
            arrived(self.xf.at[key, loc, :], self.xfsem.at[i])
            d = g.at[m, z, y, own_rows, :]
            if pair:
                self.fin[m, own_rows, :] = d[...]
                self.fin[at.theirs(blocks), own_rows, :] = self.xf[key, loc, :]
            else:
                add_into(self.fin.at[m, own_rows, :], d, self.xf.at[key, loc, :])
            for k, j in enumerate((m, at.theirs(blocks)) if pair else blocks):
                f = self.fin.at[j, own_rows, :]
                self.sender.put(("f%d" % k, i), "c", f, f, self.fsem.at[i, k], at.sib)
        elif op == "H":
            for k, j in enumerate((m, at.theirs(blocks)) if pair else blocks):
                arrived(self.fin.at[j, sib_rows, :], self.fsem.at[i, k])

    def vectors(self, op):
        at, vec, vr, vsem = self.at, self.vec, self.vr, self.vsem
        if op == "V0":
            self.sender.put(("vc", 0), "c", vec.at[0], vr.at[0], vsem.at[0], at.sib)
        elif op == "V1":
            arrived(vr.at[0], vsem.at[0])
            vec[1] = vec[0] + vr[0]
            self.sender.put(("vx", 0), "x", vec.at[1], vr.at[1], vsem.at[1], at.xn)
        elif op == "V2":
            arrived(vr.at[1], vsem.at[1])
            vec[2] = vec[1] + vr[1]
            self.sender.put(("vy", 0), "y", vec.at[2], vr.at[2], vsem.at[2], at.yn)
        elif op == "V3":
            arrived(vr.at[2], vsem.at[2])
            vec[3] = vec[2] + vr[2]
            vr[3 + at.z] = vec[3]
            for d, to in ((1, at.up), (2, at.far), (3, at.down)):
                self.sender.put(("vz%d" % d, 0), "z", vec.at[3], vr.at[3 + at.z], vsem.at[3 + at.z], to)
        else:
            for d in (1, 2, 3):
                arrived(vr.at[3 + (at.z + d) % 4], vsem.at[3 + (at.z + d) % 4])
            vec[4] = ((vr[3] + vr[4]) + vr[5]) + vr[6]


def reduce_barrier(at):
    barrier = pltpu.get_barrier_semaphore()
    peers = [at.sib, at.xn, at.xn_sib, at.yn, at.up, at.far, at.down]
    for peer in peers:
        pl.semaphore_signal(barrier, inc=1, device_id=peer, device_id_type=MESH)
    pl.semaphore_wait(barrier, len(peers))


def reduce_scratch(n):
    dma = pltpu.SemaphoreType.DMA
    return [
        pltpu.VMEM((BLOCKS, 4, 2, H, CW), BF),
        pltpu.VMEM((len(PAIR_SLOT), 4, 2, H, CW), BF),
        pltpu.VMEM((len(SLOT), 4, H, CW), BF),
        pltpu.VMEM((len(SLOT), 5, H, CW), BF),
        pltpu.VMEM((len(SLOT), H, CW), BF),
        pltpu.VMEM((len(SLOT), H, CW), BF),
        pltpu.VMEM((len(SLOT), H, CW), BF),
        pltpu.VMEM((5, 8, CW), F32),
        pltpu.VMEM((7, 8, CW), F32),
        dma((n, 2)),
        dma((n, 2)),
        dma((n, 2)),
        dma((n, 3)),
        dma((n,)),
        dma((n, 2)),
        dma((7,)),
        dma((sum(WINDOW.values()),)),
    ]


LOADS = ("g0", "g1", "g2", "g3", "gl", "dg", "d0", "d1", "d2", "d3", "e2", "mid", "cot", "out", "att", "proj", "probs", "e1", "tok")


def backward_tasks():
    rows = [(("gd", k), 0.02, []) for k in range(4)]
    rows += [(("gr", s), 0.6, []) for s in range(8)]
    rows += [(("gu", k, i), 0.6, [("gr", 2 * k), ("gr", 2 * k + 1)]) for k in range(4) for i in range(2)]
    rows += [(("b2", b), 2.4, [("gr", s) for s in range(8)]) for b in range(2)]
    two = [("b2", b) for b in range(2)]
    rows += [(("go", i), 0.75, two) for i in range(2)]
    rows += [(("ga", b), 0.75, [("b2", b)]) for b in range(2)]
    rows += [(("ab", b, k), 3.4, [("ga", b)]) for b in range(2) for k in range(2)]
    heads = [("ab", b, k) for b in range(2) for k in range(2)]
    rows += [(("gq", j, i), 0.7, heads) for j in range(3) for i in range(2)]
    rows += [(("b1", b), 2.1, heads) for b in range(2)]
    made = [[("gq", j, i) for i in range(2)] for j in range(3)]
    made += [[("go", i) for i in range(2)]]
    made += [[("gu", k, i) for i in range(2)] for k in range(4)]
    made += [[("gd", k)] for k in range(4)]
    last = [("b1", b) for b in range(2)] + [("gq", j, i) for j in range(3) for i in range(2)]
    rows += [(("la",), 0.1, last)] + [(("lo", b), 2.0, [("la",)]) for b in range(2)]
    tasks = [Task(name, time, needs, (), COMPUTE_RANK + 0.001 * k) for k, (name, time, needs) in enumerate(rows)]
    return tasks, made, [("b1", b) for b in range(2)]


def backward_kernel(
    items, order,
    flags, counts, pv, act_h, cot_h, dg_h, gl_h, gd_h, w_h, e2_h, mid_h, att_h, proj_h, probs_h, e1_h, tok_h,
    lo_h, tg_h, fin, vec_out,
    act, cot, dg, w, e2, mid, att, proj, probs, e1, tok, fcol, gl, gm, ml, g, load_sem, out_sem, *reduce_refs,
):
    at = Place()
    source = dict(gl=gl_h, cot=cot_h, dg=dg_h, e2=e2_h, mid=mid_h, att=att_h, proj=proj_h, probs=probs_h, e1=e1_h, tok=tok_h)
    target = dict(gl=gl, cot=cot, dg=dg, e2=e2, mid=mid, att=att, proj=proj, probs=probs, e1=e1, tok=tok)
    loads = {}

    def load(name, src, dst):
        loads[name] = pltpu.make_async_copy(src, dst, load_sem.at[len(loads)])
        loads[name].start()

    def need(*names):
        for name in names:
            if loads[name] is not None:
                loads[name].wait()
                loads[name] = None

    for name in LOADS:
        if name in source:
            load(name, source[name], target[name])
        elif name == "out":
            load(name, w_h.at[3], w.at[4])
        elif name[0] == "g":
            load(name, gd_h.at[int(name[1])], g.at[8 + int(name[1])])
        else:
            load(name, w_h.at[8 + int(name[1])], w.at[int(name[1])])
    vec = reduce_refs[7]
    vec[0] = jnp.zeros((8, CW), F32)
    flag_column(flags, fcol)
    reduce_barrier(at)
    sender = Sender(reduce_refs[-1], WINDOW)
    steps = Reducer(at, items, sender, g, fin, *reduce_refs[:9], reduce_refs[9:16])
    dproj, ga, tg, lo = act, gl, ml, gl

    def compute(op, *k):
        if op == "gd":
            need("g%d" % k)
        elif op == "gr":
            need("gl", "dg", "d0", "d1", "d2", "d3")
            grad_rising_part(gl, w, dg, *k)
            if k[0] == 7:
                for j in range(4):
                    load("u%d" % j, w_h.at[4 + j], w.at[j])
        elif op == "gu":
            need("e2")
            weight_grad_part(e2, dg.at[k[0]], g, 4 + k[0], k[1])
        elif op == "b2":
            need("mid", "cot", "u0", "u1", "u2", "u3")
            back_two_part(dg, w, mid, pv, cot, fcol, counts, gm, ml, vec, *k, rows=IMAGE)
            if k[0] == 1:
                for j in range(3):
                    load("q%d" % j, w_h.at[j], w.at[j])
        elif op == "go":
            need("att")
            weight_grad_part(att, ml, g, 3, *k)
        elif op == "ga":
            need("out")
            grad_attended_part(ml, w, ga, *k)
        elif op == "ab":
            need("proj", "probs")
            attend_back(proj, probs, ga, dproj, *k)
        elif op == "gq":
            need("e1")
            weight_grad_part(e1, dproj.at[k[0]], g, *k)
        elif op == "b1":
            need("tok", "q0", "q1", "q2")
            back_one_part(dproj, w, tok, fcol, pv, gm, tg, vec, *k, rows=IMAGE)
            if k[0] == 1:
                pltpu.make_async_copy(tg, tg_h, out_sem.at[0]).start()
        elif op == "la":
            load("act", act_h, act)
            for j in range(4):
                load("l%d" % j, w_h.at[8 + j], w.at[j])
        elif op == "lo":
            need("act", "l0", "l1", "l2", "l3")
            lower(act, w, mid, lo, *k, first=0)
            if k[0] == 1:
                pltpu.make_async_copy(lo, lo_h, out_sem.at[1]).start()

    for entry in order:
        if entry[0] == "issue":
            sender.issue(entry[1], entry[2])
        elif entry[0] == "waits":
            sender.wait(entry[1])
        elif entry[1][0][0].isupper():
            steps.run(*entry[1])
        else:
            compute(*entry[1])
    pltpu.make_async_copy(tg, tg_h, out_sem.at[0]).wait()
    pltpu.make_async_copy(lo, lo_h, out_sem.at[1]).wait()
    vec_out[...] = vec[4]


def backward(flags, counts, pv, act, cot, dg, gl, gd, w, e2, mid, att, proj, probs, e1, tok):
    items = reduce_items()
    steps, made, vector_made = backward_tasks()
    order = plan(steps + reduce_tasks(items, made) + vector_tasks(vector_made), RATES, WINDOW, ARRIVE, SENT, ISSUE)
    vmem, anywhere = pl.BlockSpec(memory_space=pltpu.VMEM), pl.BlockSpec(memory_space=pl.ANY)
    whole, three, four = (ROWS, CW), (3, ROWS, CW), (4, ROWS, CW)
    dma = pltpu.SemaphoreType.DMA
    return pl.pallas_call(
        functools.partial(backward_kernel, items, order),
        out_shape=[
            jax.ShapeDtypeStruct(whole, BF),
            jax.ShapeDtypeStruct(whole, BF),
            jax.ShapeDtypeStruct((BLOCKS, RU, CW), BF),
            jax.ShapeDtypeStruct((8, CW), F32),
        ],
        in_specs=[vmem, pl.BlockSpec(memory_space=pltpu.SMEM), vmem] + [anywhere] * 13,
        out_specs=[anywhere, anywhere, vmem, vmem],
        scratch_shapes=[
            pltpu.VMEM(four, BF),
            pltpu.VMEM(whole, BF),
            pltpu.VMEM(four, BF),
            pltpu.VMEM((5, 4, 2, RU, CW), BF),
            pltpu.VMEM(whole, BF),
            pltpu.VMEM(whole, F32),
            pltpu.VMEM(whole, BF),
            pltpu.VMEM(three, BF),
            pltpu.VMEM((4, 8, IMAGE, IMAGE), BF),
            pltpu.VMEM(whole, BF),
            pltpu.VMEM(whole, BF),
            pltpu.VMEM((ROWS, 1), F32),
            pltpu.VMEM(whole, BF),
            pltpu.VMEM(whole, F32),
            pltpu.VMEM(whole, BF),
            pltpu.VMEM((BLOCKS, 4, 2, RU, CW), BF),
            dma((32,)),
            dma((2,)),
        ]
        + reduce_scratch(len(items)),
        compiler_params=pltpu.CompilerParams(collective_id=1, has_side_effects=True, vmem_limit_bytes=VMEM_LIMIT),
        name="backward",
    )(flags, counts, pv, act, cot, dg, gl, gd, w, e2, mid, att, proj, probs, e1, tok)


ADAM_AHEAD = 12


def adamw_step(weight, grad, first, second, rate):
    new_first = BETA_ONE * first + (1.0 - BETA_ONE) * grad
    new_second = BETA_TWO * second + (1.0 - BETA_TWO) * grad * grad
    v = new_second * (1.0 / (1.0 - BETA_TWO**STEP))
    ratio = new_first * (1.0 / (1.0 - BETA_ONE**STEP)) / (v * lax.rsqrt(v) + ADAM_EPS)
    return (new_first, new_second, weight - rate * (ratio + DECAY * weight))


def adam_kernel(fin, vec, fs, *refs):
    states, vecs, done, outs, vec_outs, handed = refs[:12], refs[12:15], refs[15:17], refs[17:29], refs[29:33], refs[33:35]
    ins, news, kept, in_sem, out_sem, done_sem = refs[35:]
    keep = [pltpu.make_async_copy(done[k], kept.at[k], done_sem.at[k]) for k in range(2)]
    hand_on = [pltpu.make_async_copy(kept.at[k], handed[k], done_sem.at[2 + k]) for k in range(2)]

    def block(ref, j):
        if j < 3:
            return ref.at[:, pl.ds(j * CW, CW)]
        if j == 3:
            return ref
        if j < 8:
            return ref.at[:, pl.ds((j - 4) * CW, CW)]
        return ref.at[pl.ds((j - 8) * RU, RU), :]

    matrix_of = [0] * 3 + [1] + [2] * 4 + [3] * 4
    loads, saves = [], []
    for j in range(BLOCKS):
        three = [
            pltpu.make_async_copy(block(states[3 * matrix_of[j] + k], j), ins.at[j, k], in_sem.at[j, k]) for k in range(3)
        ]
        loads.append(three)

    def start(j):
        for copy in loads[j]:
            copy.start()

    for j in range(ADAM_AHEAD):
        start(j)
        if j == 2:
            for copy in keep:
                copy.start()
    column = lax.broadcasted_iota(jnp.int32, (RU, CW), 1) == lax.broadcasted_iota(jnp.int32, (RU, CW), 0) + fs[0] * RU
    grad = lax.dot_general(
        vec[...], column.astype(F32), (((1,), (1,)), ((), ())), preferred_element_type=F32,
        precision=lax.Precision.HIGHEST,
    )
    first, second, new = adamw(vecs[0][...], grad[0:5], vecs[1][...], vecs[2][...], RATE_VECTORS)
    vec_outs[0][...] = first
    vec_outs[1][0:2, :] = second[0:2]
    vec_outs[1][2:3, :] = second[4:5]
    vec_outs[2][...] = second[2:4]
    vec_outs[3][...] = new
    for j in range(BLOCKS):
        rate = (RATE_QKV, RATE_OUT, RATE_UP, RATE_DOWN)[matrix_of[j]]
        if j == 2:
            for k in range(2):
                keep[k].wait()
                hand_on[k].start()
        if j + ADAM_AHEAD < BLOCKS:
            start(j + ADAM_AHEAD)
        for copy in loads[j]:
            copy.wait()

        def rows(i, _, j=j, rate=rate):
            r = part(i, 32)
            result = adamw_step(ins[j, 0, r, :], fin[j, r, :].astype(F32), ins[j, 1, r, :], ins[j, 2, r, :], rate)
            for k in range(3):
                news[j, k, r, :] = result[k]
            return 0

        lax.fori_loop(0, RU // 32, rows, 0)
        for k in range(3):
            copy = pltpu.make_async_copy(news.at[j, k], block(outs[3 * matrix_of[j] + k], j), out_sem.at[j, k])
            copy.start()
            saves.append(copy)
    for copy in saves + hand_on:
        copy.wait()


def adam(fin, vec, fs, states, vecs, done):
    vmem, anywhere = pl.BlockSpec(memory_space=pltpu.VMEM), pl.BlockSpec(memory_space=pl.ANY)
    dma = pltpu.SemaphoreType.DMA
    return pl.pallas_call(
        adam_kernel,
        out_shape=[jax.ShapeDtypeStruct(s.shape, F32) for s in states]
        + [jax.ShapeDtypeStruct((n, RU), F32) for n in (5, 3, 2, 5)]
        + [jax.ShapeDtypeStruct(d.shape, d.dtype) for d in done],
        in_specs=[vmem, vmem, pl.BlockSpec(memory_space=pltpu.SMEM)] + [anywhere] * 12 + [vmem] * 3 + [anywhere] * 2,
        out_specs=[anywhere] * 12 + [vmem] * 4 + [anywhere] * 2,
        scratch_shapes=[
            pltpu.VMEM((BLOCKS, 3, RU, CW), F32),
            pltpu.VMEM((BLOCKS, 3, RU, CW), F32),
            pltpu.VMEM((2, ROWS, CW), BF),
            dma((BLOCKS, 3)),
            dma((BLOCKS, 3)),
            dma((4,)),
        ],
        compiler_params=pltpu.CompilerParams(vmem_limit_bytes=VMEM_LIMIT),
        name="adam",
    )(fin, vec, fs, *states, *vecs, *done)


def on_device_plain(
    tokens,
    mask_flags,
    mask_counts,
    cotangent,
    w_qkv,
    w_out,
    w_up,
    w_down,
    vectors,
    first_qkv,
    first_out,
    first_up,
    first_down,
    first_vectors,
    second_qkv,
    second_out,
    second_up,
    second_down,
    second_vectors,
):
    rows, width = tokens.shape
    images = mask_counts.shape[0]
    length = rows // images
    factor = HEAD_DIM ** (-0.5)
    attn_shards = (
        w_qkv.astype(jnp.bfloat16),
        w_out.astype(jnp.bfloat16),
        vectors.astype(jnp.bfloat16),
    )
    mlp_shards = (w_up.astype(jnp.bfloat16), w_down.astype(jnp.bfloat16))
    full_qkv, full_out, full_vec = (
        lax.all_gather(attn_shards[0], "fsdp", axis=0, tiled=True),
        lax.all_gather(attn_shards[1], "fsdp", axis=0, tiled=True),
        lax.all_gather(attn_shards[2], "fsdp", axis=0, tiled=True),
    )
    full_up, full_down = (
        lax.all_gather(mlp_shards[0], "fsdp", axis=0, tiled=True),
        lax.all_gather(mlp_shards[1], "fsdp", axis=0, tiled=True),
    )
    params = full_vec.astype(jnp.float32)
    masked = (mask_flags == 1)[:, None]
    hidden = jnp.where(masked, params[:, 4][None, :], tokens.astype(jnp.float32))
    normed_one, inverse_one = standardize(hidden)
    entry_one = (normed_one * params[:, 0] + params[:, 1]).astype(jnp.bfloat16)
    project = jnp.dot(entry_one, full_qkv, preferred_element_type=jnp.float32).astype(jnp.bfloat16)
    split = project.reshape(images, length, 3, HEADS, HEAD_DIM)
    queries = split[:, :, 0]
    keys = split[:, :, 1]
    values = split[:, :, 2]
    scores = (
        jnp.einsum("bqhd,bkhd->bhqk", queries, keys, preferred_element_type=jnp.float32) * factor
    )
    top = jnp.max(scores, axis=-1, keepdims=True)
    total = jnp.sum(jnp.exp(scores - top), axis=-1, keepdims=True)
    logsum = top + jnp.log(total)
    probs_low = jnp.exp(scores - logsum).astype(jnp.bfloat16)
    mixed = jnp.einsum("bhqk,bkhd->bqhd", probs_low, values, preferred_element_type=jnp.float32)
    attended = mixed.astype(jnp.bfloat16).reshape(rows, width)
    middle = hidden + jnp.dot(attended, full_out, preferred_element_type=jnp.float32)
    normed_two, inverse_two = standardize(middle)
    entry_two = (normed_two * params[:, 2] + params[:, 3]).astype(jnp.bfloat16)
    rising = jnp.dot(entry_two, full_up, preferred_element_type=jnp.float32)
    activated, gelu_pull = jax.vjp(gelu_exact, rising)
    active = activated.astype(jnp.bfloat16)
    layer_out = (middle + jnp.dot(active, full_down, preferred_element_type=jnp.float32)).astype(
        jnp.bfloat16
    )
    row_weight = jnp.repeat(
        length / mask_counts.astype(jnp.float32), length, total_repeat_length=rows
    )
    grad_out = (
        cotangent.astype(jnp.float32) * (row_weight * mask_flags.astype(jnp.float32))[:, None]
    )
    back_up, back_down = (
        lax.all_gather(mlp_shards[0], "fsdp", axis=0, tiled=True),
        lax.all_gather(mlp_shards[1], "fsdp", axis=0, tiled=True),
    )
    back_qkv, back_out, back_vec = (
        lax.all_gather(attn_shards[0], "fsdp", axis=0, tiled=True),
        lax.all_gather(attn_shards[1], "fsdp", axis=0, tiled=True),
        lax.all_gather(attn_shards[2], "fsdp", axis=0, tiled=True),
    )
    gains = back_vec.astype(jnp.float32)
    grad_low = grad_out.astype(jnp.bfloat16)
    grad_down = jnp.einsum("tf,td->fd", active, grad_low, preferred_element_type=jnp.float32)
    grad_active = jnp.einsum("td,fd->tf", grad_low, back_down, preferred_element_type=jnp.float32)
    grad_rising = gelu_pull(grad_active)[0].astype(jnp.bfloat16)
    grad_up = jnp.einsum("td,tf->df", entry_two, grad_rising, preferred_element_type=jnp.float32)
    grad_entry_two = jnp.einsum(
        "tf,df->td", grad_rising, back_up, preferred_element_type=jnp.float32
    )
    mlp_sums = (
        lax.psum_scatter(grad_up, "fsdp", scatter_dimension=0, tiled=True),
        lax.psum_scatter(grad_down, "fsdp", scatter_dimension=0, tiled=True),
    )
    back_two, gain_two, bias_two = norm_back(grad_entry_two, normed_two, inverse_two, gains[:, 2])
    grad_middle = grad_out + back_two
    middle_low = grad_middle.astype(jnp.bfloat16)
    grad_wout = jnp.einsum("tc,td->cd", attended, middle_low, preferred_element_type=jnp.float32)
    grad_attended = jnp.einsum(
        "td,cd->tc", middle_low, back_out, preferred_element_type=jnp.float32
    )
    grad_attended = grad_attended.astype(jnp.bfloat16).reshape(images, length, HEADS, HEAD_DIM)
    again_scores = (
        jnp.einsum("bqhd,bkhd->bhqk", queries, keys, preferred_element_type=jnp.float32) * factor
    )
    probs = jnp.exp(again_scores - logsum)
    again_low = probs.astype(jnp.bfloat16)
    grad_values = jnp.einsum(
        "bhqk,bqhd->bkhd", again_low, grad_attended, preferred_element_type=jnp.float32
    )
    grad_probs = jnp.einsum(
        "bqhd,bkhd->bhqk", grad_attended, values, preferred_element_type=jnp.float32
    )
    grad_scores = probs * (grad_probs - jnp.sum(grad_probs * probs, axis=-1, keepdims=True))
    grad_raw = (grad_scores * factor).astype(jnp.bfloat16)
    grad_queries = jnp.einsum("bhqk,bkhd->bqhd", grad_raw, keys, preferred_element_type=jnp.float32)
    grad_keys = jnp.einsum("bhqk,bqhd->bkhd", grad_raw, queries, preferred_element_type=jnp.float32)
    grad_project = (
        jnp.stack([grad_queries, grad_keys, grad_values], axis=2)
        .reshape(rows, 3 * width)
        .astype(jnp.bfloat16)
    )
    grad_qkv = jnp.einsum("td,te->de", entry_one, grad_project, preferred_element_type=jnp.float32)
    grad_entry_one = jnp.einsum(
        "te,de->td", grad_project, back_qkv, preferred_element_type=jnp.float32
    )
    back_one, gain_one, bias_one = norm_back(grad_entry_one, normed_one, inverse_one, gains[:, 0])
    grad_hidden = back_one + grad_middle
    token_grad = jnp.where(masked, 0.0, grad_hidden).astype(jnp.bfloat16)
    grad_mask = jnp.sum(jnp.where(masked, grad_hidden, 0.0), axis=0)
    grad_vec = jnp.stack([gain_one, bias_one, gain_two, bias_two, grad_mask], axis=1)
    attn_sums = (
        lax.psum_scatter(grad_qkv, "fsdp", scatter_dimension=0, tiled=True),
        lax.psum_scatter(grad_wout, "fsdp", scatter_dimension=0, tiled=True),
        lax.psum_scatter(grad_vec, "fsdp", scatter_dimension=0, tiled=True),
    )
    sum_qkv, sum_out, sum_vec, sum_up, sum_down = (
        lax.psum(attn_sums[0].astype(jnp.bfloat16), "dp").astype(jnp.float32),
        lax.psum(attn_sums[1].astype(jnp.bfloat16), "dp").astype(jnp.float32),
        lax.psum(attn_sums[2].astype(jnp.bfloat16), "dp").astype(jnp.float32),
        lax.psum(mlp_sums[0].astype(jnp.bfloat16), "dp").astype(jnp.float32),
        lax.psum(mlp_sums[1].astype(jnp.bfloat16), "dp").astype(jnp.float32),
    )
    qkv_first, qkv_second, qkv_new = adamw(w_qkv, sum_qkv, first_qkv, second_qkv, RATE_QKV)
    out_first, out_second, out_new = adamw(w_out, sum_out, first_out, second_out, RATE_OUT)
    up_first, up_second, up_new = adamw(w_up, sum_up, first_up, second_up, RATE_UP)
    down_first, down_second, down_new = adamw(w_down, sum_down, first_down, second_down, RATE_DOWN)
    vec_first, vec_second, vec_new = adamw(
        vectors, sum_vec, first_vectors, second_vectors, RATE_VECTORS
    )
    second_front = jnp.concatenate([vec_second[:, 0:2], vec_second[:, 4:5]], axis=1)
    second_later = vec_second[:, 2:4]
    return (
        layer_out,
        token_grad,
        qkv_first,
        out_first,
        up_first,
        down_first,
        vec_first,
        qkv_second,
        out_second,
        up_second,
        down_second,
        second_front,
        second_later,
        qkv_new,
        out_new,
        up_new,
        down_new,
        vec_new,
    )


def on_device_fast(
    tokens,
    mask_flags,
    mask_counts,
    cotangent,
    w_qkv,
    w_out,
    w_up,
    w_down,
    vectors,
    first_qkv,
    first_out,
    first_up,
    first_down,
    first_vectors,
    second_qkv,
    second_out,
    second_up,
    second_down,
    second_vectors,
):
    flags = mask_flags.reshape(1, ROWS)
    w, pv, e1, proj, probs, att, mid, e2, act, dg, gl, gd = forward(
        w_qkv, w_out, w_up, w_down, vectors.T, tokens, flags, mask_counts, cotangent
    )
    layer_out, token_grad, sums, sum_vec = backward(
        flags, mask_counts, pv, act, cotangent, dg, gl, gd, w, e2, mid, att, proj, probs, e1, tokens
    )
    states = (
        w_qkv, first_qkv, second_qkv, w_out, first_out, second_out,
        w_up, first_up, second_up, w_down, first_down, second_down,
    )
    fs = lax.axis_index("fsdp").astype(jnp.int32).reshape(1)
    new = adam(sums, sum_vec, fs, states, (vectors.T, first_vectors.T, second_vectors.T), (layer_out, token_grad))
    new_w, new_first, new_second = [[new[3 * m + k] for m in range(4)] for k in (2, 0, 1)]
    vec_first, second_front, second_later, vec_new = [v.T for v in new[12:16]]
    layer_out, token_grad = new[16:]
    return (
        layer_out, token_grad, *new_first, vec_first, *new_second, second_front, second_later, *new_w, vec_new
    )


def solution(mesh):
    placed = (
        P(("dp", "fsdp"), None),
        P(("dp", "fsdp")),
        P(("dp", "fsdp")),
        P(("dp", "fsdp"), None),
        P("fsdp", None),
        P("fsdp", None),
        P("fsdp", None),
        P("fsdp", None),
        P("fsdp", None),
        P("fsdp", None),
        P("fsdp", None),
        P("fsdp", None),
        P("fsdp", None),
        P("fsdp", None),
        P("fsdp", None),
        P("fsdp", None),
        P("fsdp", None),
        P("fsdp", None),
        P("fsdp", None),
    )
    shape = dict(mesh.shape)
    fast = shape["dp"] == 4 and shape["fsdp"] == 8
    return jax.shard_map(
        on_device_fast if fast else on_device_plain,
        mesh=mesh,
        in_specs=placed,
        out_specs=(
            P(("dp", "fsdp"), None),
            P(("dp", "fsdp"), None),
            P("fsdp", None),
            P("fsdp", None),
            P("fsdp", None),
            P("fsdp", None),
            P("fsdp", None),
            P("fsdp", None),
            P("fsdp", None),
            P("fsdp", None),
            P("fsdp", None),
            P("fsdp", None),
            P("fsdp", None),
            P("fsdp", None),
            P("fsdp", None),
            P("fsdp", None),
            P("fsdp", None),
            P("fsdp", None),
        ),
        check_vma=False,
    )
```

```python
import functools

import jax
import jax.numpy as jnp
from jax import lax
from jax.experimental import pallas as pl
from jax.experimental.pallas import tpu as pltpu
from jax.sharding import PartitionSpec as P

DP, FSDP = "dp", "fsdp"
PAIRS, MIXED, MIXED_BACK = "bqhd,bkhd->bhqk", "bhqk,bkhd->bqhd", "bhqk,bqhd->bkhd"
ACTIVE, QUEUE, OVER, LATE, LAST = range(5)
HEADS = 16
HEAD_DIM = 48
STEP = 10


EPS_NORM = 1e-06
BETA_ONE = 0.5
BETA_TWO = 0.5
ADAM_EPS = 1e-08
DECAY = 0.01
RATE_QKV = 0.02
RATE_OUT = 0.1
RATE_UP = 0.02
RATE_DOWN = 0.01
RATE_VECTORS = 0.2

BF = jnp.bfloat16
F32 = jnp.float32
MESH = pl.DeviceIdType.MESH

RU, CW, H = 96, 768, 48
BLOCKS = 12
GATHER_ITEMS = (
    ((0, 1), 1, False), ((2,), 1, False), ((3, 4), 1, False), ((11,), 1, False), ((7, 10), 1, True), ((5,), 1, True),
    ((6, 8), 1, False), ((9,), 1, True),
)
GATHER_RATES = dict(u=46e3, d=46e3, y=46e3, x=46e3, c=280e3)
GATHER_WINDOW = dict(u=2, d=2, y=4, x=8, c=6)
GATHER_ISSUE = 0.2
VMEM_LIMIT = 62 * 2**20


def standardize(values):
    mean = jnp.mean(values, axis=-1, keepdims=True)
    centred = values - mean
    inverse = lax.rsqrt(jnp.mean(centred * centred, axis=-1, keepdims=True) + EPS_NORM)
    return (centred * inverse, inverse)


def norm_back(grad, normed, inverse, gain):
    scaled = grad * gain[None, :]
    first = jnp.mean(scaled, axis=-1, keepdims=True)
    second = jnp.mean(scaled * normed, axis=-1, keepdims=True)
    return (
        inverse * (scaled - first - normed * second),
        jnp.sum(grad * normed, axis=0),
        jnp.sum(grad, axis=0),
    )


def gelu_exact(values):
    return jax.nn.gelu(values, approximate=False)


def adamw(weight, grad, first, second, rate):
    new_first = BETA_ONE * first + (1.0 - BETA_ONE) * grad
    new_second = BETA_TWO * second + (1.0 - BETA_TWO) * grad * grad
    fix_one = 1.0 - BETA_ONE**STEP
    fix_two = 1.0 - BETA_TWO**STEP
    ratio = new_first / fix_one / (jnp.sqrt(new_second / fix_two) + ADAM_EPS)
    return (new_first, new_second, weight - rate * (ratio + DECAY * weight))


class Place:
    def __init__(self):
        dp, fs = lax.axis_index(DP), lax.axis_index(FSDP)
        self.x, self.c = dp // 2, dp % 2
        self.z, self.y = fs // 2, fs % 2
        x, y, z, c = self.x, self.y, self.z, self.c
        self.sib = self.dev(x, y, z, 1 - c)
        self.xn = self.dev(1 - x, y, z, c)
        self.xn_sib = self.dev(1 - x, y, z, 1 - c)
        self.yn = self.dev(x, 1 - y, z, c)
        self.end = (z == 0) | (z == 3)
        self.mid = (z == 1) | (z == 2)
        self.inner = self.dev(x, y, z + 1 - 2 * (z // 2), c)
        self.outer = self.dev(x, y, (z + 3 + 2 * (z // 2)) % 4, c)
        self.up = self.dev(x, y, (z + 1) % 4, c)
        self.down = self.dev(x, y, (z + 3) % 4, c)
        self.far = self.dev(x, y, (z + 2) % 4, c)

    def dev(self, x, y, z, c):
        return (x * 2 + c, z * 2 + y)

    def mine(self, blocks):
        return blocks[0] if len(blocks) == 1 else blocks[0] + self.x * (blocks[1] - blocks[0])

    def theirs(self, blocks):
        return blocks[1] + self.x * (blocks[0] - blocks[1])


def arrived(ref, sem):
    pltpu.make_async_copy(ref, ref, sem).wait()


def add_into(dst, left, right):
    for row in range(0, dst.shape[-2], 16):
        dst[row : row + 16] = (left[row : row + 16].astype(F32) + right[row : row + 16].astype(F32)).astype(BF)


ROWS, IMAGE = 512, 256
FACTOR = HEAD_DIM**-0.5
LOG2E = 1.4426950408889634


def dot(left, right, over_left=1, over_right=0):
    return lax.dot_general(left, right, (((over_left,), (over_right,)), ((), ())), preferred_element_type=F32)


def matrix(w, j):
    return w[j].reshape(CW, CW)


def down_rows(w, s, first=8):
    return jnp.concatenate([w[first + k, s // 2, s % 2] for k in range(4)], axis=0)


def part(i, rows):
    return pl.ds(pl.multiple_of(i * rows, rows), rows)


def flag_column(flags, fcol):
    spot = lax.broadcasted_iota(jnp.int32, (IMAGE, IMAGE), 0) == lax.broadcasted_iota(jnp.int32, (IMAGE, IMAGE), 1)
    for b in range(2):
        row = jnp.broadcast_to((flags[:, b * IMAGE : (b + 1) * IMAGE] == 1).astype(F32), (8, IMAGE)).astype(BF)
        fcol[b * IMAGE : (b + 1) * IMAGE, :] = dot(spot.astype(F32).astype(BF), row, 1, 1)[:, 0:1]


def vector_tile(vectors, tile):
    tile[...] = jnp.zeros_like(tile)
    tile[0:5, 0:RU] = vectors[...].astype(BF)


def spread(s):
    row = lax.broadcasted_iota(jnp.int32, (128, CW), 0)
    column = lax.broadcasted_iota(jnp.int32, (128, CW), 1)
    return ((row < RU) & (column == row + s * RU)).astype(F32).astype(BF)


def vector_rows(tiles, pv):
    total = dot(tiles[0], spread(0))
    for s in range(1, 8):
        total = total + dot(tiles[s], spread(s))
    pv[...] = total


def hidden_rows(tok, fcol, pv, r):
    return jnp.where(fcol[r, :] > 0.5, pv[4:5, :], tok[r, :].astype(F32))


def norm_one(tok, fcol, pv, e1, i, rows=128):
    for k in range(rows // 64):
        r = pl.ds(pl.multiple_of(i * rows + k * 64, 64), 64)
        n, _ = standardize(hidden_rows(tok, fcol, pv, r))
        e1[r, :] = (n * pv[0:1, :] + pv[1:2, :]).astype(BF)


def project_part(e1, w, proj, j, i):
    r = part(i, 256)
    proj[j, r, :] = dot(e1[r, :], matrix(w, j)).astype(BF)


def head_lanes():
    return [(h * HEAD_DIM, range(h * HEAD_DIM // 128, (h * HEAD_DIM + HEAD_DIM - 1) // 128 + 1)) for h in range(8)]


def lane_mask(first, t):
    lane = lax.broadcasted_iota(jnp.int32, (1, 128), 1) + t * 128
    return ((lane >= first) & (lane < first + HEAD_DIM)).astype(F32).astype(BF)


def attend(proj, att, probs, b, group):
    rows = part(b, IMAGE)

    def lanes(t):
        return slice(group * 384 + t * 128, group * 384 + t * 128 + 128)

    acc = [None] * 3
    for h, (first, tiles) in enumerate(head_lanes()):
        masks = {t: lane_mask(first, t) for t in tiles}
        s = sum(dot(proj[1, rows, lanes(t)], proj[0, rows, lanes(t)] * masks[t], 1, 1) for t in tiles)
        top = jnp.max(s, axis=0, keepdims=True)
        e = jnp.exp2((s - top) * (FACTOR * LOG2E))
        p = (e * (1.0 / jnp.sum(e, axis=0, keepdims=True))).astype(BF)
        probs[2 * b + group, h] = p
        for t in tiles:
            o = dot(p, proj[2, rows, lanes(t)] * masks[t], 0, 0)
            acc[t] = o if acc[t] is None else acc[t] + o
    for t in range(3):
        att[rows, lanes(t)] = acc[t].astype(BF)


def norm_two(tok, fcol, pv, att, w, mid, e2, i):
    r = part(i, 256)
    v = hidden_rows(tok, fcol, pv, r) + dot(att[r, :], matrix(w, 3))
    mid[r, :] = v
    n, _ = standardize(v)
    e2[r, :] = (n * pv[2:3, :] + pv[3:4, :]).astype(BF)


def rise(e2, w, act, dg, k, i, rows=128):
    r = part(i, rows)
    v = dot(e2[r, :], matrix(w, 4 + k))
    cdf = 0.5 * (1.0 + lax.erf(v * 0.7071067811865476))
    act[k, r, :] = (v * cdf).astype(BF)
    dg[k, r, :] = (cdf + v * (jnp.exp2(v * v * (-0.5 * LOG2E)) * 0.3989422804014327)).astype(BF)


def lower(act, w, mid, out, i, first=8):
    r = part(i, 256)
    total = mid[r, :]
    for s in range(8):
        total = total + dot(act[s // 2, r, (s % 2) * 384 : (s % 2) * 384 + 384], down_rows(w, s, first))
    out[r, :] = total.astype(BF)


PLAN_END = []


class Task:
    def __init__(self, name, time, needs, sends=(), rank=0):
        self.name, self.time, self.needs, self.sends, self.rank = name, time, tuple(needs), tuple(sends), rank


def plan(tasks, rates, window, arrive, sent, issue=0.1):
    now = 0.0
    links = {name: {ACTIVE: {}, QUEUE: [], OVER: [], LATE: [], LAST: 0.0} for name in rates}
    done, left, order, count = {}, list(tasks), [], 0

    def advance(to):
        for name, link in links.items():
            at = link[LAST]
            while link[ACTIVE]:
                token, rest = next(iter(link[ACTIVE].items()))
                end = at + rest / rates[name]
                if end > to + 1e-9:
                    link[ACTIVE][token] -= (to - at) * rates[name]
                    at = to
                    break
                del link[ACTIVE][token]
                at = end
                done[token] = end + arrive
                link[LATE].append((end + sent, token))
            link[LAST] = max(at, to)

    while left or any(link[QUEUE] or link[ACTIVE] for link in links.values()):
        advance(now)
        moved = False
        for name, link in links.items():
            link[OVER] += [q[1] for q in link[LATE] if q[0] <= now]
            link[LATE] = [q for q in link[LATE] if q[0] > now]
            while link[QUEUE] and len(link[ACTIVE]) + len(link[LATE]) < window[name]:
                link[QUEUE].sort()
                _, _, token, size = link[QUEUE].pop(0)
                order.append(("issue", token, link[OVER]))
                link[OVER] = []
                now += issue
                advance(now)
                link[ACTIVE][token] = size
                moved = True
        ready = [q for q in left if all(done.get(need, 1e18) <= now for need in q.needs)]
        if ready:
            task = min(ready, key=lambda q: q.rank)
            left.remove(task)
            order.append(("run", task.name))
            now += task.time
            advance(now)
            done[task.name] = now
            for name, size, token, rank in task.sends:
                count += 1
                links[name][QUEUE].append((rank, count, token, size))
            moved = True
        if not moved:
            times = [v for v in done.values() if v > now]
            for name, link in links.items():
                times += [q[0] for q in link[LATE] if q[0] > now]
                if link[ACTIVE]:
                    times.append(link[LAST] + next(iter(link[ACTIVE].values())) / rates[name])
            now = max(min(times), now) + 1e-6
    PLAN_END.append(now)
    order.append(("waits", [t for link in links.values() for t in link[OVER] + [q[1] for q in link[LATE]]]))
    return order


ARRIVE, SENT, ISSUE = 1.5, 1.0, 0.06


class Sender:
    def __init__(self, sems, window):
        self.sems, self.queued, self.under_way = sems, {}, {}
        self.free, first = {}, 0
        for name, slots in window.items():
            self.free[name] = list(range(first, first + slots))
            first += slots

    def put(self, token, link, src, dst, sem, to, cond=None):
        self.queued[token] = (link, src, dst, sem, to, cond)

    def issue(self, token, over):
        self.wait(over)
        link, src, dst, sem, to, cond = self.queued.pop(token)
        slot = self.free[link].pop(0)
        copy = pltpu.make_async_remote_copy(
            src_ref=src, dst_ref=dst, send_sem=self.sems.at[slot], recv_sem=sem, device_id=to, device_id_type=MESH
        )
        if cond is None:
            copy.start()
        else:
            pl.when(cond)(copy.start)
        self.under_way[token] = (link, slot, copy, cond)

    def wait(self, tokens):
        for token in tokens:
            link, slot, copy, cond = self.under_way.pop(token)
            self.free[link].append(slot)
            if cond is None:
                copy.wait_send()
            else:
                pl.when(cond)(copy.wait_send)


def grad_out_rows(cot, fcol, counts, r, b):
    weight = float(IMAGE) / jnp.full((1, 1), counts[b], jnp.int32).astype(F32)
    return cot[r, :].astype(F32) * (fcol[r, :] * weight)


def grad_low_part(cot, fcol, counts, gl, b):
    for k in range(4):
        r = pl.ds(b * IMAGE + k * 64, 64)
        gl[r, :] = grad_out_rows(cot, fcol, counts, r, b).astype(BF)


def grad_down_part(act, gl, g, s):
    d = dot(act[s // 2, :, (s % 2) * 384 : (s % 2) * 384 + 384], gl[...], 0, 0).astype(BF)
    for k in range(4):
        g[k, s // 2, s % 2] = d[k * RU : (k + 1) * RU]


def grad_rising_part(gl, w, dg, k):
    rows = jnp.concatenate([down_rows(w, 2 * k, 0), down_rows(w, 2 * k + 1, 0)], axis=0)
    dg[k] = (dot(gl[...], rows, 1, 1) * dg[k].astype(F32)).astype(BF)


def weight_grad_part(left, right, g, j, i):
    d = dot(left[:, i * 384 : i * 384 + 384], right[...], 0, 0).astype(BF)
    g[j, 2 * i : 2 * i + 2] = d.reshape(2, 2, RU, CW)


def norm_back_rows(grad, n, inverse, gain):
    scaled = grad * gain
    first = jnp.mean(scaled, axis=-1, keepdims=True)
    second = jnp.mean(scaled * n, axis=-1, keepdims=True)
    return inverse * (scaled - first - n * second)


def row_sum(values):
    return jnp.sum(values, axis=0, keepdims=True)


def back_two_part(gr, w, mid, pv, cot, fcol, counts, gm, ml, vec, i, rows=128):
    r = part(i, rows)
    grad = sum(dot(gr[k, r, :], matrix(w, k), 1, 1) for k in range(4))
    n, inverse = standardize(mid[r, :])
    total = grad_out_rows(cot, fcol, counts, r, i * rows // IMAGE) + norm_back_rows(grad, n, inverse, pv[2:3, :])
    gm[r, :] = total
    ml[r, :] = total.astype(BF)
    vec[0, 2:3, :] += row_sum(grad * n)
    vec[0, 3:4, :] += row_sum(grad)


def grad_attended_part(ml, w, ga, i):
    r = part(i, 256)
    ga[r, :] = dot(ml[r, :], matrix(w, 4), 1, 1).astype(BF)


def attend_back(proj, probs, ga, dproj, b, group):
    rows = part(b, IMAGE)

    def lanes(t):
        return slice(group * 384 + t * 128, group * 384 + t * 128 + 128)

    acc = [[None] * 3 for _ in range(3)]

    def add(k, t, value):
        acc[k][t] = value if acc[k][t] is None else acc[k][t] + value

    for h, (first, tiles) in enumerate(head_lanes()):
        masks = {t: lane_mask(first, t) for t in tiles}
        low = probs[2 * b + group, h]
        grad = sum(dot(proj[2, rows, lanes(t)], ga[rows, lanes(t)] * masks[t], 1, 1) for t in tiles)
        p = low.astype(F32)
        delta = jnp.sum(grad * p, axis=0, keepdims=True)
        raw = (p * ((grad - delta) * FACTOR)).astype(BF)
        for t in tiles:
            add(0, t, dot(raw, proj[1, rows, lanes(t)] * masks[t], 0, 0))
            add(1, t, dot(raw, proj[0, rows, lanes(t)] * masks[t]))
            add(2, t, dot(low, ga[rows, lanes(t)] * masks[t]))
    for k in range(3):
        for t in range(3):
            dproj[k, rows, lanes(t)] = acc[k][t].astype(BF)


def back_one_part(dproj, w, tok, fcol, pv, gm, tg, vec, i, rows=128):
    r = part(i, rows)
    grad = sum(dot(dproj[k, r, :], matrix(w, k), 1, 1) for k in range(3))
    n, inverse = standardize(hidden_rows(tok, fcol, pv, r))
    total = norm_back_rows(grad, n, inverse, pv[0:1, :]) + gm[r, :]
    on = fcol[r, :] > 0.5
    tg[r, :] = jnp.where(on, 0.0, total).astype(BF)
    vec[0, 0:1, :] += row_sum(grad * n)
    vec[0, 1:2, :] += row_sum(grad)
    vec[0, 4:5, :] += row_sum(jnp.where(on, total, 0.0))


class Gatherer:
    def __init__(self, at, items, w, sender, cast, zs, ys, xs, cs):
        self.at, self.items, self.w, self.sender, self.cast = at, items, w, sender, cast
        self.zs, self.ys, self.xs, self.cs = zs, ys, xs, cs
        self.others = [((at.z + dz) % 4, (at.y + dy) % 2) for dz in range(4) for dy in range(2) if dz + dy > 0]

    def run(self, op, i):
        at, z, y = self.at, self.at.z, self.at.y
        blocks, y_first, first, count = self.items[i]
        pair, j = len(blocks) == 2, at.mine(blocks)
        rows = pl.ds(pl.multiple_of(at.c * H + first, 16), count)
        sib_rows = pl.ds(pl.multiple_of((1 - at.c) * H + first, 16), count)

        def send(name, link, p, sem, to, cond=None):
            self.sender.put((name, i), link, p, p, sem, to, cond)

        def share(k, t):
            send("c%d" % k, "c", self.w.at[t, :, :, rows, :], self.cs.at[i, k], at.sib)

        def start_z(p):
            send("u0", "u", p, self.zs.at[i, 0, 0], at.up, z < 3)
            send("d0", "d", p, self.zs.at[i, 0, 1], at.down, z > 0)

        if op == "S":
            for t in blocks:
                self.cast(t, first, count)
            p = self.w.at[j, z, y, rows, :]
            send("yo", "y", p, self.ys.at[i, z], at.yn)
            if not y_first:
                start_z(p)
        elif op == "Y":
            p = self.w.at[j, z, 1 - y, rows, :]
            arrived(p, self.ys.at[i, z])
            start_z(self.w.at[j, z, :, rows, :])
            if pair:
                send("xq", "x", p, self.xs.at[i, z], at.xn)
        elif op[0] == "P":
            d = int(op[1])
            for way in (0, 1):
                has = (z - d - 1 >= 0) if way == 0 else (z + d + 1 <= 3)
                zz = jnp.maximum(z - d - 1, 0) if way == 0 else jnp.minimum(z + d + 1, 3)
                p = self.w.at[j, zz, :, rows, :] if y_first else self.w.at[j, zz, y, rows, :]
                pl.when(has)(functools.partial(arrived, p, self.zs.at[i, d, way]))
                if d < 2 and way == 0:
                    send("u%d" % (d + 1), "u", p, self.zs.at[i, d + 1, 0], at.up, has & (z < 3))
                if d < 2 and way == 1:
                    send("d%d" % (d + 1), "d", p, self.zs.at[i, d + 1, 1], at.down, has & (z > 0))
                name = "ab"[way] + op[1]
                if not y_first:
                    send("y" + name, "y", p, self.ys.at[i, zz], at.yn, has)
                if pair:
                    send("x" + name, "x", p, self.xs.at[i, zz], at.xn, has)
            if y_first and d == 2:
                share(0, j)
        elif op == "Q":
            for zz in range(4):
                arrived(self.w.at[j, zz, 1 - y, rows, :], self.ys.at[i, zz])
            if pair:
                send("xq", "x", self.w.at[j, :, 1 - y, rows, :], self.xs.at[i, 4], at.xn)
            share(0, j)
        elif op == "X":
            t = at.theirs(blocks)
            for dz in (1, 2, 3):
                zz = (z + dz) % 4
                p = self.w.at[t, zz, :, rows, :] if y_first else self.w.at[t, zz, y, rows, :]
                arrived(p, self.xs.at[i, zz])
            if y_first:
                arrived(self.w.at[t, z, 1 - y, rows, :], self.xs.at[i, z])
            else:
                arrived(self.w.at[t, :, 1 - y, rows, :], self.xs.at[i, 4])
            share(1, t)
        else:
            for k, t in enumerate((j, at.theirs(blocks)) if pair else (j,)):
                arrived(self.w.at[t, :, :, sib_rows, :], self.cs.at[i, k])


def gather_items():
    return [
        (blocks, y_first, k * (H // parts), H // parts) for blocks, parts, y_first in GATHER_ITEMS for k in range(parts)
    ]


def gather_tasks(items):
    tasks, there = [], [[] for _ in range(BLOCKS)]
    for i, (blocks, y_first, _, rows) in enumerate(items):
        pair, size = len(blocks) == 2, rows * CW * 2
        wide = size * (2 if y_first else 1)
        to_z = [("u", wide, ("u0", i), i), ("d", wide, ("d0", i), i)]
        to_sib = [("c", 8 * size, ("c0", i), i)]
        tasks.append(Task(("S", i), 0.15 * len(blocks), [], [("y", size, ("yo", i), i)] + ([] if y_first else to_z), i))
        if y_first:
            to_x = [("x", size, ("xq", i), i)] if pair else []
            tasks.append(Task(("Y", i), 0.05, [("yo", i)], to_z + to_x, i))
        across, handed = [("yo", i)], [("xq", i)]
        for d, part_of in enumerate((0.75, 0.5, 0.25)):
            sends = []
            for way in "ab":
                if d < 2:
                    name = "ud"[way == "b"] + str(d + 1)
                    sends.append((name[0], wide, (name, i), i))
                if not y_first:
                    sends.append(("y", part_of * size, ("y%s%d" % (way, d), i), i))
                    across.append(("y%s%d" % (way, d), i))
                if pair:
                    sends.append(("x", part_of * wide, ("x%s%d" % (way, d), i), i))
                    handed.append(("x%s%d" % (way, d), i))
            if y_first and d == 2:
                sends += to_sib
            tasks.append(Task(("P%d" % d, i), 0.1, [("u%d" % d, i), ("d%d" % d, i)], sends, i))
        if not y_first:
            to_x = [("x", 4 * size, ("xq", i), i)] if pair else []
            tasks.append(Task(("Q", i), 0.1, across, to_x + to_sib, i))
        if pair:
            tasks.append(Task(("X", i), 0.1, handed, [("c", 8 * size, ("c1", i), i)], i))
        tasks.append(Task(("C", i), 0.1, [("c%d" % k, i) for k in range(len(blocks))], [], i))
        for j in blocks:
            there[j].append(("C", i))
    return tasks, there


def forward_kernel(
    items, order,
    w_qkv, w_out, w_up, w_down, vectors, tok, flags, counts, cot,
    w_h, pv_h, e1_h, proj_h, probs_h, att_h, mid_h, e2_h, act_h, dg_h, gl_h, gd_h,
    w, own, tile, tiles, pv, fcol, e1, proj, probs, att, mid, e2, act, dg, gl, gd, zs, ys, xs, cs, vs, save_sem, tile_sem, own_sem, send_sem,
):
    at = Place()
    fs = at.z * 2 + at.y
    sender = Sender(send_sem, GATHER_WINDOW)
    loads = []
    mine = pl.ds(pl.multiple_of(at.c * H, H), H)
    parts = [(w_qkv.at[mine, pl.ds(k * CW, CW)]) for k in range(3)] + [w_out.at[mine, :]]
    parts += [w_up.at[mine, pl.ds(k * CW, CW)] for k in range(4)]
    parts += [w_down.at[pl.ds(pl.multiple_of(k * RU + at.c * H, H), H), :] for k in range(4)]
    for blocks, _, _ in GATHER_ITEMS:
        for j in blocks:
            loads.append(pltpu.make_async_copy(parts[j], own.at[j], own_sem.at[j]))
            loads[-1].start()
    order_of = [j for blocks, _, _ in GATHER_ITEMS for j in blocks]

    def cast(j, first, count):
        k = order_of.index(j)
        if loads[k] is not None:
            loads[k].wait()
            loads[k] = None
        rows = pl.ds(pl.multiple_of(at.c * H + first, 16), count)
        w[j, at.z, at.y, rows, :] = own[j, first : first + count, :].astype(BF)

    comm = Gatherer(at, items, w, sender, cast, zs, ys, xs, cs)
    barrier = pltpu.get_barrier_semaphore()
    peers = [at.sib, at.xn] + [at.dev(at.x, yy, zz, at.c) for zz, yy in comm.others]
    for peer in peers:
        pl.semaphore_signal(barrier, inc=1, device_id=peer, device_id_type=MESH)
    vector_tile(vectors, tile)
    tiles[fs] = tile[...]
    pl.semaphore_wait(barrier, len(peers))
    tile_sends = [
        pltpu.make_async_remote_copy(
            src_ref=tile, dst_ref=tiles.at[fs], send_sem=tile_sem.at[k], recv_sem=vs.at[fs],
            device_id=at.dev(at.x, yy, zz, at.c), device_id_type=MESH,
        )
        for k, (zz, yy) in enumerate(comm.others)
    ]
    for copy in tile_sends:
        copy.start()
    saves = []

    def save(src, dst):
        copy = pltpu.make_async_copy(src, dst, save_sem.at[len(saves)])
        copy.start()
        saves.append(copy)

    def vectors_in():
        for zz, yy in comm.others:
            arrived(tiles.at[zz * 2 + yy], vs.at[zz * 2 + yy])
        vector_rows(tiles, pv)
        save(pv, pv_h)

    def compute(op, *k):
        if op == "flags":
            flag_column(flags, fcol)
        elif op == "vectors":
            vectors_in()
        elif op == "one":
            norm_one(tok, fcol, pv, e1, *k)
        elif op == "project":
            project_part(e1, w, proj, *k)
        elif op == "attend":
            attend(proj, att, probs, *k)
        elif op == "two":
            norm_two(tok, fcol, pv, att, w, mid, e2, *k)
        elif op == "rise":
            rise(e2, w, act, dg, *k)
        elif op == "low":
            grad_low_part(cot, fcol, counts, gl, *k)
        elif op == "down":
            grad_down_part(act, gl, gd, *k)
        elif op == "whole":
            save(w.at[k[0]], w_h.at[k[0]])
        else:
            j = k[0]
            refs = dict(e1=(e1, e1_h), proj=(proj, proj_h), probs=(probs, probs_h), att=(att, att_h), mid=(mid, mid_h))
            refs.update(e2=(e2, e2_h), gl=(gl, gl_h), gd=(gd.at[j], gd_h.at[j]), act=(act.at[j], act_h.at[j]), dg=(dg.at[j], dg_h.at[j]))
            save(*refs[op[5:]])

    for entry in order:
        if entry[0] == "issue":
            sender.issue(entry[1], entry[2])
        elif entry[0] == "waits":
            sender.wait(entry[1])
        elif entry[1][0][0].isupper():
            comm.run(*entry[1])
        else:
            compute(*entry[1])
    for copy in tile_sends:
        copy.wait_send()
    for copy in saves:
        copy.wait()


def forward_tasks(there):
    rows = [(("flags",), 0.3, []), (("vectors",), 0.8, [("u0", 1)])]
    rows += [(("one", i), 0.5, [("vectors",)]) for i in range(4)]
    rows += [(("low", b), 0.5, [("flags",)]) for b in range(2)]
    lows = [("low", b) for b in range(2)]
    ones = [("one", i) for i in range(4)] + [("flags",)]
    rows += [(("project", j, i), 0.55, there[j] + ones) for j in range(3) for i in range(2)]
    projected = [("project", j, i) for j in range(3) for i in range(2)]
    rows += [(("attend", b, k), 2.4, projected) for b in range(2) for k in range(2)]
    rows += [(("two", b), 1.2, there[3] + [("attend", b, k) for k in range(2)]) for b in range(2)]
    rows += [(("rise", k, i), 0.35, there[4 + k] + [("two", i // 2)]) for k in range(4) for i in range(4)]
    rows += [(("down", s), 0.45, lows + [("rise", s // 2, i) for i in range(4)]) for s in range(8)]
    two = [("two", b) for b in range(2)]
    heads = [("attend", b, k) for b in range(2) for k in range(2)]
    rows += [(("whole", j), 0.05, there[j]) for j in range(BLOCKS)]
    rows += [(("save e1", 0), 0.05, ones), (("save proj", 0), 0.05, projected), (("save probs", 0), 0.05, heads)]
    rows += [(("save att", 0), 0.05, heads), (("save mid", 0), 0.05, two), (("save e2", 0), 0.05, two)]
    for k in range(4):
        rows += [(("save " + n, k), 0.05, [("rise", k, i) for i in range(4)]) for n in ("act", "dg")]
    rows += [(("save gl", 0), 0.05, lows)]
    rows += [(("save gd", k), 0.05, [("down", s) for s in range(8)]) for k in range(4)]
    return [Task(name, time, needs, (), 1000 + k) for k, (name, time, needs) in enumerate(rows)]


def forward(w_qkv, w_out, w_up, w_down, vectors, tokens, flags, counts, cotangent):
    items = gather_items()
    n = len(items)
    tasks, there = gather_tasks(items)
    order = plan(tasks + forward_tasks(there), GATHER_RATES, GATHER_WINDOW, ARRIVE, SENT, GATHER_ISSUE)
    vmem, anywhere = pl.BlockSpec(memory_space=pltpu.VMEM), pl.BlockSpec(memory_space=pl.ANY)
    dma = pltpu.SemaphoreType.DMA
    whole, three, four = (ROWS, CW), (3, ROWS, CW), (4, ROWS, CW)
    shapes = [
        ((BLOCKS, 4, 2, RU, CW), BF), ((16, CW), F32), (whole, BF), (three, BF), ((4, 8, IMAGE, IMAGE), BF), (whole, BF), (whole, F32),
        (whole, BF), (four, BF), (four, BF), (whole, BF), ((4, 4, 2, RU, CW), BF),
    ]
    return pl.pallas_call(
        functools.partial(forward_kernel, items, order),
        out_shape=[jax.ShapeDtypeStruct(s, t) for s, t in shapes],
        in_specs=[anywhere] * 4 + [vmem] * 3 + [pl.BlockSpec(memory_space=pltpu.SMEM), vmem],
        out_specs=[anywhere] * len(shapes),
        scratch_shapes=[
            pltpu.VMEM((BLOCKS, 4, 2, RU, CW), BF),
            pltpu.VMEM((BLOCKS, H, CW), F32),
            pltpu.VMEM((16, 128), BF),
            pltpu.VMEM((8, 16, 128), BF),
            pltpu.VMEM((16, CW), F32),
            pltpu.VMEM((ROWS, 1), F32),
            pltpu.VMEM(whole, BF),
            pltpu.VMEM(three, BF),
            pltpu.VMEM((4, 8, IMAGE, IMAGE), BF),
            pltpu.VMEM(whole, BF),
            pltpu.VMEM(whole, F32),
            pltpu.VMEM(whole, BF),
            pltpu.VMEM(four, BF),
            pltpu.VMEM(four, BF),
            pltpu.VMEM(whole, BF),
            pltpu.VMEM((4, 4, 2, RU, CW), BF),
            dma((n, 3, 2)),
            dma((n, 4)),
            dma((n, 5)),
            dma((n, 2)),
            dma((8,)),
            dma((32,)),
            dma((8,)),
            dma((BLOCKS,)),
            dma((sum(GATHER_WINDOW.values()),)),
        ],
        compiler_params=pltpu.CompilerParams(collective_id=0, has_side_effects=True, vmem_limit_bytes=VMEM_LIMIT),
        name="forward",
    )(w_qkv, w_out, w_up, w_down, vectors, tokens, flags, counts, cotangent)


RATES = dict(c=350e3, x=45e3, y=45e3, z=45e3, w=45e3, v=45e3)
WINDOW = dict(c=8, x=8, y=3, z=4, w=6, v=3)
REDUCE_ITEMS = (
    ((2,), 3, False), ((11,), 1, False), ((7, 4), 3, False), ((5, 8), 1, False), ((3,), 1, False), ((10,), 1, True),
    ((9,), 1, False), ((1, 0), 3, True), ((6,), 1, False),
)
HALVES = 1
COMPUTE_RANK = 1000
SLOT = {blocks: k for k, (blocks, _, _) in enumerate(REDUCE_ITEMS)}
PAIR_SLOT = {blocks: k for k, blocks in enumerate(b for b, _, _ in REDUCE_ITEMS if len(b) == 2)}


def reduce_items():
    return [(blocks, direct, k * (H // parts), H // parts) for blocks, parts, direct in REDUCE_ITEMS for k in range(parts)]


def reduce_tasks(items, made):
    tasks = []
    for i, (blocks, direct, _, rows) in enumerate(items):
        pair, size, add = len(blocks) == 2, rows * CW * 2, 0.04 * rows / H
        needs = [token for j in blocks for token in made[j]]
        to_sib = [("c", 8 * size, ("mine", i), i)]
        halves = range(HALVES)
        to_y = [("y", 4 // HALVES * size, ("y%d" % q, i), i) for q in halves]
        if pair:
            to_x = [("x", 8 // HALVES * size, ("x%d" % q, i), i) for q in halves]
            tasks.append(Task(("A", i), 0.05, needs, [("c", 8 * size, ("theirs", i), i)] + to_sib, i))
            tasks.append(Task(("Bt", i), 8 * add, [("theirs", i)], to_x, i))
            tasks.append(Task(("Bm", i), 8 * add, [("mine", i)], [], i))
            tasks.append(Task(("C", i), 8 * add, [("x%d" % q, i) for q in halves] + [("Bm", i)], to_y, i))
        else:
            tasks.append(Task(("A", i), 0.05, needs, to_sib, i))
            tasks.append(Task(("Bm", i), 8 * add, [("mine", i)], to_y, i))
        tasks.append(Task(("D", i), 4 * add, [("y%d" % q, i) for q in halves], [("z", 3 * size, ("za", i), i)], i))
        tasks.append(Task(("E1", i), 3 * add, [("za", i)], [("w", 2 * size, ("zb", i), i - 50)], i))
        tasks.append(Task(("E2", i), 2 * add, [("zb", i)], [("v", size, ("zc", i), i - 50)], i))
        finals = [("x", size, ("xf", i), i - 100)]
        if direct:
            finals += [("x", size, ("xd", i), i - 100), ("c", size, ("cf", i), i - 100)]
        tasks.append(Task(("E3", i), add, [("zc", i)], finals, i))
        if direct:
            tasks.append(Task(("L", i), 4 * add, [("xf", i), ("xd", i), ("cf", i)], [], i))
            continue
        finals = [("f%d" % k, i) for k in range(len(blocks))]
        tasks.append(Task(("G", i), 2 * add, [("xf", i)], [("c", size, f, i) for f in finals], i))
        tasks.append(Task(("H", i), 0.05, finals, [], i))
    return tasks


def vector_tasks(made):
    size = 8 * CW * 4
    return [
        Task(("V0", 0), 0.05, made, [("c", size, ("vc", 0), -200)], -200),
        Task(("V1", 0), 0.05, [("vc", 0)], [("x", size, ("vx", 0), -200)], -200),
        Task(("V2", 0), 0.05, [("vx", 0)], [("y", size, ("vy", 0), -200)], -200),
        Task(("V3", 0), 0.05, [("vy", 0)], [("z", size, ("vz%d" % d, 0), -200) for d in (1, 2, 3)], -200),
        Task(("V4", 0), 0.05, [("vz%d" % d, 0) for d in (1, 2, 3)], [], -200),
    ]


class Reducer:
    def __init__(self, at, items, sender, g, fin, sr, xr, yr, zr, xf, xd, cf, vec, vr, sems):
        self.at, self.items, self.sender = at, items, sender
        self.g, self.fin, self.sr, self.xr, self.yr, self.zr, self.xf = g, fin, sr, xr, yr, zr, xf
        self.xd, self.cf = xd, cf
        self.vec, self.vr = vec, vr
        self.ssem, self.xsem, self.ysem, self.zsem, self.xfsem, self.fsem, self.vsem = sems

    def run(self, op, i):
        if op[0] == "V":
            return self.vectors(op)
        at, g, y, z = self.at, self.g, self.at.y, self.at.z
        blocks, direct, first, count = self.items[i]
        pair, key, m = len(blocks) == 2, SLOT[blocks], self.at.mine(blocks)
        xkey = PAIR_SLOT.get(blocks)
        loc = pl.ds(first, count)
        own_rows = pl.ds(pl.multiple_of(at.c * H + first, 16), count)
        sib_rows = pl.ds(pl.multiple_of((1 - at.c) * H + first, 16), count)

        def add_shards(j, src):
            def body(k, _):
                d = g.at[j, k // 2, k % 2, own_rows, :]
                add_into(d, d, src.at[k // 2, k % 2, loc, :])
                return 0

            lax.fori_loop(0, 8, body, 0)

        def to_y():
            for q in range(HALVES):
                two = pl.ds(4 // HALVES * q, 4 // HALVES)
                self.sender.put(
                    ("y%d" % q, i), "y", g.at[m, two, 1 - y, own_rows, :], self.yr.at[key, two, loc, :],
                    self.ysem.at[i, q], at.yn,
                )

        if op == "A":
            if pair:
                t = at.theirs(blocks)
                self.sender.put(
                    ("theirs", i), "c", g.at[t, :, :, sib_rows, :], self.sr.at[t, :, :, loc, :], self.ssem.at[i, 1], at.sib
                )
            self.sender.put(
                ("mine", i), "c", g.at[m, :, :, sib_rows, :], self.sr.at[m, :, :, loc, :], self.ssem.at[i, 0], at.sib
            )
        elif op == "Bm":
            arrived(self.sr.at[m, :, :, loc, :], self.ssem.at[i, 0])
            add_shards(m, self.sr.at[m])
            if not pair:
                to_y()
        elif op == "Bt":
            t = at.theirs(blocks)
            arrived(self.sr.at[t, :, :, loc, :], self.ssem.at[i, 1])
            add_shards(t, self.sr.at[t])
            for q in range(HALVES):
                two = pl.ds(4 // HALVES * q, 4 // HALVES)
                self.sender.put(
                    ("x%d" % q, i), "x", g.at[t, two, :, own_rows, :], self.xr.at[xkey, two, :, loc, :],
                    self.xsem.at[i, q], at.xn,
                )
        elif op == "C":
            for q in range(HALVES):
                arrived(self.xr.at[xkey, pl.ds(4 // HALVES * q, 4 // HALVES), :, loc, :], self.xsem.at[i, q])
            add_shards(m, self.xr.at[xkey])
            to_y()
        elif op == "D":
            for q in range(HALVES):
                arrived(self.yr.at[key, pl.ds(4 // HALVES * q, 4 // HALVES), loc, :], self.ysem.at[i, q])

            def body(k, _):
                d = g.at[m, k, y, own_rows, :]
                add_into(d, d, self.yr.at[key, k, loc, :])
                return 0

            lax.fori_loop(0, 4, body, 0)
            self.sender.put(
                ("za", i), "z", g.at[m, pl.ds(1 - z // 3, 3), y, own_rows, :], self.zr.at[key, pl.ds(0, 3), loc, :],
                self.zsem.at[i, 0], at.inner, at.end,
            )
        elif op == "L":
            for buffer, sem in ((self.xf, self.xfsem.at[i]), (self.xd, self.fsem.at[i, 0]), (self.cf, self.fsem.at[i, 1])):
                arrived(buffer.at[key, loc, :], sem)
            mine = g.at[m, z, y, own_rows, :]
            if pair:
                t = at.theirs(blocks)
                self.fin[m, own_rows, :] = mine[...]
                self.fin[m, sib_rows, :] = self.cf[key, loc, :]
                self.fin[t, own_rows, :] = self.xf[key, loc, :]
                self.fin[t, sib_rows, :] = self.xd[key, loc, :]
            else:
                add_into(self.fin.at[m, own_rows, :], mine, self.xf.at[key, loc, :])
                add_into(self.fin.at[m, sib_rows, :], self.cf.at[key, loc, :], self.xd.at[key, loc, :])
        elif op == "E1":

            @pl.when(at.mid)
            def _():
                arrived(self.zr.at[key, pl.ds(0, 3), loc, :], self.zsem.at[i, 0])
                for k in range(3):
                    d = g.at[m, 2 - z + k, y, own_rows, :]
                    add_into(d, d, self.zr.at[key, k, loc, :])

            self.sender.put(
                ("zb", i), "w", g.at[m, pl.ds(2 * (2 - z), 2), y, own_rows, :], self.zr.at[key, pl.ds(3, 2), loc, :],
                self.zsem.at[i, 1], at.inner, at.mid,
            )
        elif op == "E2":

            @pl.when(at.mid)
            def _():
                arrived(self.zr.at[key, pl.ds(3, 2), loc, :], self.zsem.at[i, 1])
                for k in range(2):
                    d = g.at[m, 2 * (z - 1) + k, y, own_rows, :]
                    add_into(d, d, self.zr.at[key, 3 + k, loc, :])

            self.sender.put(
                ("zc", i), "v", g.at[m, 3 * (z - 1), y, own_rows, :], self.zr.at[key, 0, loc, :],
                self.zsem.at[i, 2], at.outer, at.mid,
            )
        elif op == "E3":
            d = g.at[m, z, y, own_rows, :]

            @pl.when(at.end)
            def _():
                arrived(self.zr.at[key, 0, loc, :], self.zsem.at[i, 2])
                add_into(d, d, self.zr.at[key, 0, loc, :])

            self.sender.put(("xf", i), "x", d, self.xf.at[key, loc, :], self.xfsem.at[i], at.xn)
            if direct:
                self.sender.put(("xd", i), "x", d, self.xd.at[key, loc, :], self.fsem.at[i, 0], at.xn_sib)
                self.sender.put(("cf", i), "c", d, self.cf.at[key, loc, :], self.fsem.at[i, 1], at.sib)
        elif op == "G":
            arrived(self.xf.at[key, loc, :], self.xfsem.at[i])
            d = g.at[m, z, y, own_rows, :]
            if pair:
                self.fin[m, own_rows, :] = d[...]
                self.fin[at.theirs(blocks), own_rows, :] = self.xf[key, loc, :]
            else:
                add_into(self.fin.at[m, own_rows, :], d, self.xf.at[key, loc, :])
            for k, j in enumerate((m, at.theirs(blocks)) if pair else blocks):
                f = self.fin.at[j, own_rows, :]
                self.sender.put(("f%d" % k, i), "c", f, f, self.fsem.at[i, k], at.sib)
        elif op == "H":
            for k, j in enumerate((m, at.theirs(blocks)) if pair else blocks):
                arrived(self.fin.at[j, sib_rows, :], self.fsem.at[i, k])

    def vectors(self, op):
        at, vec, vr, vsem = self.at, self.vec, self.vr, self.vsem
        if op == "V0":
            self.sender.put(("vc", 0), "c", vec.at[0], vr.at[0], vsem.at[0], at.sib)
        elif op == "V1":
            arrived(vr.at[0], vsem.at[0])
            vec[1] = vec[0] + vr[0]
            self.sender.put(("vx", 0), "x", vec.at[1], vr.at[1], vsem.at[1], at.xn)
        elif op == "V2":
            arrived(vr.at[1], vsem.at[1])
            vec[2] = vec[1] + vr[1]
            self.sender.put(("vy", 0), "y", vec.at[2], vr.at[2], vsem.at[2], at.yn)
        elif op == "V3":
            arrived(vr.at[2], vsem.at[2])
            vec[3] = vec[2] + vr[2]
            vr[3 + at.z] = vec[3]
            for d, to in ((1, at.up), (2, at.far), (3, at.down)):
                self.sender.put(("vz%d" % d, 0), "z", vec.at[3], vr.at[3 + at.z], vsem.at[3 + at.z], to)
        else:
            for d in (1, 2, 3):
                arrived(vr.at[3 + (at.z + d) % 4], vsem.at[3 + (at.z + d) % 4])
            vec[4] = ((vr[3] + vr[4]) + vr[5]) + vr[6]


def reduce_barrier(at):
    barrier = pltpu.get_barrier_semaphore()
    peers = [at.sib, at.xn, at.xn_sib, at.yn, at.up, at.far, at.down]
    for peer in peers:
        pl.semaphore_signal(barrier, inc=1, device_id=peer, device_id_type=MESH)
    pl.semaphore_wait(barrier, len(peers))


def reduce_scratch(n):
    dma = pltpu.SemaphoreType.DMA
    return [
        pltpu.VMEM((BLOCKS, 4, 2, H, CW), BF),
        pltpu.VMEM((len(PAIR_SLOT), 4, 2, H, CW), BF),
        pltpu.VMEM((len(SLOT), 4, H, CW), BF),
        pltpu.VMEM((len(SLOT), 5, H, CW), BF),
        pltpu.VMEM((len(SLOT), H, CW), BF),
        pltpu.VMEM((len(SLOT), H, CW), BF),
        pltpu.VMEM((len(SLOT), H, CW), BF),
        pltpu.VMEM((5, 8, CW), F32),
        pltpu.VMEM((7, 8, CW), F32),
        dma((n, 2)),
        dma((n, 2)),
        dma((n, 2)),
        dma((n, 3)),
        dma((n,)),
        dma((n, 2)),
        dma((7,)),
        dma((sum(WINDOW.values()),)),
    ]


LOADS = ("g0", "g1", "g2", "g3", "gl", "dg", "d0", "d1", "d2", "d3", "e2", "mid", "cot", "out", "att", "proj", "probs", "e1", "tok")


def backward_tasks():
    rows = [(("gd", k), 0.02, []) for k in range(4)]
    rows += [(("gr", k), 1.0, []) for k in range(4)]
    rows += [(("gu", k, i), 0.6, [("gr", k)]) for k in range(4) for i in range(2)]
    rows += [(("b2", b), 2.4, [("gr", k) for k in range(4)]) for b in range(2)]
    two = [("b2", b) for b in range(2)]
    rows += [(("go", i), 0.75, two) for i in range(2)]
    rows += [(("ga", b), 0.75, [("b2", b)]) for b in range(2)]
    rows += [(("ab", b, k), 3.4, [("ga", b)]) for b in range(2) for k in range(2)]
    heads = [("ab", b, k) for b in range(2) for k in range(2)]
    rows += [(("gq", j, i), 0.7, heads) for j in range(3) for i in range(2)]
    rows += [(("b1", b), 2.1, heads) for b in range(2)]
    made = [[("gq", j, i) for i in range(2)] for j in range(3)]
    made += [[("go", i) for i in range(2)]]
    made += [[("gu", k, i) for i in range(2)] for k in range(4)]
    made += [[("gd", k)] for k in range(4)]
    last = [("b1", b) for b in range(2)] + [("gq", j, i) for j in range(3) for i in range(2)]
    rows += [(("la",), 0.1, last)] + [(("lo", b), 2.0, [("la",)]) for b in range(2)]
    tasks = [Task(name, time, needs, (), COMPUTE_RANK + 0.001 * k) for k, (name, time, needs) in enumerate(rows)]
    return tasks, made, [("b1", b) for b in range(2)]


def backward_kernel(
    items, order,
    flags, counts, pv, act_h, cot_h, dg_h, gl_h, gd_h, w_h, e2_h, mid_h, att_h, proj_h, probs_h, e1_h, tok_h,
    lo_h, tg_h, fin, vec_out,
    act, cot, dg, w, e2, mid, att, proj, probs, e1, tok, fcol, gl, gm, ml, g, load_sem, out_sem, *reduce_refs,
):
    at = Place()
    source = dict(gl=gl_h, cot=cot_h, dg=dg_h, e2=e2_h, mid=mid_h, att=att_h, proj=proj_h, probs=probs_h, e1=e1_h, tok=tok_h)
    target = dict(gl=gl, cot=cot, dg=dg, e2=e2, mid=mid, att=att, proj=proj, probs=probs, e1=e1, tok=tok)
    loads = {}

    def load(name, src, dst):
        loads[name] = pltpu.make_async_copy(src, dst, load_sem.at[len(loads)])
        loads[name].start()

    def need(*names):
        for name in names:
            if loads[name] is not None:
                loads[name].wait()
                loads[name] = None

    for name in LOADS:
        if name in source:
            load(name, source[name], target[name])
        elif name == "out":
            load(name, w_h.at[3], w.at[4])
        elif name[0] == "g":
            load(name, gd_h.at[int(name[1])], g.at[8 + int(name[1])])
        else:
            load(name, w_h.at[8 + int(name[1])], w.at[int(name[1])])
    vec = reduce_refs[7]
    vec[0] = jnp.zeros((8, CW), F32)
    flag_column(flags, fcol)
    reduce_barrier(at)
    sender = Sender(reduce_refs[-1], WINDOW)
    steps = Reducer(at, items, sender, g, fin, *reduce_refs[:9], reduce_refs[9:16])
    dproj, ga, tg, lo = act, gl, ml, gl

    def compute(op, *k):
        if op == "gd":
            need("g%d" % k)
        elif op == "gr":
            need("gl", "dg", "d0", "d1", "d2", "d3")
            grad_rising_part(gl, w, dg, *k)
            if k[0] == 3:
                for j in range(4):
                    load("u%d" % j, w_h.at[4 + j], w.at[j])
        elif op == "gu":
            need("e2")
            weight_grad_part(e2, dg.at[k[0]], g, 4 + k[0], k[1])
        elif op == "b2":
            need("mid", "cot", "u0", "u1", "u2", "u3")
            back_two_part(dg, w, mid, pv, cot, fcol, counts, gm, ml, vec, *k, rows=IMAGE)
            if k[0] == 1:
                for j in range(3):
                    load("q%d" % j, w_h.at[j], w.at[j])
        elif op == "go":
            need("att")
            weight_grad_part(att, ml, g, 3, *k)
        elif op == "ga":
            need("out")
            grad_attended_part(ml, w, ga, *k)
        elif op == "ab":
            need("proj", "probs")
            attend_back(proj, probs, ga, dproj, *k)
        elif op == "gq":
            need("e1")
            weight_grad_part(e1, dproj.at[k[0]], g, *k)
        elif op == "b1":
            need("tok", "q0", "q1", "q2")
            back_one_part(dproj, w, tok, fcol, pv, gm, tg, vec, *k, rows=IMAGE)
            if k[0] == 1:
                pltpu.make_async_copy(tg, tg_h, out_sem.at[0]).start()
        elif op == "la":
            load("act", act_h, act)
            for j in range(4):
                load("l%d" % j, w_h.at[8 + j], w.at[j])
        elif op == "lo":
            need("act", "l0", "l1", "l2", "l3")
            lower(act, w, mid, lo, *k, first=0)
            if k[0] == 1:
                pltpu.make_async_copy(lo, lo_h, out_sem.at[1]).start()

    for entry in order:
        if entry[0] == "issue":
            sender.issue(entry[1], entry[2])
        elif entry[0] == "waits":
            sender.wait(entry[1])
        elif entry[1][0][0].isupper():
            steps.run(*entry[1])
        else:
            compute(*entry[1])
    pltpu.make_async_copy(tg, tg_h, out_sem.at[0]).wait()
    pltpu.make_async_copy(lo, lo_h, out_sem.at[1]).wait()
    vec_out[...] = vec[4]


def backward(flags, counts, pv, act, cot, dg, gl, gd, w, e2, mid, att, proj, probs, e1, tok):
    items = reduce_items()
    steps, made, vector_made = backward_tasks()
    order = plan(steps + reduce_tasks(items, made) + vector_tasks(vector_made), RATES, WINDOW, ARRIVE, SENT, ISSUE)
    vmem, anywhere = pl.BlockSpec(memory_space=pltpu.VMEM), pl.BlockSpec(memory_space=pl.ANY)
    whole, three, four = (ROWS, CW), (3, ROWS, CW), (4, ROWS, CW)
    dma = pltpu.SemaphoreType.DMA
    return pl.pallas_call(
        functools.partial(backward_kernel, items, order),
        out_shape=[
            jax.ShapeDtypeStruct(whole, BF),
            jax.ShapeDtypeStruct(whole, BF),
            jax.ShapeDtypeStruct((BLOCKS, RU, CW), BF),
            jax.ShapeDtypeStruct((8, CW), F32),
        ],
        in_specs=[vmem, pl.BlockSpec(memory_space=pltpu.SMEM), vmem] + [anywhere] * 13,
        out_specs=[anywhere, anywhere, vmem, vmem],
        scratch_shapes=[
            pltpu.VMEM(four, BF),
            pltpu.VMEM(whole, BF),
            pltpu.VMEM(four, BF),
            pltpu.VMEM((5, 4, 2, RU, CW), BF),
            pltpu.VMEM(whole, BF),
            pltpu.VMEM(whole, F32),
            pltpu.VMEM(whole, BF),
            pltpu.VMEM(three, BF),
            pltpu.VMEM((4, 8, IMAGE, IMAGE), BF),
            pltpu.VMEM(whole, BF),
            pltpu.VMEM(whole, BF),
            pltpu.VMEM((ROWS, 1), F32),
            pltpu.VMEM(whole, BF),
            pltpu.VMEM(whole, F32),
            pltpu.VMEM(whole, BF),
            pltpu.VMEM((BLOCKS, 4, 2, RU, CW), BF),
            dma((32,)),
            dma((2,)),
        ]
        + reduce_scratch(len(items)),
        compiler_params=pltpu.CompilerParams(collective_id=1, has_side_effects=True, vmem_limit_bytes=VMEM_LIMIT),
        name="backward",
    )(flags, counts, pv, act, cot, dg, gl, gd, w, e2, mid, att, proj, probs, e1, tok)


ADAM_AHEAD = 12


def adamw_step(weight, grad, first, second, rate):
    new_first = BETA_ONE * first + (1.0 - BETA_ONE) * grad
    new_second = BETA_TWO * second + (1.0 - BETA_TWO) * grad * grad
    v = new_second * (1.0 / (1.0 - BETA_TWO**STEP))
    ratio = new_first * (1.0 / (1.0 - BETA_ONE**STEP)) / (v * lax.rsqrt(v) + ADAM_EPS)
    return (new_first, new_second, weight - rate * (ratio + DECAY * weight))


def adam_kernel(fin, vec, fs, *refs):
    states, vecs, done, outs, vec_outs, handed = refs[:12], refs[12:15], refs[15:17], refs[17:29], refs[29:33], refs[33:35]
    ins, news, kept, in_sem, out_sem, done_sem = refs[35:]
    keep = [pltpu.make_async_copy(done[k], kept.at[k], done_sem.at[k]) for k in range(2)]
    hand_on = [pltpu.make_async_copy(kept.at[k], handed[k], done_sem.at[2 + k]) for k in range(2)]

    def block(ref, j):
        if j < 3:
            return ref.at[:, pl.ds(j * CW, CW)]
        if j == 3:
            return ref
        if j < 8:
            return ref.at[:, pl.ds((j - 4) * CW, CW)]
        return ref.at[pl.ds((j - 8) * RU, RU), :]

    matrix_of = [0] * 3 + [1] + [2] * 4 + [3] * 4
    loads, saves = [], []
    for j in range(BLOCKS):
        three = [
            pltpu.make_async_copy(block(states[3 * matrix_of[j] + k], j), ins.at[j, k], in_sem.at[j, k]) for k in range(3)
        ]
        loads.append(three)

    def start(j):
        for copy in loads[j]:
            copy.start()

    for j in range(ADAM_AHEAD):
        start(j)
        if j == 2:
            for copy in keep:
                copy.start()
    column = lax.broadcasted_iota(jnp.int32, (RU, CW), 1) == lax.broadcasted_iota(jnp.int32, (RU, CW), 0) + fs[0] * RU
    grad = lax.dot_general(
        vec[...], column.astype(F32), (((1,), (1,)), ((), ())), preferred_element_type=F32,
        precision=lax.Precision.HIGHEST,
    )
    first, second, new = adamw(vecs[0][...], grad[0:5], vecs[1][...], vecs[2][...], RATE_VECTORS)
    vec_outs[0][...] = first
    vec_outs[1][0:2, :] = second[0:2]
    vec_outs[1][2:3, :] = second[4:5]
    vec_outs[2][...] = second[2:4]
    vec_outs[3][...] = new
    for j in range(BLOCKS):
        rate = (RATE_QKV, RATE_OUT, RATE_UP, RATE_DOWN)[matrix_of[j]]
        if j == 2:
            for k in range(2):
                keep[k].wait()
                hand_on[k].start()
        if j + ADAM_AHEAD < BLOCKS:
            start(j + ADAM_AHEAD)
        for copy in loads[j]:
            copy.wait()

        def rows(i, _, j=j, rate=rate):
            r = part(i, 32)
            result = adamw_step(ins[j, 0, r, :], fin[j, r, :].astype(F32), ins[j, 1, r, :], ins[j, 2, r, :], rate)
            for k in range(3):
                news[j, k, r, :] = result[k]
            return 0

        lax.fori_loop(0, RU // 32, rows, 0)
        for k in range(3):
            copy = pltpu.make_async_copy(news.at[j, k], block(outs[3 * matrix_of[j] + k], j), out_sem.at[j, k])
            copy.start()
            saves.append(copy)
    for copy in saves + hand_on:
        copy.wait()


def adam(fin, vec, fs, states, vecs, done):
    vmem, anywhere = pl.BlockSpec(memory_space=pltpu.VMEM), pl.BlockSpec(memory_space=pl.ANY)
    dma = pltpu.SemaphoreType.DMA
    return pl.pallas_call(
        adam_kernel,
        out_shape=[jax.ShapeDtypeStruct(s.shape, F32) for s in states]
        + [jax.ShapeDtypeStruct((n, RU), F32) for n in (5, 3, 2, 5)]
        + [jax.ShapeDtypeStruct(d.shape, d.dtype) for d in done],
        in_specs=[vmem, vmem, pl.BlockSpec(memory_space=pltpu.SMEM)] + [anywhere] * 12 + [vmem] * 3 + [anywhere] * 2,
        out_specs=[anywhere] * 12 + [vmem] * 4 + [anywhere] * 2,
        scratch_shapes=[
            pltpu.VMEM((BLOCKS, 3, RU, CW), F32),
            pltpu.VMEM((BLOCKS, 3, RU, CW), F32),
            pltpu.VMEM((2, ROWS, CW), BF),
            dma((BLOCKS, 3)),
            dma((BLOCKS, 3)),
            dma((4,)),
        ],
        compiler_params=pltpu.CompilerParams(vmem_limit_bytes=VMEM_LIMIT),
        name="adam",
    )(fin, vec, fs, *states, *vecs, *done)


def on_device_plain(
    tokens,
    mask_flags,
    mask_counts,
    cotangent,
    w_qkv,
    w_out,
    w_up,
    w_down,
    vectors,
    first_qkv,
    first_out,
    first_up,
    first_down,
    first_vectors,
    second_qkv,
    second_out,
    second_up,
    second_down,
    second_vectors,
):
    rows, width = tokens.shape
    images = mask_counts.shape[0]
    length = rows // images
    factor = HEAD_DIM ** (-0.5)
    attn_shards = (
        w_qkv.astype(jnp.bfloat16),
        w_out.astype(jnp.bfloat16),
        vectors.astype(jnp.bfloat16),
    )
    mlp_shards = (w_up.astype(jnp.bfloat16), w_down.astype(jnp.bfloat16))
    full_qkv, full_out, full_vec = (
        lax.all_gather(attn_shards[0], FSDP, axis=0, tiled=True),
        lax.all_gather(attn_shards[1], FSDP, axis=0, tiled=True),
        lax.all_gather(attn_shards[2], FSDP, axis=0, tiled=True),
    )
    full_up, full_down = (
        lax.all_gather(mlp_shards[0], FSDP, axis=0, tiled=True),
        lax.all_gather(mlp_shards[1], FSDP, axis=0, tiled=True),
    )
    params = full_vec.astype(jnp.float32)
    masked = (mask_flags == 1)[:, None]
    hidden = jnp.where(masked, params[:, 4][None, :], tokens.astype(jnp.float32))
    normed_one, inverse_one = standardize(hidden)
    entry_one = (normed_one * params[:, 0] + params[:, 1]).astype(jnp.bfloat16)
    project = jnp.dot(entry_one, full_qkv, preferred_element_type=jnp.float32).astype(jnp.bfloat16)
    split = project.reshape(images, length, 3, HEADS, HEAD_DIM)
    queries = split[:, :, 0]
    keys = split[:, :, 1]
    values = split[:, :, 2]
    scores = (
        jnp.einsum(PAIRS, queries, keys, preferred_element_type=jnp.float32) * factor
    )
    top = jnp.max(scores, axis=-1, keepdims=True)
    total = jnp.sum(jnp.exp(scores - top), axis=-1, keepdims=True)
    logsum = top + jnp.log(total)
    probs_low = jnp.exp(scores - logsum).astype(jnp.bfloat16)
    mixed = jnp.einsum(MIXED, probs_low, values, preferred_element_type=jnp.float32)
    attended = mixed.astype(jnp.bfloat16).reshape(rows, width)
    middle = hidden + jnp.dot(attended, full_out, preferred_element_type=jnp.float32)
    normed_two, inverse_two = standardize(middle)
    entry_two = (normed_two * params[:, 2] + params[:, 3]).astype(jnp.bfloat16)
    rising = jnp.dot(entry_two, full_up, preferred_element_type=jnp.float32)
    activated, gelu_pull = jax.vjp(gelu_exact, rising)
    active = activated.astype(jnp.bfloat16)
    layer_out = (middle + jnp.dot(active, full_down, preferred_element_type=jnp.float32)).astype(
        jnp.bfloat16
    )
    row_weight = jnp.repeat(
        length / mask_counts.astype(jnp.float32), length, total_repeat_length=rows
    )
    grad_out = (
        cotangent.astype(jnp.float32) * (row_weight * mask_flags.astype(jnp.float32))[:, None]
    )
    back_up, back_down = (
        lax.all_gather(mlp_shards[0], FSDP, axis=0, tiled=True),
        lax.all_gather(mlp_shards[1], FSDP, axis=0, tiled=True),
    )
    back_qkv, back_out, back_vec = (
        lax.all_gather(attn_shards[0], FSDP, axis=0, tiled=True),
        lax.all_gather(attn_shards[1], FSDP, axis=0, tiled=True),
        lax.all_gather(attn_shards[2], FSDP, axis=0, tiled=True),
    )
    gains = back_vec.astype(jnp.float32)
    grad_low = grad_out.astype(jnp.bfloat16)
    grad_down = jnp.einsum("tf,td->fd", active, grad_low, preferred_element_type=jnp.float32)
    grad_active = jnp.einsum("td,fd->tf", grad_low, back_down, preferred_element_type=jnp.float32)
    grad_rising = gelu_pull(grad_active)[0].astype(jnp.bfloat16)
    grad_up = jnp.einsum("td,tf->df", entry_two, grad_rising, preferred_element_type=jnp.float32)
    grad_entry_two = jnp.einsum(
        "tf,df->td", grad_rising, back_up, preferred_element_type=jnp.float32
    )
    mlp_sums = (
        lax.psum_scatter(grad_up, FSDP, scatter_dimension=0, tiled=True),
        lax.psum_scatter(grad_down, FSDP, scatter_dimension=0, tiled=True),
    )
    back_two, gain_two, bias_two = norm_back(grad_entry_two, normed_two, inverse_two, gains[:, 2])
    grad_middle = grad_out + back_two
    middle_low = grad_middle.astype(jnp.bfloat16)
    grad_wout = jnp.einsum("tc,td->cd", attended, middle_low, preferred_element_type=jnp.float32)
    grad_attended = jnp.einsum(
        "td,cd->tc", middle_low, back_out, preferred_element_type=jnp.float32
    )
    grad_attended = grad_attended.astype(jnp.bfloat16).reshape(images, length, HEADS, HEAD_DIM)
    again_scores = (
        jnp.einsum(PAIRS, queries, keys, preferred_element_type=jnp.float32) * factor
    )
    probs = jnp.exp(again_scores - logsum)
    again_low = probs.astype(jnp.bfloat16)
    grad_values = jnp.einsum(
        MIXED_BACK, again_low, grad_attended, preferred_element_type=jnp.float32
    )
    grad_probs = jnp.einsum(
        PAIRS, grad_attended, values, preferred_element_type=jnp.float32
    )
    grad_scores = probs * (grad_probs - jnp.sum(grad_probs * probs, axis=-1, keepdims=True))
    grad_raw = (grad_scores * factor).astype(jnp.bfloat16)
    grad_queries = jnp.einsum(MIXED, grad_raw, keys, preferred_element_type=jnp.float32)
    grad_keys = jnp.einsum(MIXED_BACK, grad_raw, queries, preferred_element_type=jnp.float32)
    grad_project = (
        jnp.stack([grad_queries, grad_keys, grad_values], axis=2)
        .reshape(rows, 3 * width)
        .astype(jnp.bfloat16)
    )
    grad_qkv = jnp.einsum("td,te->de", entry_one, grad_project, preferred_element_type=jnp.float32)
    grad_entry_one = jnp.einsum(
        "te,de->td", grad_project, back_qkv, preferred_element_type=jnp.float32
    )
    back_one, gain_one, bias_one = norm_back(grad_entry_one, normed_one, inverse_one, gains[:, 0])
    grad_hidden = back_one + grad_middle
    token_grad = jnp.where(masked, 0.0, grad_hidden).astype(jnp.bfloat16)
    grad_mask = jnp.sum(jnp.where(masked, grad_hidden, 0.0), axis=0)
    grad_vec = jnp.stack([gain_one, bias_one, gain_two, bias_two, grad_mask], axis=1)
    attn_sums = (
        lax.psum_scatter(grad_qkv, FSDP, scatter_dimension=0, tiled=True),
        lax.psum_scatter(grad_wout, FSDP, scatter_dimension=0, tiled=True),
        lax.psum_scatter(grad_vec, FSDP, scatter_dimension=0, tiled=True),
    )
    sum_qkv, sum_out, sum_vec, sum_up, sum_down = (
        lax.psum(attn_sums[0].astype(jnp.bfloat16), DP).astype(jnp.float32),
        lax.psum(attn_sums[1].astype(jnp.bfloat16), DP).astype(jnp.float32),
        lax.psum(attn_sums[2].astype(jnp.bfloat16), DP).astype(jnp.float32),
        lax.psum(mlp_sums[0].astype(jnp.bfloat16), DP).astype(jnp.float32),
        lax.psum(mlp_sums[1].astype(jnp.bfloat16), DP).astype(jnp.float32),
    )
    qkv_first, qkv_second, qkv_new = adamw(w_qkv, sum_qkv, first_qkv, second_qkv, RATE_QKV)
    out_first, out_second, out_new = adamw(w_out, sum_out, first_out, second_out, RATE_OUT)
    up_first, up_second, up_new = adamw(w_up, sum_up, first_up, second_up, RATE_UP)
    down_first, down_second, down_new = adamw(w_down, sum_down, first_down, second_down, RATE_DOWN)
    vec_first, vec_second, vec_new = adamw(
        vectors, sum_vec, first_vectors, second_vectors, RATE_VECTORS
    )
    second_front = jnp.concatenate([vec_second[:, 0:2], vec_second[:, 4:5]], axis=1)
    second_later = vec_second[:, 2:4]
    return (
        layer_out,
        token_grad,
        qkv_first,
        out_first,
        up_first,
        down_first,
        vec_first,
        qkv_second,
        out_second,
        up_second,
        down_second,
        second_front,
        second_later,
        qkv_new,
        out_new,
        up_new,
        down_new,
        vec_new,
    )


def on_device_fast(
    tokens,
    mask_flags,
    mask_counts,
    cotangent,
    w_qkv,
    w_out,
    w_up,
    w_down,
    vectors,
    first_qkv,
    first_out,
    first_up,
    first_down,
    first_vectors,
    second_qkv,
    second_out,
    second_up,
    second_down,
    second_vectors,
):
    flags = mask_flags.reshape(1, ROWS)
    w, pv, e1, proj, probs, att, mid, e2, act, dg, gl, gd = forward(
        w_qkv, w_out, w_up, w_down, vectors.T, tokens, flags, mask_counts, cotangent
    )
    layer_out, token_grad, sums, sum_vec = backward(
        flags, mask_counts, pv, act, cotangent, dg, gl, gd, w, e2, mid, att, proj, probs, e1, tokens
    )
    states = (
        w_qkv, first_qkv, second_qkv, w_out, first_out, second_out,
        w_up, first_up, second_up, w_down, first_down, second_down,
    )
    fs = lax.axis_index(FSDP).astype(jnp.int32).reshape(1)
    new = adam(sums, sum_vec, fs, states, (vectors.T, first_vectors.T, second_vectors.T), (layer_out, token_grad))
    new_w, new_first, new_second = [[new[3 * m + k] for m in range(4)] for k in (2, 0, 1)]
    vec_first, second_front, second_later, vec_new = [v.T for v in new[12:16]]
    layer_out, token_grad = new[16:]
    return (
        layer_out, token_grad, *new_first, vec_first, *new_second, second_front, second_later, *new_w, vec_new
    )


def solution(mesh):
    placed = (
        P((DP, FSDP), None),
        P((DP, FSDP)),
        P((DP, FSDP)),
        P((DP, FSDP), None),
        P(FSDP, None),
        P(FSDP, None),
        P(FSDP, None),
        P(FSDP, None),
        P(FSDP, None),
        P(FSDP, None),
        P(FSDP, None),
        P(FSDP, None),
        P(FSDP, None),
        P(FSDP, None),
        P(FSDP, None),
        P(FSDP, None),
        P(FSDP, None),
        P(FSDP, None),
        P(FSDP, None),
    )
    shape = dict(mesh.shape)
    fast = shape[DP] == 4 and shape[FSDP] == 8
    return jax.shard_map(
        on_device_fast if fast else on_device_plain,
        mesh=mesh,
        in_specs=placed,
        out_specs=(
            P((DP, FSDP), None),
            P((DP, FSDP), None),
            P(FSDP, None),
            P(FSDP, None),
            P(FSDP, None),
            P(FSDP, None),
            P(FSDP, None),
            P(FSDP, None),
            P(FSDP, None),
            P(FSDP, None),
            P(FSDP, None),
            P(FSDP, None),
            P(FSDP, None),
            P(FSDP, None),
            P(FSDP, None),
            P(FSDP, None),
            P(FSDP, None),
            P(FSDP, None),
        ),
        check_vma=False,
    )
```
